32 devices in a mesh: fsdp: 8 (over z, y), tensor: 4 (over x, core).
Axes of the slice: x: 2, y: 2, z: 4, core: 2. Of those that a mesh axis runs over, the one named last changes fastest.
Arguments:
- layer_in: bfloat16 [16384, 1152], P(('fsdp', 'tensor')), may hold values from -6 to 6
- teacher: bfloat16 [16384, 1152], P(('fsdp', 'tensor')), may hold values from -8 to 8
- query_proj: bfloat16 [1152, 1024], P('fsdp', 'tensor'), may hold values from -0.1875 to 0.1875
- key_proj: bfloat16 [1152, 256], P(('fsdp', 'tensor')), may hold values from -0.1875 to 0.1875
- value_proj: bfloat16 [1152, 256], P(('fsdp', 'tensor')), may hold values from -0.1875 to 0.1875
- out_proj: bfloat16 [1024, 1152], P('tensor', 'fsdp'), may hold values from -0.1875 to 0.1875
- gate_proj: bfloat16 [1152, 6912], P('fsdp', 'tensor'), may hold values from -0.1875 to 0.1875
- up_proj: bfloat16 [1152, 6912], P('fsdp', 'tensor'), may hold values from -0.1875 to 0.1875
- down_proj: bfloat16 [6912, 1152], P('tensor', 'fsdp'), may hold values from -0.078125 to 0.078125
- attn_norm: bfloat16 [1152], P(('fsdp', 'tensor')), may hold values from -0.3984375 to 0.59765625
- attn_post: bfloat16 [1152], P(('fsdp', 'tensor')), may hold values from -0.3984375 to 0.59765625
- ffw_norm: bfloat16 [1152], P(('fsdp', 'tensor')), may hold values from -0.3984375 to 0.59765625
- ffw_post: bfloat16 [1152], P(('fsdp', 'tensor')), may hold values from -0.3984375 to 0.59765625
- query_norm: bfloat16 [256], P(('fsdp', 'tensor')), may hold values from -0.3984375 to 0.59765625
- key_norm: bfloat16 [256], P(('fsdp', 'tensor')), may hold values from -0.3984375 to 0.59765625
- cont_prompt: int32 [32], P('fsdp'), may hold values from 0 to 3
- cont_length: int32 [32], P('fsdp'), may hold values from 128 to 256, as said below
- token_count: int32 [], replicated, may hold values from 8192 to 16384
- loss_scale: float32 [], replicated, may hold values from 4096 to 16384
Outputs:
- layer_out: bfloat16 [16384, 1152], P(('fsdp', 'tensor'))
- loss: float32 [], replicated
- grad_in: bfloat16 [16384, 1152], P(('fsdp', 'tensor'))
- grad_query: float32 [1152, 1024], P('fsdp', 'tensor')
- grad_key: float32 [1152, 256], P(('fsdp', 'tensor'))
- grad_value: float32 [1152, 256], P(('fsdp', 'tensor'))
- grad_out: float32 [1024, 1152], P('tensor', 'fsdp')
- grad_gate: float32 [1152, 6912], P('fsdp', 'tensor')
- grad_up: float32 [1152, 6912], P('fsdp', 'tensor')
- grad_down: float32 [6912, 1152], P('tensor', 'fsdp')
- grad_attn_norm: float32 [1152], P(('fsdp', 'tensor'))
- grad_attn_post: float32 [1152], P(('fsdp', 'tensor'))
- grad_ffw_norm: float32 [1152], P(('fsdp', 'tensor'))
- grad_ffw_post: float32 [1152], P(('fsdp', 'tensor'))
- grad_query_norm: float32 [256], P(('fsdp', 'tensor'))
- grad_key_norm: float32 [256], P(('fsdp', 'tensor'))
The draws below stay inside these ranges and needn't reach their ends.
Inputs may be any that keep to these rules, and one draw needn't show every extreme that they name: `cont_prompt`: each continuation follows one of the 4 prompts of its own group of 8 fsdp indices. `cont_length`: rows of a continuation from this length on are padding.
All inputs are finite; a program needn't handle non-finite values.
Results may differ from the reference program's by a relative error of at most 0.025.
Values may be sent and summed in bfloat16 or wider, within the bound.
No kernel may reach another device: no remote copies, remote signals or barrier semaphores. Data moves between devices by JAX's collectives and lax.ppermute only.
A program may use at most 256 MiB of HBM per device.

```python
import math
import jax
import jax.numpy as jnp
from jax import lax

D = 1152
HEADS = 4
HEAD = 256
FF = 6912
PROMPT = 2048
CONT = 256
GROUP = 8
GROUPS_DEV = 4
PSLICE = 256
ROWS_F = 2048
TOKENS = 16384
CONTS = 32
N_FSDP = 8


def draw_cont_length(key, part):
    lengths_out = jax.random.randint(jax.random.fold_in(key, 11), (CONTS,), CONT // 2, CONT + 1)
    picked = jax.random.permutation(jax.random.fold_in(key, 12), CONTS)
    lengths_out = lengths_out.at[picked[0]].set(CONT)
    lengths_out = lengths_out.at[picked[1]].set(CONT // 2)
    return lengths_out.astype(jnp.int32)


def draw_teacher(key, part):
    row_frac = jnp.arange(TOKENS, dtype=jnp.float32)[:, None] / (TOKENS - 1)
    spread = 0.3 + 2.2 * row_frac
    values = jnp.clip(jax.random.normal(jax.random.fold_in(key, 22), (TOKENS, D), jnp.float32), -3.2, 3.2)
    return (values * spread).astype(jnp.bfloat16)


def touch_ends(entries, stream_key, smallest, top_value):
    longest = entries.shape.index(max(entries.shape))
    spots = []
    for shift in (0, 1):
        where = [jax.random.randint(jax.random.fold_in(stream_key, axis), (), 0, length) for axis, length in enumerate(entries.shape)]
        where[longest] = (where[longest] + shift) % entries.shape[longest]
        spots.append(tuple(where))
    return entries.at[spots[0]].set(smallest).at[spots[1]].set(top_value)


def level_of(rng, shape, split, smallest, high):
    def one(axis_at, parts):
        heights = jax.random.uniform(jax.random.fold_in(jax.random.fold_in(rng, 6), axis_at), (parts,), jnp.float32, smallest / len(split), high / len(split))
        return jnp.repeat(jnp.exp(heights), shape[axis_at] // parts).reshape((-1,) + (1,) * (len(shape) - axis_at - 1))

    factor_of = one(*split[0])
    for cut in split[1:]:
        factor_of = factor_of * one(*cut)
    return factor_of


def gaussian(stream_key, shape, deviation, bound, cuts=(), kind=jnp.bfloat16):
    drawn = jax.random.normal(stream_key, shape, jnp.float32) * deviation
    if len(cuts) > 0:
        drawn = level_of(stream_key, shape, cuts, -0.22, 0.18) * drawn
    return jnp.clip(drawn, min=-bound, max=bound).astype(kind)


def setup_inputs(seed: int = 0) -> dict:
    seeds = jax.random.split(jax.random.key(seed), 20)
    return {
        "layer_in": gaussian(seeds[0], (TOKENS, D), 1.0, 6.0, ((0, 32),)),
        "teacher": draw_teacher(jax.random.fold_in(seeds[19], 71), 0),
        "query_proj": gaussian(seeds[2], (D, HEADS * HEAD), D ** -0.5, 0.1875, ((0, 8), (1, 4))),
        "key_proj": gaussian(seeds[3], (D, HEAD), D ** -0.5, 0.1875, ((0, 32),)),
        "value_proj": gaussian(seeds[4], (D, HEAD), D ** -0.5, 0.1875, ((0, 32),)),
        "out_proj": gaussian(seeds[5], (HEADS * HEAD, D), (HEADS * HEAD) ** -0.5, 0.1875, ((0, 4), (1, 8))),
        "gate_proj": gaussian(seeds[6], (D, FF), D ** -0.5, 0.1875, ((0, 8), (1, 4))),
        "up_proj": gaussian(seeds[7], (D, FF), D ** -0.5, 0.1875, ((0, 8), (1, 4))),
        "down_proj": gaussian(seeds[8], (FF, D), FF ** -0.5, 0.078125, ((0, 4), (1, 8))),
        "attn_norm": jnp.clip(-0.3984375 + 0.99609375 * jax.random.uniform(seeds[9], (D,), jnp.float32) ** level_of(seeds[9], (D,), ((0, 32),), -0.2, 0.2), -0.3984375, 0.59765625).astype(jnp.bfloat16),
        "attn_post": jnp.clip(-0.3984375 + 0.99609375 * jax.random.uniform(seeds[10], (D,), jnp.float32) ** level_of(seeds[10], (D,), ((0, 32),), -0.2, 0.2), -0.3984375, 0.59765625).astype(jnp.bfloat16),
        "ffw_norm": jnp.clip(-0.3984375 + 0.99609375 * jax.random.uniform(seeds[11], (D,), jnp.float32) ** level_of(seeds[11], (D,), ((0, 32),), -0.2, 0.2), -0.3984375, 0.59765625).astype(jnp.bfloat16),
        "ffw_post": jnp.clip(-0.3984375 + 0.99609375 * jax.random.uniform(seeds[12], (D,), jnp.float32) ** level_of(seeds[12], (D,), ((0, 32),), -0.2, 0.2), -0.3984375, 0.59765625).astype(jnp.bfloat16),
        "query_norm": jnp.clip(-0.3984375 + 0.99609375 * jax.random.uniform(seeds[13], (HEAD,), jnp.float32) ** level_of(seeds[13], (HEAD,), ((0, 32),), -0.2, 0.2), -0.3984375, 0.59765625).astype(jnp.bfloat16),
        "key_norm": jnp.clip(-0.3984375 + 0.99609375 * jax.random.uniform(seeds[14], (HEAD,), jnp.float32) ** level_of(seeds[14], (HEAD,), ((0, 32),), -0.2, 0.2), -0.3984375, 0.59765625).astype(jnp.bfloat16),
        "cont_prompt": touch_ends(jax.random.randint(seeds[15], (CONTS,), 0, GROUPS_DEV), jax.random.fold_in(seeds[15], 1), 0, GROUPS_DEV - 1).astype(jnp.int32),
        "cont_length": draw_cont_length(jax.random.fold_in(seeds[19], 71), 0),
        "token_count": jax.random.randint(seeds[17], (), TOKENS // 2, TOKENS + 1).astype(jnp.int32),
        "loss_scale": jnp.clip(jnp.exp(jax.random.uniform(seeds[18], (), jnp.float32, math.log(4096.0), math.log(16384.0))), 4096.0, 16384.0),
    }


@jax.custom_vjp
def low(v):
    return lax.optimization_barrier(v.astype(jnp.bfloat16)).astype(jnp.float32)

@jax.custom_vjp
def low_back(v):
    return v

def low_keep(v):
    return (low(v), None)

def low_pass(kept, grad):
    return (grad,)

def back_keep(v):
    return (v, None)

def back_low(kept, grad):
    return (low(grad),)
low.defvjp(low_keep, low_pass)
low_back.defvjp(back_keep, back_low)
eps_norm = 1e-06
rope_base = 1000000.0
masked_score = -1e+30
highest = lax.Precision.HIGHEST

def matmul_high(left_side, right_side):
    return jnp.dot(left_side, right_side, precision=highest, preferred_element_type=jnp.float32)

def rms_scale(tensor_in, gain_vec):
    return tensor_in * lax.rsqrt(lax.optimization_barrier(jnp.mean(tensor_in * tensor_in, axis=-1, keepdims=True)) + eps_norm) * (1.0 + gain_vec)

def rotate(tensor_in, angles):
    half_dim = tensor_in.shape[-1] // 2
    first_half = tensor_in[..., :half_dim]
    second_half = tensor_in[..., half_dim:]
    cosine = jnp.cos(angles)
    sine_part = jnp.sin(angles)
    return jnp.concatenate([first_half * cosine - second_half * sine_part, second_half * cosine + first_half * sine_part], axis=-1)

def inverse_freq():
    return jnp.exp(-math.log(rope_base) * 2.0 * jnp.arange(HEAD // 2, dtype=jnp.float32) / HEAD)

def block_mask(slice_pos, length):
    shape_qk = (PSLICE + CONT, 2 * PROMPT + CONT)
    query_ids = lax.broadcasted_iota(jnp.int32, shape_qk, 0)
    key_ids = lax.broadcasted_iota(jnp.int32, shape_qk, 1)
    prompt_query = query_ids < PSLICE
    cont_query = query_ids >= PSLICE
    own_prompt = prompt_query & (key_ids < PROMPT) & (key_ids <= slice_pos * PSLICE + query_ids)
    mapped_prompt = cont_query & (key_ids >= PROMPT) & (key_ids < 2 * PROMPT)
    cont_key = key_ids - 2 * PROMPT
    own_cont = cont_query & (cont_key >= 0) & (cont_key <= query_ids - PSLICE) & (cont_key < length)
    return own_prompt | mapped_prompt | own_cont

def forward(layer_x, query_w, key_w, value_w, out_w, gate_w, up_w, down_w, attn_g, attn_post_g, ffw_g, ffw_post_g, query_g, key_g, teacher_f, live_f, angles, cont_prompt, cont_length, count_f):
    prompt_part = GROUPS_DEV * PSLICE
    score_scale = 1.0 / math.sqrt(HEAD)
    normed_in = low(rms_scale(layer_x, attn_g))
    query_raw = low_back(matmul_high(normed_in, query_w)).reshape(TOKENS, HEADS, HEAD)
    key_raw = matmul_high(normed_in, key_w)
    value_raw = matmul_high(normed_in, value_w)
    key_copies = jnp.stack([low_back(key_raw) for head_number in range(HEADS)], axis=1)
    value_copies = jnp.stack([low(low_back(value_raw)) for head_number in range(HEADS)], axis=1)
    query_rot = low(rotate(rms_scale(query_raw, query_g), angles[:, None, :]))
    key_rot = low(rotate(rms_scale(key_copies, key_g), angles[:, None, :]))
    pairs = jnp.concatenate([key_rot, value_copies], axis=-1)
    query_rows = query_rot.reshape(N_FSDP, ROWS_F, HEADS, HEAD)
    query_blocks = jnp.concatenate([query_rows[:, :prompt_part].reshape(N_FSDP, GROUPS_DEV, PSLICE, HEADS, HEAD), query_rows[:, prompt_part:].reshape(N_FSDP, GROUPS_DEV, CONT, HEADS, HEAD)], axis=2)
    query_blocks = query_blocks.reshape(N_FSDP * GROUPS_DEV, PSLICE + CONT, HEADS, HEAD)
    pair_rows = pairs.reshape(N_FSDP, ROWS_F, HEADS, 2 * HEAD)
    prompts = pair_rows[:, :prompt_part].reshape(N_FSDP // GROUP, GROUP, GROUPS_DEV, PSLICE, HEADS, 2 * HEAD)
    prompts = prompts.transpose(0, 2, 1, 3, 4, 5).reshape(N_FSDP // GROUP, GROUPS_DEV, PROMPT, HEADS, 2 * HEAD)
    cont_pairs = pair_rows[:, prompt_part:].reshape(N_FSDP * GROUPS_DEV, CONT, HEADS, 2 * HEAD)
    block_ids = jnp.arange(N_FSDP * GROUPS_DEV, dtype=jnp.int32)

    def one_block(inputs):
        query_blk, cont_blk, block_id, mapped, length = inputs
        fsdp_id = block_id // GROUPS_DEV
        group_id = fsdp_id // GROUP
        slot_id = block_id % GROUPS_DEV
        own_pairs = prompts[group_id, slot_id]
        other_pairs = prompts[group_id, mapped]
        keys_pairs = jnp.concatenate([own_pairs, other_pairs, cont_blk], axis=0)
        scores = low_back(jnp.einsum('qhd,khd->hqk', query_blk, keys_pairs[..., :HEAD], precision=highest) * score_scale)
        key_mask = block_mask(fsdp_id % GROUP, length)
        scores = jnp.where(key_mask[None], scores, masked_score)
        row_max = lax.optimization_barrier(jnp.max(scores, axis=-1, keepdims=True))
        shifted = jnp.exp(scores - row_max)
        row_probs = shifted / lax.optimization_barrier(jnp.sum(shifted, axis=-1, keepdims=True))
        return jnp.einsum('hqk,khd->qhd', low(row_probs), keys_pairs[..., HEAD:], precision=highest)
    attn_blocks = lax.map(jax.checkpoint(one_block), (query_blocks, cont_pairs, block_ids, cont_prompt, cont_length))
    attn_blocks = attn_blocks.reshape(N_FSDP, GROUPS_DEV, PSLICE + CONT, HEADS * HEAD)
    attn_rows = jnp.concatenate([attn_blocks[:, :, :PSLICE].reshape(N_FSDP, prompt_part, HEADS * HEAD), attn_blocks[:, :, PSLICE:].reshape(N_FSDP, GROUPS_DEV * CONT, HEADS * HEAD)], axis=1)
    attn_low = low(low_back(attn_rows.reshape(TOKENS, HEADS * HEAD)))
    attn_sum = low_back(matmul_high(attn_low, out_w))
    mixed = layer_x + rms_scale(attn_sum, attn_post_g)
    normed_mid = low(rms_scale(mixed, ffw_g))
    gate_raw = low_back(matmul_high(normed_mid, gate_w))
    up_raw = low_back(matmul_high(normed_mid, up_w))
    act_low = low(jax.nn.gelu(gate_raw, approximate=True) * up_raw)
    ffw_sum = low_back(matmul_high(act_low, down_w))
    result = mixed + rms_scale(ffw_sum, ffw_post_g)
    diff = result - teacher_f
    loss = jnp.sum(live_f[:, None] * diff * diff) / count_f
    return (loss, result)

def reference(layer_in, teacher, query_proj, key_proj, value_proj, out_proj, gate_proj, up_proj, down_proj, attn_norm, attn_post, ffw_norm, ffw_post, query_norm, key_norm, cont_prompt, cont_length, token_count, loss_scale):
    prompt_part = GROUPS_DEV * PSLICE
    params = [member.astype(jnp.float32) for member in (layer_in, query_proj, key_proj, value_proj, out_proj, gate_proj, up_proj, down_proj, attn_norm, attn_post, ffw_norm, ffw_post, query_norm, key_norm)]
    fsdp_ids = jnp.arange(N_FSDP, dtype=jnp.int32)[:, None]
    row_ids = jnp.arange(ROWS_F, dtype=jnp.int32)[None, :]
    positions = jnp.where(row_ids < prompt_part, fsdp_ids % GROUP * PSLICE + row_ids % PSLICE, PROMPT + (row_ids - prompt_part) % CONT)
    angles = positions.reshape(TOKENS).astype(jnp.float32)[:, None] * inverse_freq()[None, :]
    slot_of_row = jnp.clip((row_ids - prompt_part) // CONT, 0, GROUPS_DEV - 1)
    lengths = cont_length.reshape(N_FSDP, GROUPS_DEV)
    row_length = jnp.take_along_axis(lengths, jnp.broadcast_to(slot_of_row, (N_FSDP, ROWS_F)), axis=1)
    live = (row_ids < prompt_part) | ((row_ids - prompt_part) % CONT < row_length)
    live_f = jnp.where(live, 1.0, 0.0).astype(jnp.float32).reshape(TOKENS)
    teacher_f = teacher.astype(jnp.float32)
    count_f = token_count.astype(jnp.float32)

    def objective(*weights):
        return forward(*weights, teacher_f, live_f, angles, cont_prompt, cont_length, count_f)
    loss, pullback, result = jax.vjp(objective, *params, has_aux=True)
    grads = pullback(loss_scale)
    return (result.astype(jnp.bfloat16), loss, grads[0].astype(jnp.bfloat16), grads[1], grads[2], grads[3], grads[4], grads[5], grads[6], grads[7], grads[8], grads[9], grads[10], grads[11], grads[12], grads[13])
```

```python
import math

import jax
import jax.numpy as jnp
from jax import lax
from jax.sharding import PartitionSpec as P

HEAD = 256
HEADS = 4
PROMPT = 2048
CONT = 256
GROUP = 8
GROUPS_DEV = 4
PSLICE = 256
UNITS = 2
TENSOR = 4

RING = (0, 2, 4, 6, 7, 5, 3, 1)
PLACE = tuple(RING.index(member) for member in range(GROUP))

eps_norm = 1e-06
rope_base = 1000000.0
masked_score = -1e30
score_scale = 1.0 / math.sqrt(HEAD)
bf = jnp.bfloat16
f32 = jnp.float32


def swap_core(value):
    return lax.ppermute(value, "tensor", [(t, t ^ 1) for t in range(TENSOR)])


def swap_x(value):
    return lax.ppermute(value, "tensor", [(t, t ^ 2) for t in range(TENSOR)])


def swap_bit(value, bit):
    size = lax.axis_size("fsdp")
    return lax.ppermute(value, "fsdp", [(f, f ^ bit) for f in range(size)])


def shift_z(value, step):
    pairs = [(z * 2 + y, (z + step) % 4 * 2 + y) for z in range(4) for y in range(2)]
    return lax.ppermute(value, "fsdp", pairs)


def ring_step(value, way):
    size = lax.axis_size("fsdp")
    pairs = []
    for base in range(0, size, GROUP):
        for at in range(GROUP):
            pairs.append((base + RING[at], base + RING[(at + way) % GROUP]))
    return lax.ppermute(value, "fsdp", pairs)


def spread_tensor(own):
    far = swap_x(own)
    near = swap_core(own)
    return own, near, far, swap_core(far)


def collect_tensor(part_0, part_1, part_2, part_3):
    far = (part_2.astype(f32) + swap_core(part_3.astype(bf)).astype(f32)).astype(bf)
    far = swap_x(far)
    near = part_0.astype(f32) + swap_core(part_1.astype(bf)).astype(f32)
    return near + far.astype(f32)


def pick(stack, index, axis=0):
    return lax.dynamic_index_in_dim(stack, index, axis, keepdims=False)


def spread_fsdp(own, fsdp_pos):
    if lax.axis_size("fsdp") != GROUP:
        return lax.all_gather(own, "fsdp", axis=0)
    z, y = fsdp_pos // 2, fsdp_pos % 2
    column = jnp.stack([own] + [shift_z(own, step) for step in (1, 2, 3)])
    both = jnp.concatenate([column, swap_bit(column, 1)])
    return jnp.stack(
        [
            pick(both, (z - zz) % 4 + 4 * jnp.where(y == yy, 0, 1))
            for zz in range(4)
            for yy in range(2)
        ]
    )


def collect_fsdp(parts, fsdp_pos):
    if lax.axis_size("fsdp") != GROUP:
        return lax.psum_scatter(parts.astype(bf), "fsdp", scatter_dimension=0).astype(f32)
    z, y = fsdp_pos // 2, fsdp_pos % 2
    paired = parts.reshape((4, 2) + parts.shape[1:])
    give = pick(paired, 1 - y, 1).astype(bf)
    column = pick(paired, y, 1).astype(f32) + swap_bit(give, 1).astype(f32)
    total = pick(column, z)
    for step in (1, 2, 3):
        total = total + shift_z(pick(column, (z + step) % 4).astype(bf), step).astype(f32)
    return total


def order_tensor(blocks, tensor_pos):
    odd = tensor_pos % 2 == 1
    high = tensor_pos // 2 == 1
    a, b, c, d = blocks
    a, b = jnp.where(odd, b, a), jnp.where(odd, a, b)
    c, d = jnp.where(odd, d, c), jnp.where(odd, c, d)
    return (
        jnp.where(high, c, a),
        jnp.where(high, d, b),
        jnp.where(high, a, c),
        jnp.where(high, b, d),
    )


def sum_all(value):
    value = value + swap_core(value)
    value = value + swap_x(value)
    bit = 1
    while bit < lax.axis_size("fsdp"):
        value = value + swap_bit(value, bit)
        bit *= 2
    return value


def ring_spread(first, second):
    firsts, seconds = [first], [second]
    for _ in range(GROUP - 1):
        firsts.append(ring_step(firsts[-1], 1))
        seconds.append(ring_step(seconds[-1], -1))
    return firsts, seconds


def ring_collect(take_first, take_second):
    first, second = take_first(GROUP - 1), take_second(GROUP - 1)
    for s in reversed(range(GROUP - 1)):
        moved_first = ring_step(first.astype(bf), -1)
        moved_second = ring_step(second.astype(bf), 1)
        first = moved_first.astype(f32) + take_first(s)
        second = moved_second.astype(f32) + take_second(s)
    return first, second


def rms_scale(tensor_in, gain_vec):
    return (
        tensor_in
        * lax.rsqrt(jnp.mean(tensor_in * tensor_in, axis=-1, keepdims=True) + eps_norm)
        * (1.0 + gain_vec)
    )


def rotate(tensor_in, cosine, sine_part):
    half_dim = tensor_in.shape[-1] // 2
    first_half = tensor_in[..., :half_dim]
    second_half = tensor_in[..., half_dim:]
    return jnp.concatenate(
        [
            first_half * cosine - second_half * sine_part,
            second_half * cosine + first_half * sine_part,
        ],
        axis=-1,
    )


def head_prep(raw_in, gain_vec, cosine, sine_part):
    return rotate(rms_scale(raw_in, gain_vec), cosine, sine_part)


def dot_nn(left, right):
    return jnp.dot(left, right, preferred_element_type=f32)


def dot_tn(left, right):
    return lax.dot_general(left, right, (((0,), (0,)), ((), ())), preferred_element_type=f32)


def dot_nt(left, right):
    return lax.dot_general(left, right, (((1,), (1,)), ((), ())), preferred_element_type=f32)


def masked_scores(query, keys, mask):
    scores = dot_nt(query, keys) * score_scale
    return jnp.where(mask, scores.reshape(HEADS, PSLICE, -1), masked_score)


def attend(query, pairs, mask):
    scores = masked_scores(query, pairs[:, :HEAD], mask)
    row_max = jnp.max(scores, axis=-1, keepdims=True)
    shifted = jnp.exp(scores - row_max)
    row_sum = jnp.sum(shifted, axis=-1, keepdims=True)
    probs = (shifted / row_sum).reshape(HEADS * PSLICE, -1)
    return dot_nn(probs.astype(bf), pairs[:, HEAD:]), row_max + jnp.log(row_sum)


def attend_back(query, pairs, mask, log_sum, grad_out):
    scores = masked_scores(query, pairs[:, :HEAD], mask)
    probs = jnp.exp(scores - log_sum).reshape(HEADS * PSLICE, -1)
    grad_probs = dot_nt(grad_out, pairs[:, HEAD:])
    row_dot = jnp.sum(probs * grad_probs, axis=-1, keepdims=True)
    grad_scores = (probs * (grad_probs - row_dot)).astype(bf)
    grad_query = dot_nn(grad_scores, pairs[:, :HEAD]) * score_scale
    grad_keys = dot_tn(grad_scores, query) * score_scale
    grad_values = dot_tn(probs.astype(bf), grad_out)
    return grad_query, jnp.concatenate([grad_keys, grad_values], 1)


def local(
    layer_in,
    teacher,
    query_proj,
    key_proj,
    value_proj,
    out_proj,
    gate_proj,
    up_proj,
    down_proj,
    attn_norm,
    attn_post,
    ffw_norm,
    ffw_post,
    query_norm,
    key_norm,
    cont_prompt,
    cont_length,
    token_count,
    loss_scale,
):
    members = lax.axis_size("fsdp")
    fsdp_pos = lax.axis_index("fsdp")
    tensor_pos = lax.axis_index("tensor")
    core, side = tensor_pos % 2, tensor_pos // 2
    is_cont = side == 1
    group_slot = fsdp_pos % GROUP
    place = jnp.array(PLACE, jnp.int32)[group_slot]
    ring_of = jnp.array(RING, jnp.int32)
    dim = layer_in.shape[1]
    hidden = gate_proj.shape[1]
    whole_ring = members == GROUP

    shard_kv = key_proj.shape[0]
    shard_gain, shard_head = attn_norm.shape[0], query_norm.shape[0]
    gains_own = jnp.concatenate([attn_norm, attn_post, ffw_norm, ffw_post, query_norm, key_norm])
    gains_own = jnp.pad(gains_own, (0, 2 * HEAD - gains_own.shape[0]))
    packed = jnp.concatenate([jnp.concatenate([key_proj, value_proj], 1), gains_own[None]], 0)
    packed = jnp.pad(packed, ((0, -packed.shape[0] % 8), (0, 0)))
    packed_all = jnp.stack(
        order_tensor(spread_tensor(spread_fsdp(packed, fsdp_pos)), tensor_pos), 1
    )
    kv_full = packed_all[:, :, :shard_kv].reshape(dim, 2 * HEAD)
    gains_all = packed_all[:, :, shard_kv].astype(f32)

    def gain_of(number):
        start = number * shard_gain
        return gains_all[:, :, start : start + shard_gain].reshape(dim)

    def head_gain_of(number):
        start = 4 * shard_gain + number * shard_head
        return gains_all[:, :, start : start + shard_head].reshape(HEAD)

    attn_gain, attn_post_gain, ffw_gain, ffw_post_gain = (gain_of(k) for k in range(4))
    query_gain, key_gain = head_gain_of(0), head_gain_of(1)

    qo_own = jnp.concatenate([query_proj, out_proj.T], 1)
    qo_column = spread_fsdp(qo_own, fsdp_pos).reshape(dim, 2 * HEAD)
    qo_blocks = spread_tensor(qo_column)
    query_full = jnp.concatenate([block[:, :HEAD] for block in qo_blocks], 1)
    out_full = jnp.concatenate([block[:, HEAD:] for block in qo_blocks], 1)

    down_own = down_proj.T
    if whole_ring:
        rows = gate_proj.shape[0]
        cut = 80
        firsts, seconds = ring_spread(
            jnp.concatenate([gate_proj, down_own[:cut]], 0),
            jnp.concatenate([up_proj, down_own[cut:]], 0),
        )
        gate_full = jnp.zeros((dim, hidden), bf)
        up_full = jnp.zeros((dim, hidden), bf)
        down_full = jnp.zeros((dim, hidden), bf)
        for s in range(GROUP):
            at_first = ring_of[(place - s) % GROUP] * rows
            at_second = ring_of[(place + s) % GROUP] * rows
            gate_full = lax.dynamic_update_slice(gate_full, firsts[s][:rows], (at_first, 0))
            down_full = lax.dynamic_update_slice(down_full, firsts[s][rows:], (at_first, 0))
            up_full = lax.dynamic_update_slice(up_full, seconds[s][:rows], (at_second, 0))
            down_full = lax.dynamic_update_slice(
                down_full, seconds[s][rows:], (at_second + cut, 0)
            )
    else:
        gate_full = lax.all_gather(gate_proj, "fsdp", axis=0, tiled=True)
        up_full = lax.all_gather(up_proj, "fsdp", axis=0, tiled=True)
        down_full = lax.all_gather(down_own, "fsdp", axis=0, tiled=True)

    local_rows = layer_in.shape[0]
    unit_ids = jnp.arange(local_rows, dtype=jnp.int32) % PSLICE
    positions = unit_ids + jnp.where(is_cont, PROMPT, group_slot * PSLICE)
    inverse_freq = jnp.exp(
        -math.log(rope_base) * 2.0 * jnp.arange(HEAD // 2, dtype=f32) / HEAD
    )
    angles = positions.astype(f32)[:, None] * inverse_freq[None, :]
    cosine, sine_part = jnp.cos(angles), jnp.sin(angles)
    input_f = layer_in.astype(f32)
    normed_in = rms_scale(input_f, attn_gain).astype(bf)

    kv_raw = dot_nn(normed_in, kv_full)
    key_raw = kv_raw[:, :HEAD]
    key_rot = head_prep(key_raw, key_gain, cosine, sine_part).astype(bf)
    own_pairs = jnp.concatenate([key_rot, kv_raw[:, HEAD:].astype(bf)], 1)
    across = lax.ppermute(own_pairs, "tensor", [(0, 2), (1, 3)])
    prompt_pairs = jnp.where(is_cont, across, own_pairs)
    pair_firsts, pair_seconds = ring_spread(prompt_pairs[:PSLICE], prompt_pairs[PSLICE:])
    held = jnp.stack([jnp.concatenate(pair_firsts), jnp.concatenate(pair_seconds)])
    held = jnp.concatenate([held, lax.ppermute(held, "tensor", [(2, 3), (3, 2)])])

    query_raw = dot_nn(normed_in, query_full)
    query_heads = [
        head_prep(query_raw[:, h * HEAD : (h + 1) * HEAD], query_gain, cosine, sine_part).astype(bf)
        for h in range(HEADS)
    ]

    row_of = lax.broadcasted_iota(jnp.int32, (PSLICE, PSLICE), 0)
    key_of = lax.broadcasted_iota(jnp.int32, (PSLICE, PSLICE), 1)
    steps = jnp.arange(GROUP, dtype=jnp.int32)
    units = []
    outs = []
    for unit in range(UNITS):
        way = 1 if unit == 0 else -1
        source = ring_of[(place - way * steps) % GROUP]
        length = cont_length[core * UNITS + unit]
        mapped = cont_prompt[core * UNITS + unit]
        index = jnp.where(
            is_cont, jnp.where(mapped // UNITS == core, 0, UNITS) + mapped % UNITS, unit
        )
        triangle = key_of <= row_of
        mask = jnp.concatenate(
            [
                is_cont
                | (source[s] < group_slot)
                | ((source[s] == group_slot) & triangle)
                for s in range(GROUP)
            ]
            + [is_cont & triangle & (key_of < length)],
            1,
        )
        at = slice(unit * PSLICE, (unit + 1) * PSLICE)
        query = jnp.concatenate([head[at] for head in query_heads], 0)
        pairs = jnp.concatenate([pick(held, index), own_pairs[at]], 0)
        out, log_sum = attend(query, pairs, mask)
        units.append((query, pairs, mask, log_sum, index))
        out = out.astype(bf)
        outs.append(
            jnp.concatenate([out[h * PSLICE : (h + 1) * PSLICE] for h in range(HEADS)], 1)
        )
    attn_low = jnp.concatenate(outs, 0)
    attn_sum = dot_nt(attn_low, out_full)
    mixed = input_f + rms_scale(attn_sum, attn_post_gain)
    normed_mid = rms_scale(mixed, ffw_gain).astype(bf)

    mid_blocks = spread_tensor(normed_mid)
    mid_halves = [jnp.concatenate(mid_blocks[:2], 0), jnp.concatenate(mid_blocks[2:], 0)]
    gates, ups, acts, downs = [], [], [], []
    for mid in mid_halves:
        gate_raw, up_raw = dot_nn(mid, gate_full), dot_nn(mid, up_full)
        act = (jax.nn.gelu(gate_raw, approximate=True) * up_raw).astype(bf)
        down = dot_nt(act, down_full).astype(bf)
        gates.append(gate_raw)
        ups.append(up_raw)
        acts.append(act)
        downs += [down[:local_rows], down[local_rows:]]
    ffw_sum = collect_tensor(*downs)
    result = mixed + rms_scale(ffw_sum, ffw_post_gain)

    row_length = jnp.where(
        jnp.arange(local_rows) < PSLICE,
        cont_length[core * UNITS],
        cont_length[core * UNITS + 1],
    )
    live_rows = jnp.where(is_cont & (unit_ids >= row_length), 0.0, 1.0).astype(f32)
    diff = result - teacher.astype(f32)
    loss_part = jnp.sum(live_rows[:, None] * diff * diff)
    count_f = token_count.astype(f32)
    grad_result = loss_scale / count_f * 2.0 * live_rows[:, None] * diff

    _, ffw_pull = jax.vjp(rms_scale, ffw_sum, ffw_post_gain)
    grad_ffw_sum, grad_ffw_post_gain = ffw_pull(grad_result)
    grad_blocks = spread_tensor(grad_ffw_sum.astype(bf))
    grad_halves = [jnp.concatenate(grad_blocks[:2], 0), jnp.concatenate(grad_blocks[2:], 0)]
    gate_lows, up_lows, mids = [], [], []
    for half in range(2):
        grad_act = dot_nn(grad_halves[half], down_full)
        _, act_pull = jax.vjp(
            lambda g, u: jax.nn.gelu(g, approximate=True) * u, gates[half], ups[half]
        )
        grad_gate, grad_up = act_pull(grad_act)
        gate_low, up_low = grad_gate.astype(bf), grad_up.astype(bf)
        mid = (dot_nt(gate_low, gate_full) + dot_nt(up_low, up_full)).astype(bf)
        gate_lows.append(gate_low)
        up_lows.append(up_low)
        mids += [mid[:local_rows], mid[local_rows:]]
    grad_mid = collect_tensor(*mids)
    mid_all = jnp.concatenate(mid_halves, 0)
    grad_down_w = dot_tn(jnp.concatenate(grad_halves, 0), jnp.concatenate(acts, 0)).astype(bf)
    grad_gate_w = dot_tn(mid_all, jnp.concatenate(gate_lows, 0)).astype(bf)
    grad_up_w = dot_tn(mid_all, jnp.concatenate(up_lows, 0)).astype(bf)
    if whole_ring:

        def take(wide, narrow, low, high, way):
            def term(s):
                start = ring_of[(place - way * s) % GROUP] * rows
                return jnp.concatenate(
                    [
                        lax.dynamic_slice(wide, (start, 0), (rows, hidden)),
                        lax.dynamic_slice(narrow, (start + low, 0), (high - low, hidden)),
                    ],
                    0,
                ).astype(f32)

            return term

        sum_first, sum_second = ring_collect(
            take(grad_gate_w, grad_down_w, 0, cut, 1),
            take(grad_up_w, grad_down_w, cut, rows, -1),
        )
        out_gate, out_up = sum_first[:rows], sum_second[:rows]
        out_down = jnp.concatenate([sum_first[rows:], sum_second[rows:]], 0).T
    else:
        out_gate, out_up, out_down = (
            lax.psum_scatter(part, "fsdp", scatter_dimension=0, tiled=True).astype(f32)
            for part in (grad_gate_w, grad_up_w, grad_down_w)
        )
        out_down = out_down.T

    _, mid_pull = jax.vjp(rms_scale, mixed, ffw_gain)
    grad_mixed_part, grad_ffw_gain = mid_pull(grad_mid)
    grad_mixed = grad_result + grad_mixed_part
    _, post_pull = jax.vjp(rms_scale, attn_sum, attn_post_gain)
    grad_attn_sum, grad_attn_post_gain = post_pull(grad_mixed)
    grad_attn_low = grad_attn_sum.astype(bf)
    grad_out_w = dot_tn(grad_attn_low, attn_low)
    grad_attn_rows = dot_nn(grad_attn_low, out_full).astype(bf)
    grad_query_units, grad_held, grad_own = [], [], []
    for unit in range(UNITS):
        query, pairs, mask, log_sum, index = units[unit]
        at = slice(unit * PSLICE, (unit + 1) * PSLICE)
        grad_rows = jnp.concatenate(
            [grad_attn_rows[at, h * HEAD : (h + 1) * HEAD] for h in range(HEADS)], 0
        )
        grad_query, grad_pairs = attend_back(query, pairs, mask, log_sum, grad_rows)
        grad_query_units.append(grad_query)
        grad_held.append(grad_pairs[:PROMPT])
        grad_own.append(grad_pairs[PROMPT:])

    def slot_grad(slot):
        total = 0.0
        for unit in range(UNITS):
            total = total + jnp.where(units[unit][4] == slot, grad_held[unit], 0.0)
        return total

    given = jnp.stack([slot_grad(2), slot_grad(3)]).astype(bf)
    given = lax.ppermute(given, "tensor", [(2, 3), (3, 2)])
    kept = [slot_grad(0) + given[0].astype(f32), slot_grad(1) + given[1].astype(f32)]
    ring_firsts, ring_seconds = ring_collect(
        lambda s: kept[0][s * PSLICE : (s + 1) * PSLICE],
        lambda s: kept[1][s * PSLICE : (s + 1) * PSLICE],
    )
    summed = jnp.concatenate([ring_firsts, ring_seconds], 0)
    back = lax.ppermute(summed.astype(bf), "tensor", [(2, 0), (3, 1)]).astype(f32)
    grad_pairs = jnp.where(is_cont, jnp.concatenate(grad_own, 0), summed + back)

    _, query_pull = jax.vjp(
        lambda raw, gain: tuple(
            head_prep(raw[:, h * HEAD : (h + 1) * HEAD], gain, cosine, sine_part)
            for h in range(HEADS)
        ),
        query_raw,
        query_gain,
    )
    grad_query_raw, grad_query_gain = query_pull(
        tuple(
            jnp.concatenate([g[h * PSLICE : (h + 1) * PSLICE] for g in grad_query_units], 0)
            for h in range(HEADS)
        )
    )
    _, key_pull = jax.vjp(
        lambda raw, gain: head_prep(raw, gain, cosine, sine_part), key_raw, key_gain
    )
    grad_key_raw, grad_key_gain = key_pull(grad_pairs[:, :HEAD])
    grad_query_low = grad_query_raw.astype(bf)
    grad_kv_low = jnp.concatenate([grad_key_raw, grad_pairs[:, HEAD:]], 1).astype(bf)
    grad_query_w = dot_tn(normed_in, grad_query_low)
    grad_kv_w = dot_tn(normed_in, grad_kv_low)
    grad_normed = dot_nt(grad_query_low, query_full) + dot_nt(grad_kv_low, kv_full)
    _, input_pull = jax.vjp(rms_scale, input_f, attn_gain)
    grad_input_part, grad_attn_gain = input_pull(grad_normed)
    grad_input = grad_mixed + grad_input_part

    def collect_heads(grad_w):
        column = collect_tensor(*(grad_w[:, h * HEAD : (h + 1) * HEAD] for h in range(HEADS)))
        return collect_fsdp(column.reshape(members, dim // members, HEAD), fsdp_pos)

    out_out = collect_heads(grad_out_w).T
    out_query = collect_heads(grad_query_w)
    kv_blocks = grad_kv_w.reshape(members, TENSOR, shard_kv, 2 * HEAD)
    kv_column = collect_tensor(
        *order_tensor([kv_blocks[:, t] for t in range(TENSOR)], tensor_pos)
    )
    out_kv = collect_fsdp(kv_column, fsdp_pos)

    small = jnp.concatenate(
        [
            grad_attn_gain,
            grad_attn_post_gain,
            grad_ffw_gain,
            grad_ffw_post_gain,
            grad_query_gain,
            grad_key_gain,
            loss_part[None],
        ]
    )
    length = small.shape[0]
    small = jnp.pad(small, (0, -length % 1024)).reshape(-1, 128)
    small = sum_all(small).reshape(-1)
    device = fsdp_pos * TENSOR + tensor_pos
    wide = [
        lax.dynamic_slice(small, (k * dim + device * shard_gain,), (shard_gain,)) for k in range(4)
    ]
    narrow = [
        lax.dynamic_slice(small, (4 * dim + k * HEAD + device * shard_head,), (shard_head,))
        for k in range(2)
    ]
    loss = small[length - 1] / count_f
    return (
        result.astype(bf),
        loss,
        grad_input.astype(bf),
        out_query,
        out_kv[:, :HEAD],
        out_kv[:, HEAD:],
        out_out,
        out_gate,
        out_up,
        out_down,
        *wide,
        *narrow,
    )


def solution(mesh):
    rows = P(("fsdp", "tensor"), None)
    split = P(("fsdp", "tensor"))
    inward, outward = P("fsdp", "tensor"), P("tensor", "fsdp")
    return jax.shard_map(
        local,
        mesh=mesh,
        in_specs=(
            rows,
            rows,
            inward,
            rows,
            rows,
            outward,
            inward,
            inward,
            outward,
            *(split,) * 6,
            P("fsdp"),
            P("fsdp"),
            P(),
            P(),
        ),
        out_specs=(
            rows,
            P(),
            rows,
            inward,
            rows,
            rows,
            outward,
            inward,
            inward,
            outward,
            *(split,) * 6,
        ),
        check_vma=False,
    )
```

```python
import functools
import math

import jax
import jax.numpy as jnp
import numpy as np
from jax import lax
from jax.experimental import pallas as pl
from jax.experimental.pallas import tpu as pltpu
from jax.sharding import PartitionSpec as P

HEAD = 256
HEADS = 4
PROMPT = 2048
CONT = 256
GROUP = 8
GROUPS_DEV = 4
PSLICE = 256
UNITS = 2
TENSOR = 4

RING = (0, 2, 4, 6, 7, 5, 3, 1)
PLACE = tuple(RING.index(member) for member in range(GROUP))

eps_norm = 1e-06
rope_base = 1000000.0
masked_score = -1e30
score_scale = 1.0 / math.sqrt(HEAD)
bf = jnp.bfloat16
f32 = jnp.float32


def swap_core(value):
    return lax.ppermute(value, "tensor", [(t, t ^ 1) for t in range(TENSOR)])


def swap_x(value):
    return lax.ppermute(value, "tensor", [(t, t ^ 2) for t in range(TENSOR)])


def swap_bit(value, bit):
    size = lax.axis_size("fsdp")
    return lax.ppermute(value, "fsdp", [(f, f ^ bit) for f in range(size)])


def shift_z(value, step):
    pairs = [(z * 2 + y, (z + step) % 4 * 2 + y) for z in range(4) for y in range(2)]
    return lax.ppermute(value, "fsdp", pairs)


def ring_step(value, way):
    size = lax.axis_size("fsdp")
    pairs = []
    for base in range(0, size, GROUP):
        for at in range(GROUP):
            pairs.append((base + RING[at], base + RING[(at + way) % GROUP]))
    return lax.ppermute(value, "fsdp", pairs)


def spread_tensor(own):
    far = swap_x(own)
    near = swap_core(own)
    return own, near, far, swap_core(far)


def spread_near(own):
    return swap_core(own), swap_x(own)


def collect_tensor(part_0, part_1, part_2, part_3):
    return collect_near(part_0, part_1, collect_far(part_2, part_3))


def collect_far(part_2, part_3):
    return (part_2.astype(f32) + swap_core(part_3.astype(bf)).astype(f32)).astype(bf)


def collect_near(part_0, part_1, far):
    far = swap_x(far)
    near = part_0.astype(f32) + swap_core(part_1.astype(bf)).astype(f32)
    return near + far.astype(f32)


def after(value, *earlier):
    return lax.optimization_barrier((value,) + earlier)[0]


def pick(stack, index, axis=0):
    return lax.dynamic_index_in_dim(stack, index, axis, keepdims=False)


def spread_fsdp(own, *earlier):
    if lax.axis_size("fsdp") != GROUP:
        return lax.all_gather(own, "fsdp", axis=0)
    column = jnp.stack([own] + [shift_z(own, step) for step in (1, 2, 3)])
    if earlier:
        column = after(column, *earlier)
    return jnp.concatenate([column, swap_bit(column, 1)])


def collect_fsdp(parts, fsdp_pos):
    if lax.axis_size("fsdp") != GROUP:
        return lax.psum_scatter(parts.astype(bf), "fsdp", scatter_dimension=0).astype(f32)
    z, y = fsdp_pos // 2, fsdp_pos % 2
    paired = parts.reshape((4, 2) + parts.shape[1:])
    give = pick(paired, 1 - y, 1).astype(bf)
    column = pick(paired, y, 1).astype(f32) + swap_bit(give, 1).astype(f32)
    total = pick(column, z)
    for step in (1, 2, 3):
        total = total + shift_z(pick(column, (z + step) % 4).astype(bf), step).astype(f32)
    return total


def order_tensor(blocks, tensor_pos):
    odd = tensor_pos % 2 == 1
    high = tensor_pos // 2 == 1
    a, b, c, d = blocks
    a, b = jnp.where(odd, b, a), jnp.where(odd, a, b)
    c, d = jnp.where(odd, d, c), jnp.where(odd, c, d)
    return (
        jnp.where(high, c, a),
        jnp.where(high, d, b),
        jnp.where(high, a, c),
        jnp.where(high, b, d),
    )


def sum_all(value):
    value = value + swap_core(value)
    value = value + swap_x(value)
    bit = 1
    while bit < lax.axis_size("fsdp"):
        value = value + swap_bit(value, bit)
        bit *= 2
    return value


class Spread:
    def __init__(self, first, second):
        self.firsts, self.seconds = [first], [second]

    def step(self, *earlier):
        first, second = self.firsts[-1], self.seconds[-1]
        if earlier:
            first, second = after(first, *earlier), after(second, *earlier)
        self.firsts.append(ring_step(first, 1))
        self.seconds.append(ring_step(second, -1))
        return self.firsts[-1], self.seconds[-1]


class Collect:
    def __init__(self, take_first, take_second):
        self.take_first, self.take_second = take_first, take_second
        self.at = GROUP - 1
        self.first, self.second = take_first(self.at), take_second(self.at)

    def step(self, *earlier):
        first, second = self.first.astype(bf), self.second.astype(bf)
        if earlier:
            first, second = after(first, *earlier), after(second, *earlier)
        self.at -= 1
        self.first = ring_step(first, -1).astype(f32) + self.take_first(self.at)
        self.second = ring_step(second, 1).astype(f32) + self.take_second(self.at)
        return self.first, self.second


def rms_scale(tensor_in, gain_vec):
    return (
        tensor_in
        * lax.rsqrt(jnp.mean(tensor_in * tensor_in, axis=-1, keepdims=True) + eps_norm)
        * (1.0 + gain_vec)
    )


def rotate(tensor_in, cosine, sine_part):
    half_dim = tensor_in.shape[-1] // 2
    first_half = tensor_in[..., :half_dim]
    second_half = tensor_in[..., half_dim:]
    return jnp.concatenate(
        [
            first_half * cosine - second_half * sine_part,
            second_half * cosine + first_half * sine_part,
        ],
        axis=-1,
    )


def head_prep(raw_in, gain_vec, cosine, sine_part):
    return rotate(rms_scale(raw_in, gain_vec), cosine, sine_part)


def dot_nn(left, right):
    return jnp.dot(left, right, preferred_element_type=f32)


def dot_tn(left, right):
    return lax.dot_general(left, right, (((0,), (0,)), ((), ())), preferred_element_type=f32)


def dot_nt(left, right):
    return lax.dot_general(left, right, (((1,), (1,)), ((), ())), preferred_element_type=f32)


AT_FSDP, AT_TENSOR, AT_REACH, AT_CONT, AT_CORE = 0, 64, 68, 84, 85
TABLE_WIDTH = 128
FAR = 1 << 20


def place_table(members):
    table = np.zeros((members * TENSOR, TABLE_WIDTH), np.int32)
    for f in range(members):
        slot = f % GROUP
        place = PLACE[slot]
        for t in range(TENSOR):
            row = table[f * TENSOR + t]
            for r in range(members):
                if members == GROUP:
                    row[AT_FSDP + r] = (f // 2 - r % 4) % 4 * 2 + (f % 2 ^ r // 4)
                else:
                    row[AT_FSDP + r] = r
            row[AT_TENSOR : AT_TENSOR + TENSOR] = [t ^ j for j in range(TENSOR)]
            for unit in range(UNITS):
                for s in range(GROUP):
                    source = RING[(place - s * (1 - 2 * unit)) % GROUP]
                    reach = FAR if t // 2 else (slot - source) * PSLICE
                    row[AT_REACH + unit * GROUP + s] = reach
            row[AT_CONT], row[AT_CORE] = t // 2, t % 2
    return table


KEYS = PROMPT + CONT
CHUNKS = 2 * UNITS * GROUP
smem = pl.BlockSpec(memory_space=pltpu.SMEM)
anywhere = pl.BlockSpec(memory_space=pl.ANY)


def place_kernel(table, *refs):
    for j in range(TENSOR):
        refs[TENSOR][0, table[AT_TENSOR + j]] = refs[j][0]


def place(table, blocks):
    members, rows, width = blocks[0].shape
    return pl.pallas_call(
        place_kernel,
        out_shape=jax.ShapeDtypeStruct((members, TENSOR, rows, width), bf),
        grid_spec=pltpu.PrefetchScalarGridSpec(
            num_scalar_prefetch=1,
            grid=(members,),
            in_specs=[pl.BlockSpec((1, rows, width), lambda r, table: (r, 0, 0))] * TENSOR,
            out_specs=pl.BlockSpec(
                (1, TENSOR, rows, width), lambda r, table: (table[AT_FSDP + r], 0, 0, 0)
            ),
        ),
        name="place_pairs",
    )(table, *blocks)


def place_heads_kernel(table, *refs):
    query_ref, out_ref = refs[TENSOR:]
    for j in range(TENSOR):
        at = slice(j * HEAD, (j + 1) * HEAD)
        query_ref[0, :, at] = refs[j][0, :, :HEAD]
        out_ref[0, :, at] = refs[j][0, :, HEAD:]


def place_heads(table, blocks):
    members, rows, width = blocks[0].shape
    shape = jax.ShapeDtypeStruct((members, rows, HEADS * HEAD), bf)
    spec = pl.BlockSpec(
        (1, rows, HEADS * HEAD), lambda r, table: (table[AT_FSDP + r], 0, 0)
    )
    return pl.pallas_call(
        place_heads_kernel,
        out_shape=(shape, shape),
        grid_spec=pltpu.PrefetchScalarGridSpec(
            num_scalar_prefetch=1,
            grid=(members,),
            in_specs=[pl.BlockSpec((1, rows, width), lambda r, table: (r, 0, 0))] * TENSOR,
            out_specs=(spec, spec),
        ),
        name="place_heads",
    )(table, *blocks)


def slot_of(table, mapped, unit):
    core = table[AT_CORE]
    target = mapped[core * UNITS + unit]
    other = jnp.where(target // UNITS == core, 0, UNITS)
    return jnp.where(table[AT_CONT] == 1, other + target % UNITS, unit)


def load_pairs(table, mapped, chunks, own_ref, pairs, sems, unit, start):
    slot = slot_of(table, mapped, unit)
    for s in range(GROUP):
        for option in range(2 * UNITS):

            @pl.when(slot == option)
            def _(s=s, option=option):
                copy = pltpu.make_async_copy(
                    chunks[option * GROUP + s],
                    pairs.at[unit, pl.ds(s * PSLICE, PSLICE)],
                    sems.at[unit, s],
                )
                copy.start() if start else copy.wait()

    copy = pltpu.make_async_copy(
        own_ref.at[pl.ds(unit * PSLICE, PSLICE)],
        pairs.at[unit, pl.ds(PROMPT, CONT)],
        sems.at[unit, GROUP],
    )
    copy.start() if start else copy.wait()


def all_pairs(table, mapped, chunks, own_ref, pairs, sems):
    unit, head = pl.program_id(0), pl.program_id(1)

    @pl.when((unit == 0) & (head == 0))
    def _():
        for number in range(UNITS):
            load_pairs(table, mapped, chunks, own_ref, pairs, sems, number, True)

    for number in range(UNITS):

        @pl.when((unit == number) & (head == 0))
        def _(number=number):
            load_pairs(table, mapped, chunks, own_ref, pairs, sems, number, False)


def masked(table, length, scores, unit):
    key_of = lax.broadcasted_iota(jnp.int32, (PSLICE, PSLICE), 0)
    lag = key_of - lax.broadcasted_iota(jnp.int32, (PSLICE, PSLICE), 1)
    parts = []
    for s in range(GROUP):
        reach = table[AT_REACH + unit * GROUP + s]
        part = scores[s * PSLICE : (s + 1) * PSLICE]
        parts.append(jnp.where(lag <= reach, part, masked_score))
    live = length[table[AT_CORE] * UNITS + unit]
    live = jnp.where(table[AT_CONT] == 1, live, 0)
    parts.append(jnp.where((lag <= 0) & (key_of < live), scores[PROMPT:], masked_score))
    return jnp.concatenate(parts, 0)


def attend_kernel(table, mapped, length, query_ref, own_ref, *refs):
    chunks = refs[:CHUNKS]
    out_ref, sum_ref, pairs, values_t, sems = refs[CHUNKS:]
    unit, head = pl.program_id(0), pl.program_id(1)
    all_pairs(table, mapped, chunks, own_ref, pairs, sems)

    @pl.when(head == 0)
    def _():
        values_t[...] = pairs[unit, :, HEAD:].T

    query = query_ref[...] * score_scale
    scores = masked(table, length, dot_nt(pairs[unit, :, :HEAD], query), unit)
    top = jnp.max(scores, axis=0, keepdims=True)
    shifted = jnp.exp(scores - top)
    total = jnp.sum(shifted, axis=0, keepdims=True)
    out = dot_nn(values_t[...], shifted.astype(bf)) / total
    out_ref[...] = out.T.astype(bf)
    sum_ref[0] = top + jnp.log(total)


unit_head = pl.BlockSpec((PSLICE, HEAD), lambda u, h: (u, h))
sum_spec = pl.BlockSpec((1, 1, PSLICE), lambda u, h: (u * HEADS + h, 0, 0))


def attend(table, mapped, length, query, own_pairs, chunks):
    rows = UNITS * PSLICE
    return pl.pallas_call(
        attend_kernel,
        out_shape=(
            jax.ShapeDtypeStruct((rows, HEADS * HEAD), bf),
            jax.ShapeDtypeStruct((UNITS * HEADS, 1, PSLICE), f32),
        ),
        grid=(UNITS, HEADS),
        in_specs=[smem, smem, smem, unit_head, anywhere] + [anywhere] * CHUNKS,
        out_specs=(unit_head, sum_spec),
        scratch_shapes=[
            pltpu.VMEM((UNITS, KEYS, 2 * HEAD), bf),
            pltpu.VMEM((HEAD, KEYS), bf),
            pltpu.SemaphoreType.DMA((UNITS, GROUP + 1)),
        ],
        compiler_params=pltpu.CompilerParams(vmem_limit_bytes=40 << 20),
        cost_estimate=pl.CostEstimate(
            flops=4 * rows * HEADS * KEYS * HEAD,
            bytes_accessed=2 * KEYS * 2 * HEAD * 2 + 4 * rows * HEADS * HEAD,
            transcendentals=rows * HEADS * KEYS,
        ),
        name="attend",
    )(table, mapped, length, query, own_pairs, *chunks)


def attend_back_kernel(table, mapped, length, query_ref, grad_ref, sum_ref, own_ref, *refs):
    chunks = refs[:CHUNKS]
    grad_query_ref, kept_ref, given_ref, grad_own_ref, pairs, keys_t, grads, sems = refs[CHUNKS:]
    unit, head = pl.program_id(0), pl.program_id(1)
    all_pairs(table, mapped, chunks, own_ref, pairs, sems)

    @pl.when(head == 0)
    def _():
        keys_t[...] = pairs[unit, :, :HEAD].T
        grads[unit] = jnp.zeros((KEYS, 2 * HEAD), f32)

    query = query_ref[...] * score_scale
    grad = grad_ref[...]
    scores = masked(table, length, dot_nt(pairs[unit, :, :HEAD], query), unit)
    probs = jnp.exp(scores - sum_ref[0])
    grad_probs = dot_nt(pairs[unit, :, HEAD:], grad)
    row_dot = jnp.sum(probs * grad_probs, axis=0, keepdims=True)
    grad_scores = (probs * (grad_probs - row_dot)).astype(bf)
    grads[unit, :, :HEAD] += dot_nn(grad_scores, query)
    grads[unit, :, HEAD:] += dot_nn(probs.astype(bf), grad)
    grad_query_ref[...] = dot_nn(keys_t[...], grad_scores).T * score_scale

    @pl.when((unit == UNITS - 1) & (head == HEADS - 1))
    def _():
        slots = [slot_of(table, mapped, number) for number in range(UNITS)]
        for s in range(GROUP):
            at = slice(s * PSLICE, (s + 1) * PSLICE)
            for option in range(2 * UNITS):
                total = jnp.zeros((PSLICE, 2 * HEAD), f32)
                for number in range(UNITS):
                    total += jnp.where(slots[number] == option, grads[number, at], 0.0)
                target = kept_ref if option < UNITS else given_ref
                target[option % UNITS, at] = total.astype(bf)
        for number in range(UNITS):
            grad_own_ref[number * PSLICE : (number + 1) * PSLICE] = grads[number, PROMPT:]


def attend_back(table, mapped, length, query, grad, log_sum, own_pairs, chunks):
    rows = UNITS * PSLICE
    whole = pl.BlockSpec(memory_space=pltpu.VMEM)
    return pl.pallas_call(
        attend_back_kernel,
        out_shape=(
            jax.ShapeDtypeStruct((rows, HEADS * HEAD), f32),
            jax.ShapeDtypeStruct((UNITS, PROMPT, 2 * HEAD), bf),
            jax.ShapeDtypeStruct((UNITS, PROMPT, 2 * HEAD), bf),
            jax.ShapeDtypeStruct((rows, 2 * HEAD), f32),
        ),
        grid=(UNITS, HEADS),
        in_specs=[smem, smem, smem, unit_head, unit_head, sum_spec, anywhere]
        + [anywhere] * CHUNKS,
        out_specs=(unit_head, whole, whole, whole),
        scratch_shapes=[
            pltpu.VMEM((UNITS, KEYS, 2 * HEAD), bf),
            pltpu.VMEM((HEAD, KEYS), bf),
            pltpu.VMEM((UNITS, KEYS, 2 * HEAD), f32),
            pltpu.SemaphoreType.DMA((UNITS, GROUP + 1)),
        ],
        compiler_params=pltpu.CompilerParams(vmem_limit_bytes=56 << 20),
        cost_estimate=pl.CostEstimate(
            flops=10 * rows * HEADS * KEYS * HEAD,
            bytes_accessed=2 * KEYS * 2 * HEAD * 6 + 10 * rows * HEADS * HEAD,
            transcendentals=rows * HEADS * KEYS,
        ),
        name="attend_back",
    )(table, mapped, length, query, grad, log_sum, own_pairs, *chunks)


GELU_SCALE = math.sqrt(2.0 / math.pi)
GELU_CUBE = 0.044715


def gelu_parts(gate):
    bent = jnp.tanh(GELU_SCALE * (gate + GELU_CUBE * (gate * gate * gate)))
    return bent, 0.5 * (1.0 + bent)


def whole_weight(ref):
    return ref[...].reshape(-1, ref.shape[-1])


def pick_rows(first_ref, second_ref, rows):
    step = pl.program_id(0)

    @pl.when(step == 0)
    def _():
        rows[...] = first_ref[...]

    @pl.when(step == 1)
    def _():
        rows[...] = second_ref[...]


def put_rows(first_ref, second_ref, total):
    step = pl.program_id(0)

    @pl.when(step == 0)
    def _():
        first_ref[...] = total

    @pl.when(step == 1)
    def _():
        second_ref[...] = total


def feed_kernel(first_ref, second_ref, gate_w, up_w, down_w, *refs):
    gate_ref, up_ref, act_ref, first_out, second_out, rows = refs
    pick_rows(first_ref, second_ref, rows)
    gate = dot_nn(rows[...], whole_weight(gate_w))
    up = dot_nn(rows[...], whole_weight(up_w))
    act = (gate * gelu_parts(gate)[1] * up).astype(bf)
    gate_ref[...] = gate.astype(bf)
    up_ref[...] = up.astype(bf)
    act_ref[...] = act
    put_rows(first_out, second_out, dot_nt(act, whole_weight(down_w)).astype(bf))


def feed_back_kernel(first_ref, second_ref, gate_ref, up_ref, gate_w, up_w, down_w, *refs):
    gate_out, up_out, first_out, second_out, rows = refs
    pick_rows(first_ref, second_ref, rows)
    grad_act = dot_nn(rows[...], whole_weight(down_w))
    gate, up = gate_ref[...].astype(f32), up_ref[...].astype(f32)
    bent, share = gelu_parts(gate)
    slope = share + 0.5 * gate * (1.0 - bent * bent) * (
        GELU_SCALE * (1.0 + 3.0 * GELU_CUBE * (gate * gate))
    )
    grad_gate = (grad_act * up * slope).astype(bf)
    grad_up = (grad_act * (gate * share)).astype(bf)
    gate_out[...] = grad_gate
    up_out[...] = grad_up
    total = dot_nt(grad_gate, whole_weight(gate_w)) + dot_nt(grad_up, whole_weight(up_w))
    put_rows(first_out, second_out, total.astype(bf))


def feed_call(kernel, name, first, second, hiddens, weights, n_out):
    rows, dim = first.shape
    parts, _, depth, hidden = weights.shape
    fixed = pl.BlockSpec((rows, dim), lambda i: (0, 0))
    wide = pl.BlockSpec((rows, hidden), lambda i: (i, 0))
    held = [
        pl.BlockSpec(
            (parts, 1, depth, hidden), lambda i, k=k: (0, k, 0, 0), pipeline_mode=pl.Buffered(1)
        )
        for k in range(3)
    ]
    row_shape = jax.ShapeDtypeStruct((rows, dim), bf)
    wide_shape = jax.ShapeDtypeStruct((2 * rows, hidden), bf)
    return pl.pallas_call(
        kernel,
        out_shape=(wide_shape,) * n_out + (row_shape, row_shape),
        grid=(2,),
        in_specs=[fixed, fixed] + [wide] * len(hiddens) + held,
        out_specs=(wide,) * n_out + (fixed, fixed),
        scratch_shapes=[pltpu.VMEM((rows, dim), bf)],
        compiler_params=pltpu.CompilerParams(vmem_limit_bytes=60 << 20),
        cost_estimate=pl.CostEstimate(
            flops=12 * rows * dim * hidden,
            bytes_accessed=6 * dim * hidden + 2 * rows * hidden * 2 * (n_out + len(hiddens)),
            transcendentals=2 * rows * hidden,
        ),
        name=name,
    )(first, second, *hiddens, weights, weights, weights)


def weight_grad_kernel(number, *refs):
    blocks, halves = refs[:TENSOR], refs[TENSOR : TENSOR + 2 * number]
    out_ref, turned = refs[TENSOR + 2 * number :]
    rows = blocks[0].shape[0]

    @pl.when(pl.program_id(0) == 0)
    def _():
        for j in range(TENSOR):
            turned[:, j * rows : (j + 1) * rows] = blocks[j][...].T

    for k in range(number):
        total = dot_nn(turned[:, : 2 * rows], halves[2 * k][...])
        total += dot_nn(turned[:, 2 * rows :], halves[2 * k + 1][...])
        out_ref[:, k] = total.astype(bf).reshape(out_ref.shape[0], out_ref.shape[2], -1)


def weight_grads(name, blocks, halves, parts):
    rows, dim = blocks[0].shape
    hidden = halves[0].shape[1]
    number = len(halves) // 2
    width = 256
    return pl.pallas_call(
        functools.partial(weight_grad_kernel, number),
        out_shape=jax.ShapeDtypeStruct((parts, number, dim // parts, hidden), bf),
        grid=(pl.cdiv(hidden, width),),
        in_specs=[pl.BlockSpec((rows, dim), lambda i: (0, 0), pipeline_mode=pl.Buffered(1))]
        * TENSOR
        + [pl.BlockSpec((2 * rows, width), lambda i: (0, i))] * (2 * number),
        out_specs=pl.BlockSpec((parts, number, dim // parts, width), lambda i: (0, 0, 0, i)),
        scratch_shapes=[pltpu.VMEM((dim, TENSOR * rows), bf)],
        compiler_params=pltpu.CompilerParams(vmem_limit_bytes=48 << 20),
        cost_estimate=pl.CostEstimate(
            flops=8 * number * rows * dim * hidden,
            bytes_accessed=8 * rows * dim + number * (8 * rows + 2 * dim) * hidden,
            transcendentals=0,
        ),
        name=name,
    )(*blocks, *halves)


def local(
    layer_in,
    teacher,
    query_proj,
    key_proj,
    value_proj,
    out_proj,
    gate_proj,
    up_proj,
    down_proj,
    attn_norm,
    attn_post,
    ffw_norm,
    ffw_post,
    query_norm,
    key_norm,
    cont_prompt,
    cont_length,
    token_count,
    loss_scale,
):
    members = lax.axis_size("fsdp")
    fsdp_pos = lax.axis_index("fsdp")
    tensor_pos = lax.axis_index("tensor")
    core, side = tensor_pos % 2, tensor_pos // 2
    is_cont = side == 1
    group_slot = fsdp_pos % GROUP
    table = lax.dynamic_index_in_dim(
        jnp.asarray(place_table(members)), fsdp_pos * TENSOR + tensor_pos, 0, keepdims=False
    )
    dim = layer_in.shape[1]

    shard_kv = key_proj.shape[0]
    shard_gain, shard_head = attn_norm.shape[0], query_norm.shape[0]
    gains_own = jnp.stack(
        [
            jnp.pad(gain, (0, 2 * HEAD - gain.shape[0]))
            for gain in (attn_norm, attn_post, ffw_norm, ffw_post, query_norm, key_norm)
        ]
    )
    packed = jnp.concatenate([jnp.concatenate([key_proj, value_proj], 1), gains_own], 0)
    packed = jnp.pad(packed, ((0, -packed.shape[0] % 16), (0, 0)))
    packed_all = place(table, spread_tensor(spread_fsdp(packed)))
    kv_full = packed_all[:, :, :shard_kv].reshape(dim, 2 * HEAD)
    gains_all = packed_all[:, :, shard_kv : shard_kv + 6].astype(f32)

    def gain_of(number):
        return gains_all[:, :, number, :shard_gain].reshape(dim)

    def head_gain_of(number):
        return gains_all[:, :, 4 + number, :shard_head].reshape(HEAD)

    attn_gain, attn_post_gain, ffw_gain, ffw_post_gain = (gain_of(k) for k in range(4))
    query_gain, key_gain = head_gain_of(0), head_gain_of(1)

    local_rows = layer_in.shape[0]
    unit_ids = jnp.arange(local_rows, dtype=jnp.int32) % PSLICE
    positions = unit_ids + jnp.where(is_cont, PROMPT, group_slot * PSLICE)
    inverse_freq = jnp.exp(
        -math.log(rope_base) * 2.0 * jnp.arange(HEAD // 2, dtype=f32) / HEAD
    )
    angles = positions.astype(f32)[:, None] * inverse_freq[None, :]
    cosine, sine_part = jnp.cos(angles), jnp.sin(angles)
    input_f = layer_in.astype(f32)
    normed_in = rms_scale(input_f, attn_gain).astype(bf)

    three = (gate_proj, up_proj, down_proj.T)
    if members == GROUP:
        parts = GROUP
        weights = lax.all_gather(jnp.stack(three), "fsdp", axis=0)
    else:
        parts = 1
        weights = jnp.stack([lax.all_gather(w, "fsdp", axis=0, tiled=True) for w in three])[None]

    kv_raw = dot_nn(normed_in, kv_full)
    key_raw = kv_raw[:, :HEAD]
    key_rot = head_prep(key_raw, key_gain, cosine, sine_part).astype(bf)
    own_pairs = jnp.concatenate([key_rot, kv_raw[:, HEAD:].astype(bf)], 1)
    across = lax.ppermute(own_pairs, "tensor", [(0, 2), (1, 3)])
    prompt_pairs = jnp.where(is_cont, across, own_pairs)
    prompts = Spread(prompt_pairs[:PSLICE], prompt_pairs[PSLICE:])
    passed = [prompts.step() for _ in range(GROUP - 1)]
    chunks = prompts.firsts + prompts.seconds
    chunks = chunks + [lax.ppermute(chunk, "tensor", [(2, 3), (3, 2)]) for chunk in chunks]

    qo_own = jnp.concatenate([query_proj, out_proj.T], 1)
    qo_column = after(spread_fsdp(after(qo_own, packed_all), *passed[0]), *passed[2])
    query_full, out_full = (
        part.reshape(dim, HEADS * HEAD)
        for part in place_heads(table, spread_tensor(qo_column))
    )
    query_raw = dot_nn(normed_in, query_full)
    query_heads = [
        head_prep(query_raw[:, h * HEAD : (h + 1) * HEAD], query_gain, cosine, sine_part).astype(bf)
        for h in range(HEADS)
    ]

    query_rot = jnp.concatenate(query_heads, 1)
    attn_low, log_sum = attend(
        table, cont_prompt, cont_length, query_rot, own_pairs, chunks
    )
    attn_sum = dot_nt(attn_low, out_full)
    mixed = input_f + rms_scale(attn_sum, attn_post_gain)
    normed_mid = rms_scale(mixed, ffw_gain).astype(bf)

    mid_near, mid_far = spread_near(normed_mid)
    gate_0, up_0, act_0, *downs = feed_call(
        feed_kernel, "feed", normed_mid, mid_near, (), weights, 3
    )
    mid_last = swap_core(after(mid_far, downs[0]))
    gate_1, up_1, act_1, *more = feed_call(
        feed_kernel, "feed", mid_far, mid_last, (), weights, 3
    )
    downs += more
    ffw_sum = collect_tensor(*downs)
    result = mixed + rms_scale(ffw_sum, ffw_post_gain)

    row_length = jnp.where(
        jnp.arange(local_rows) < PSLICE,
        cont_length[core * UNITS],
        cont_length[core * UNITS + 1],
    )
    live_rows = jnp.where(is_cont & (unit_ids >= row_length), 0.0, 1.0).astype(f32)
    diff = result - teacher.astype(f32)
    loss_part = jnp.sum(live_rows[:, None] * diff * diff)
    count_f = token_count.astype(f32)
    grad_result = loss_scale / count_f * 2.0 * live_rows[:, None] * diff

    _, ffw_pull = jax.vjp(rms_scale, ffw_sum, ffw_post_gain)
    grad_ffw_sum, grad_ffw_post_gain = ffw_pull(grad_result)
    grad_ffw_low = grad_ffw_sum.astype(bf)
    grad_near, grad_far = spread_near(grad_ffw_low)
    gate_low_0, up_low_0, *mids = feed_call(
        feed_back_kernel, "feed_back", grad_ffw_low, grad_near, (gate_0, up_0), weights, 2
    )
    grad_last = swap_core(after(grad_far, mids[0]))
    gate_low_1, up_low_1, *more = feed_call(
        feed_back_kernel, "feed_back", grad_far, grad_last, (gate_1, up_1), weights, 2
    )
    mids += more
    mids_far = collect_far(*mids[2:])
    grad_mid = collect_near(*mids[:2], mids_far)
    down_w = weight_grads(
        "down_grad",
        (after(grad_ffw_low, mids_far), grad_near, grad_far, grad_last),
        (act_0, act_1),
        parts,
    )
    gate_up_w = weight_grads(
        "gate_up_grad",
        (after(normed_mid, mids_far), mid_near, mid_far, mid_last),
        (gate_low_0, gate_low_1, up_low_0, up_low_1),
        parts,
    )
    if parts == GROUP:
        out_down = lax.psum_scatter(down_w, "fsdp", scatter_dimension=0)
        out_gate_up = lax.psum_scatter(gate_up_w, "fsdp", scatter_dimension=0)
    else:
        out_down = lax.psum_scatter(down_w[0], "fsdp", scatter_dimension=1, tiled=True)
        out_gate_up = lax.psum_scatter(gate_up_w[0], "fsdp", scatter_dimension=1, tiled=True)
    out_down = out_down[0].astype(f32).T
    out_gate, out_up = out_gate_up[0].astype(f32), out_gate_up[1].astype(f32)

    _, mid_pull = jax.vjp(rms_scale, mixed, ffw_gain)
    grad_mixed_part, grad_ffw_gain = mid_pull(grad_mid)
    grad_mixed = grad_result + grad_mixed_part
    _, post_pull = jax.vjp(rms_scale, attn_sum, attn_post_gain)
    grad_attn_sum, grad_attn_post_gain = post_pull(grad_mixed)
    grad_attn_low = grad_attn_sum.astype(bf)
    grad_out_w = dot_tn(grad_attn_low, attn_low)
    grad_attn_rows = dot_nn(grad_attn_low, out_full).astype(bf)
    grad_query_rot, kept, given, grad_own = attend_back(
        table, cont_prompt, cont_length, query_rot, grad_attn_rows, log_sum, own_pairs, chunks
    )
    given = lax.ppermute(given, "tensor", [(2, 3), (3, 2)])
    kept = kept.astype(f32) + given.astype(f32)
    pair_sums = Collect(
        lambda s: kept[0, s * PSLICE : (s + 1) * PSLICE],
        lambda s: kept[1, s * PSLICE : (s + 1) * PSLICE],
    )
    for _ in range(GROUP - 1):
        last_sums = pair_sums.step()
    summed = jnp.concatenate(last_sums, 0)
    back = lax.ppermute(summed.astype(bf), "tensor", [(2, 0), (3, 1)]).astype(f32)
    grad_pairs = jnp.where(is_cont, grad_own, summed + back)

    _, query_pull = jax.vjp(
        lambda raw, gain: tuple(
            head_prep(raw[:, h * HEAD : (h + 1) * HEAD], gain, cosine, sine_part)
            for h in range(HEADS)
        ),
        query_raw,
        query_gain,
    )
    grad_query_raw, grad_query_gain = query_pull(
        tuple(grad_query_rot[:, h * HEAD : (h + 1) * HEAD] for h in range(HEADS))
    )
    _, key_pull = jax.vjp(
        lambda raw, gain: head_prep(raw, gain, cosine, sine_part), key_raw, key_gain
    )
    grad_key_raw, grad_key_gain = key_pull(grad_pairs[:, :HEAD])
    grad_query_low = grad_query_raw.astype(bf)
    grad_kv_low = jnp.concatenate([grad_key_raw, grad_pairs[:, HEAD:]], 1).astype(bf)
    grad_query_w = dot_tn(normed_in, grad_query_low)
    grad_kv_w = dot_tn(normed_in, grad_kv_low)
    grad_normed = dot_nt(grad_query_low, query_full) + dot_nt(grad_kv_low, kv_full)
    _, input_pull = jax.vjp(rms_scale, input_f, attn_gain)
    grad_input_part, grad_attn_gain = input_pull(grad_normed)
    grad_input = grad_mixed + grad_input_part

    qo_sum = collect_tensor(
        *(
            jnp.concatenate(
                [grad_query_w[:, h * HEAD : (h + 1) * HEAD], grad_out_w[:, h * HEAD : (h + 1) * HEAD]],
                1,
            )
            for h in range(HEADS)
        )
    ).reshape(members, dim // members, 2 * HEAD)
    out_qo = collect_fsdp(after(qo_sum, summed), fsdp_pos)
    out_query, out_out = out_qo[:, :HEAD], out_qo[:, HEAD:].T
    kv_blocks = grad_kv_w.reshape(members, TENSOR, shard_kv, 2 * HEAD)
    kv_column = collect_tensor(
        *order_tensor([kv_blocks[:, t] for t in range(TENSOR)], tensor_pos)
    )
    out_kv = collect_fsdp(kv_column, fsdp_pos)

    small = jnp.concatenate(
        [
            grad_attn_gain,
            grad_attn_post_gain,
            grad_ffw_gain,
            grad_ffw_post_gain,
            grad_query_gain,
            grad_key_gain,
            loss_part[None],
        ]
    )
    length = small.shape[0]
    small = jnp.pad(small, (0, -length % 1024)).reshape(-1, 128)
    small = sum_all(small).reshape(-1)
    device = fsdp_pos * TENSOR + tensor_pos
    wide = [
        lax.dynamic_slice(small, (k * dim + device * shard_gain,), (shard_gain,)) for k in range(4)
    ]
    narrow = [
        lax.dynamic_slice(small, (4 * dim + k * HEAD + device * shard_head,), (shard_head,))
        for k in range(2)
    ]
    loss = small[length - 1] / count_f
    return (
        result.astype(bf),
        loss,
        grad_input.astype(bf),
        out_query,
        out_kv[:, :HEAD],
        out_kv[:, HEAD:],
        out_out,
        out_gate,
        out_up,
        out_down,
        *wide,
        *narrow,
    )


def solution(mesh):
    rows = P(("fsdp", "tensor"), None)
    split = P(("fsdp", "tensor"))
    inward, outward = P("fsdp", "tensor"), P("tensor", "fsdp")
    return jax.shard_map(
        local,
        mesh=mesh,
        in_specs=(
            rows,
            rows,
            inward,
            rows,
            rows,
            outward,
            inward,
            inward,
            outward,
            *(split,) * 6,
            P("fsdp"),
            P("fsdp"),
            P(),
            P(),
        ),
        out_specs=(
            rows,
            P(),
            rows,
            inward,
            rows,
            rows,
            outward,
            inward,
            inward,
            outward,
            *(split,) * 6,
        ),
        check_vma=False,
    )
```

```python
import functools
import math

import jax
import jax.numpy as jnp
import numpy as np
from jax import lax
from jax.experimental import pallas as pl
from jax.experimental.pallas import tpu as pltpu
from jax.sharding import PartitionSpec as P

HEAD = 256
HEADS = 4
PROMPT = 2048
CONT = 256
GROUP = 8
GROUPS_DEV = 4
PSLICE = 256
UNITS = 2
TENSOR = 4

RING = (0, 2, 4, 6, 7, 5, 3, 1)
PLACE = tuple(RING.index(member) for member in range(GROUP))

eps_norm = 1e-06
rope_base = 1000000.0
masked_score = -1e30
score_scale = 1.0 / math.sqrt(HEAD)
bf = jnp.bfloat16
f32 = jnp.float32


def swap_core(value):
    return lax.ppermute(value, "tensor", [(t, t ^ 1) for t in range(TENSOR)])


def swap_x(value):
    return lax.ppermute(value, "tensor", [(t, t ^ 2) for t in range(TENSOR)])


def swap_bit(value, bit):
    size = lax.axis_size("fsdp")
    return lax.ppermute(value, "fsdp", [(f, f ^ bit) for f in range(size)])


def shift_z(value, step):
    pairs = [(z * 2 + y, (z + step) % 4 * 2 + y) for z in range(4) for y in range(2)]
    return lax.ppermute(value, "fsdp", pairs)


def ring_step(value, way):
    size = lax.axis_size("fsdp")
    pairs = []
    for base in range(0, size, GROUP):
        for at in range(GROUP):
            pairs.append((base + RING[at], base + RING[(at + way) % GROUP]))
    return lax.ppermute(value, "fsdp", pairs)


def spread_tensor(own):
    far = swap_x(own)
    near = swap_core(own)
    return own, near, far, swap_core(far)


def spread_near(own):
    return swap_core(own), swap_x(own)


def collect_tensor(part_0, part_1, part_2, part_3):
    return collect_near(part_0, part_1, collect_far(part_2, part_3))


def collect_far(part_2, part_3):
    return (part_2.astype(f32) + swap_core(part_3.astype(bf)).astype(f32)).astype(bf)


def collect_near(part_0, part_1, far):
    far = swap_x(far)
    near = part_0.astype(f32) + swap_core(part_1.astype(bf)).astype(f32)
    return near + far.astype(f32)


def after(value, *earlier):
    return lax.optimization_barrier((value,) + earlier)[0]


def pick(stack, index, axis=0):
    return lax.dynamic_index_in_dim(stack, index, axis, keepdims=False)


def spread_z(own):
    if lax.axis_size("fsdp") != GROUP:
        return own
    return jnp.stack([own] + [shift_z(own, step) for step in (1, 2, 3)])


def spread_y(column):
    if lax.axis_size("fsdp") != GROUP:
        return lax.all_gather(column, "fsdp", axis=0)
    return jnp.concatenate([column, swap_bit(column, 1)])


def collect_fsdp(parts, fsdp_pos):
    if lax.axis_size("fsdp") != GROUP:
        return lax.psum_scatter(parts.astype(bf), "fsdp", scatter_dimension=0).astype(f32)
    z, y = fsdp_pos // 2, fsdp_pos % 2
    paired = parts.reshape((4, 2) + parts.shape[1:])
    give = pick(paired, 1 - y, 1).astype(bf)
    column = pick(paired, y, 1).astype(f32) + swap_bit(give, 1).astype(f32)
    total = pick(column, z)
    for step in (1, 2, 3):
        total = total + shift_z(pick(column, (z + step) % 4).astype(bf), step).astype(f32)
    return total


def order_tensor(blocks, tensor_pos):
    odd = tensor_pos % 2 == 1
    high = tensor_pos // 2 == 1
    a, b, c, d = blocks
    a, b = jnp.where(odd, b, a), jnp.where(odd, a, b)
    c, d = jnp.where(odd, d, c), jnp.where(odd, c, d)
    return (
        jnp.where(high, c, a),
        jnp.where(high, d, b),
        jnp.where(high, a, c),
        jnp.where(high, b, d),
    )


def sum_all(value):
    value = value + swap_core(value)
    value = value + swap_x(value)
    bit = 1
    while bit < lax.axis_size("fsdp"):
        value = value + swap_bit(value, bit)
        bit *= 2
    return value


class Spread:
    def __init__(self, first, second):
        self.firsts, self.seconds = [first], [second]

    def step(self, *earlier):
        first, second = self.firsts[-1], self.seconds[-1]
        if earlier:
            first, second = after(first, *earlier), after(second, *earlier)
        self.firsts.append(ring_step(first, 1))
        self.seconds.append(ring_step(second, -1))
        return self.firsts[-1], self.seconds[-1]


def rms_scale(tensor_in, gain_vec):
    return (
        tensor_in
        * lax.rsqrt(jnp.mean(tensor_in * tensor_in, axis=-1, keepdims=True) + eps_norm)
        * (1.0 + gain_vec)
    )


def rotate(tensor_in, cosine, sine_part):
    half_dim = tensor_in.shape[-1] // 2
    first_half = tensor_in[..., :half_dim]
    second_half = tensor_in[..., half_dim:]
    return jnp.concatenate(
        [
            first_half * cosine - second_half * sine_part,
            second_half * cosine + first_half * sine_part,
        ],
        axis=-1,
    )


def head_prep(raw_in, gain_vec, cosine, sine_part):
    return rotate(rms_scale(raw_in, gain_vec), cosine, sine_part)


def dot_nn(left, right):
    return jnp.dot(left, right, preferred_element_type=f32)


def dot_tn(left, right):
    return lax.dot_general(left, right, (((0,), (0,)), ((), ())), preferred_element_type=f32)


def dot_nt(left, right):
    return lax.dot_general(left, right, (((1,), (1,)), ((), ())), preferred_element_type=f32)


AT_FSDP, AT_TENSOR, AT_REACH, AT_CONT, AT_CORE, AT_RING = 0, 64, 68, 84, 85, 88
TABLE_WIDTH = 128
FAR = 1 << 20


def place_table(members):
    table = np.zeros((members * TENSOR, TABLE_WIDTH), np.int32)
    for f in range(members):
        slot = f % GROUP
        place = PLACE[slot]
        for t in range(TENSOR):
            row = table[f * TENSOR + t]
            for r in range(members):
                if members == GROUP:
                    row[AT_FSDP + r] = (f // 2 - r % 4) % 4 * 2 + (f % 2 ^ r // 4)
                else:
                    row[AT_FSDP + r] = r
            row[AT_TENSOR : AT_TENSOR + TENSOR] = [t ^ j for j in range(TENSOR)]
            for unit in range(UNITS):
                for s in range(GROUP):
                    source = RING[(place - s * (1 - 2 * unit)) % GROUP]
                    row[AT_RING + unit * GROUP + s] = source
            for s in range(GROUP):
                source = s if members == GROUP else RING[(place - s) % GROUP]
                row[AT_REACH + s] = FAR if t // 2 else (slot - source) * PSLICE
            row[AT_CONT], row[AT_CORE] = t // 2, t % 2
    return table


KEYS = PROMPT + CONT
smem = pl.BlockSpec(memory_space=pltpu.SMEM)
anywhere = pl.BlockSpec(memory_space=pl.ANY)


def place_kernel(table, *refs):
    for j in range(TENSOR):
        refs[TENSOR][0, table[AT_TENSOR + j]] = refs[j][0]


def place(table, blocks):
    members, rows, width = blocks[0].shape
    return pl.pallas_call(
        place_kernel,
        out_shape=jax.ShapeDtypeStruct((members, TENSOR, rows, width), bf),
        grid_spec=pltpu.PrefetchScalarGridSpec(
            num_scalar_prefetch=1,
            grid=(members,),
            in_specs=[pl.BlockSpec((1, rows, width), lambda r, table: (r, 0, 0))] * TENSOR,
            out_specs=pl.BlockSpec(
                (1, TENSOR, rows, width), lambda r, table: (table[AT_FSDP + r], 0, 0, 0)
            ),
        ),
        name="place_pairs",
    )(table, *blocks)


def place_heads_kernel(table, *refs):
    query_ref, out_ref = refs[TENSOR:]
    for j in range(TENSOR):
        at = slice(j * HEAD, (j + 1) * HEAD)
        query_ref[0, :, at] = refs[j][0, :, :HEAD]
        out_ref[0, :, at] = refs[j][0, :, HEAD:]


def place_heads(table, blocks):
    members, rows, width = blocks[0].shape
    shape = jax.ShapeDtypeStruct((members, rows, HEADS * HEAD), bf)
    spec = pl.BlockSpec(
        (1, rows, HEADS * HEAD), lambda r, table: (table[AT_FSDP + r], 0, 0)
    )
    return pl.pallas_call(
        place_heads_kernel,
        out_shape=(shape, shape),
        grid_spec=pltpu.PrefetchScalarGridSpec(
            num_scalar_prefetch=1,
            grid=(members,),
            in_specs=[pl.BlockSpec((1, rows, width), lambda r, table: (r, 0, 0))] * TENSOR,
            out_specs=(spec, spec),
        ),
        name="place_heads",
    )(table, *blocks)


def slot_of(table, mapped, unit):
    core = table[AT_CORE]
    target = mapped[core * UNITS + unit]
    other = jnp.where(target // UNITS == core, 0, UNITS)
    return jnp.where(table[AT_CONT] == 1, other + target % UNITS, unit)


def load_pairs(table, mapped, sources, own_ref, pairs, sems, unit, start):
    slot = slot_of(table, mapped, unit)
    for option in range(2 * UNITS):

        @pl.when(slot == option)
        def _(option=option):
            rows = pl.ds(option % UNITS * PSLICE, PSLICE)
            copy = pltpu.make_async_copy(
                sources[option // UNITS].at[:, rows],
                pairs.at[unit, pl.ds(0, GROUP)],
                sems.at[unit, 0],
            )
            copy.start() if start else copy.wait()

    copy = pltpu.make_async_copy(
        own_ref.at[pl.ds(unit * PSLICE, PSLICE)], pairs.at[unit, GROUP], sems.at[unit, 1]
    )
    copy.start() if start else copy.wait()


def pair_half(pairs, unit, half):
    return pairs[unit, :, :, half * HEAD : (half + 1) * HEAD].reshape(KEYS, HEAD)


def all_pairs(table, mapped, sources, own_ref, pairs, sems):
    unit, head = pl.program_id(0), pl.program_id(1)

    @pl.when((unit == 0) & (head == 0))
    def _():
        for number in range(UNITS):
            load_pairs(table, mapped, sources, own_ref, pairs, sems, number, True)

    for number in range(UNITS):

        @pl.when((unit == number) & (head == 0))
        def _(number=number):
            load_pairs(table, mapped, sources, own_ref, pairs, sems, number, False)


def masked(table, length, scores, unit):
    key_of = lax.broadcasted_iota(jnp.int32, (PSLICE, PSLICE), 0)
    lag = key_of - lax.broadcasted_iota(jnp.int32, (PSLICE, PSLICE), 1)
    parts = []
    for s in range(GROUP):
        reach = table[AT_REACH + s]
        part = scores[s * PSLICE : (s + 1) * PSLICE]
        parts.append(jnp.where(lag <= reach, part, masked_score))
    live = length[table[AT_CORE] * UNITS + unit]
    live = jnp.where(table[AT_CONT] == 1, live, 0)
    parts.append(jnp.where((lag <= 0) & (key_of < live), scores[PROMPT:], masked_score))
    return jnp.concatenate(parts, 0)


def attend_kernel(table, mapped, length, query_ref, own_ref, *refs):
    sources = refs[:2]
    out_ref, sum_ref, pairs, values_t, sems = refs[2:]
    unit, head = pl.program_id(0), pl.program_id(1)
    all_pairs(table, mapped, sources, own_ref, pairs, sems)

    @pl.when(head == 0)
    def _():
        values_t[...] = pair_half(pairs, unit, 1).T

    query = query_ref[...] * score_scale
    scores = masked(table, length, dot_nt(pair_half(pairs, unit, 0), query), unit)
    top = jnp.max(scores, axis=0, keepdims=True)
    shifted = jnp.exp(scores - top)
    total = jnp.sum(shifted, axis=0, keepdims=True)
    out = dot_nn(values_t[...], shifted.astype(bf)) / total
    out_ref[...] = out.T.astype(bf)
    sum_ref[0] = top + jnp.log(total)


unit_head = pl.BlockSpec((PSLICE, HEAD), lambda u, h: (u, h))
sum_spec = pl.BlockSpec((1, 1, PSLICE), lambda u, h: (u * HEADS + h, 0, 0))


def attend(table, mapped, length, query, own_pairs, sources):
    rows = UNITS * PSLICE
    return pl.pallas_call(
        attend_kernel,
        out_shape=(
            jax.ShapeDtypeStruct((rows, HEADS * HEAD), bf),
            jax.ShapeDtypeStruct((UNITS * HEADS, 1, PSLICE), f32),
        ),
        grid=(UNITS, HEADS),
        in_specs=[smem, smem, smem, unit_head] + [anywhere] * 3,
        out_specs=(unit_head, sum_spec),
        scratch_shapes=[
            pltpu.VMEM((UNITS, GROUP + 1, PSLICE, 2 * HEAD), bf),
            pltpu.VMEM((HEAD, KEYS), bf),
            pltpu.SemaphoreType.DMA((UNITS, 2)),
        ],
        compiler_params=pltpu.CompilerParams(vmem_limit_bytes=40 << 20),
        cost_estimate=pl.CostEstimate(
            flops=4 * rows * HEADS * KEYS * HEAD,
            bytes_accessed=2 * KEYS * 2 * HEAD * 2 + 4 * rows * HEADS * HEAD,
            transcendentals=rows * HEADS * KEYS,
        ),
        name="attend",
    )(table, mapped, length, query, own_pairs, *sources)


def attend_back_kernel(table, mapped, length, query_ref, grad_ref, sum_ref, own_ref, *refs):
    sources = refs[:2]
    grad_query_ref, grad_own_ref, *targets, pairs, keys_t, grads, sems = refs[-8:]
    unit, head = pl.program_id(0), pl.program_id(1)
    all_pairs(table, mapped, sources, own_ref, pairs, sems)

    @pl.when(head == 0)
    def _():
        keys_t[...] = pair_half(pairs, unit, 0).T
        grads[unit] = jnp.zeros((KEYS, 2 * HEAD), f32)

    query = query_ref[...] * score_scale
    grad = grad_ref[...]
    scores = masked(table, length, dot_nt(pair_half(pairs, unit, 0), query), unit)
    probs = jnp.exp(scores - sum_ref[0])
    grad_probs = dot_nt(pair_half(pairs, unit, 1), grad)
    row_dot = jnp.sum(probs * grad_probs, axis=0, keepdims=True)
    grad_scores = (probs * (grad_probs - row_dot)).astype(bf)
    grads[unit, :, :HEAD] += dot_nn(grad_scores, query)
    grads[unit, :, HEAD:] += dot_nn(probs.astype(bf), grad)
    grad_query_ref[...] = dot_nn(keys_t[...], grad_scores).T * score_scale

    @pl.when((unit == UNITS - 1) & (head == HEADS - 1))
    def _():
        slots = [slot_of(table, mapped, number) for number in range(UNITS)]
        for s in range(GROUP):
            at = slice(s * PSLICE, (s + 1) * PSLICE)
            for option in range(2 * UNITS):
                total = jnp.zeros((PSLICE, 2 * HEAD), f32)
                for number in range(UNITS):
                    total += jnp.where(slots[number] == option, grads[number, at], 0.0)
                rows = pl.ds(option % UNITS * PSLICE, PSLICE)
                targets[option // UNITS][s, rows] = total.astype(bf)
        for number in range(UNITS):
            grad_own_ref[number * PSLICE : (number + 1) * PSLICE] = grads[number, PROMPT:]


def attend_back(table, mapped, length, query, grad, log_sum, own_pairs, sources, earlier):
    rows = UNITS * PSLICE
    whole = pl.BlockSpec(memory_space=pltpu.VMEM)
    return pl.pallas_call(
        attend_back_kernel,
        out_shape=(
            jax.ShapeDtypeStruct((rows, HEADS * HEAD), f32),
            jax.ShapeDtypeStruct((rows, 2 * HEAD), f32),
        )
        + (jax.ShapeDtypeStruct((GROUP, UNITS * PSLICE, 2 * HEAD), bf),) * 2,
        grid=(UNITS, HEADS),
        in_specs=[smem, smem, smem, unit_head, unit_head, sum_spec]
        + [anywhere] * (3 + len(earlier)),
        out_specs=(unit_head,) + (whole,) * 3,
        scratch_shapes=[
            pltpu.VMEM((UNITS, GROUP + 1, PSLICE, 2 * HEAD), bf),
            pltpu.VMEM((HEAD, KEYS), bf),
            pltpu.VMEM((UNITS, KEYS, 2 * HEAD), f32),
            pltpu.SemaphoreType.DMA((UNITS, 2)),
        ],
        compiler_params=pltpu.CompilerParams(vmem_limit_bytes=56 << 20),
        cost_estimate=pl.CostEstimate(
            flops=10 * rows * HEADS * KEYS * HEAD,
            bytes_accessed=2 * KEYS * 2 * HEAD * 6 + 10 * rows * HEADS * HEAD,
            transcendentals=rows * HEADS * KEYS,
        ),
        name="attend_back",
    )(table, mapped, length, query, grad, log_sum, own_pairs, *sources, *earlier)


GELU_SCALE = math.sqrt(2.0 / math.pi)
GELU_CUBE = 0.044715


def gelu_parts(gate):
    bent = jnp.tanh(GELU_SCALE * (gate + GELU_CUBE * (gate * gate * gate)))
    return bent, 0.5 * (1.0 + bent)


CUT = 80


def weight_copies(table, pieces, held, sems):
    copies = ([], [], [])

    def add(kind, source, target):
        number = sum(len(kept) for kept in copies)
        copies[kind].append(pltpu.make_async_copy(source, target, sems.at[number]))

    if len(pieces) == 1:
        for kind in range(3):
            add(kind, pieces[0].at[kind], held[kind])
        return copies
    shard = held[0].shape[0] // GROUP
    for way in range(2):
        for s in range(GROUP):
            piece = pieces[way * GROUP + s]
            start = pl.multiple_of(table[AT_RING + way * GROUP + s] * shard, 16)
            low, high = ((0, CUT), (CUT, shard))[way]
            add(way, piece.at[pl.ds(0, shard)], held[way].at[pl.ds(start, shard)])
            add(
                2,
                piece.at[pl.ds(shard, high - low)],
                held[2].at[pl.ds(pl.multiple_of(start + low, 16), high - low)],
            )
    return copies


def bring(copies, kinds, start):
    @pl.when(pl.program_id(0) == 0)
    def _():
        for kind in kinds:
            for copy in copies[kind]:
                copy.start() if start else copy.wait()


def pick_rows(first_ref, second_ref, rows):
    step = pl.program_id(0)

    @pl.when(step == 0)
    def _():
        rows[...] = first_ref[...]

    @pl.when(step == 1)
    def _():
        rows[...] = second_ref[...]


def put_rows(first_ref, second_ref, total):
    step = pl.program_id(0)

    @pl.when(step == 0)
    def _():
        first_ref[...] = total

    @pl.when(step == 1)
    def _():
        second_ref[...] = total


def feed_kernel(n_pieces, table, first_ref, second_ref, *refs):
    pieces, refs = refs[:n_pieces], refs[n_pieces:]
    gate_ref, up_ref, act_ref, first_out, second_out, rows, gate_w, up_w, down_w, sems = refs
    copies = weight_copies(table, pieces, (gate_w, up_w, down_w), sems)
    bring(copies, (0, 1, 2), True)
    pick_rows(first_ref, second_ref, rows)
    bring(copies, (0,), False)
    gate = dot_nn(rows[...], gate_w[...])
    bring(copies, (1,), False)
    up = dot_nn(rows[...], up_w[...])
    act = (gate * gelu_parts(gate)[1] * up).astype(bf)
    gate_ref[...] = gate.astype(bf)
    up_ref[...] = up.astype(bf)
    act_ref[...] = act
    bring(copies, (2,), False)
    put_rows(first_out, second_out, dot_nt(act, down_w[...]).astype(bf))


def feed_back_kernel(n_pieces, table, first_ref, second_ref, gate_ref, up_ref, *refs):
    pieces, refs = refs[:n_pieces], refs[n_pieces:]
    gate_out, up_out, first_out, second_out, rows, gate_w, up_w, down_w, sems = refs
    copies = weight_copies(table, pieces, (gate_w, up_w, down_w), sems)
    bring(copies, (2, 0, 1), True)
    pick_rows(first_ref, second_ref, rows)
    bring(copies, (2, 0, 1), False)
    total = jnp.zeros(rows.shape, f32)
    hidden = gate_ref.shape[1]
    for low in range(0, hidden, 512):
        at = slice(low, min(low + 512, hidden))
        grad_act = dot_nn(rows[...], down_w[:, at])
        gate, up = gate_ref[:, at].astype(f32), up_ref[:, at].astype(f32)
        bent, share = gelu_parts(gate)
        slope = share + 0.5 * gate * (1.0 - bent * bent) * (
            GELU_SCALE * (1.0 + 3.0 * GELU_CUBE * (gate * gate))
        )
        grad_gate = (grad_act * up * slope).astype(bf)
        grad_up = (grad_act * (gate * share)).astype(bf)
        gate_out[:, at] = grad_gate
        up_out[:, at] = grad_up
        total += dot_nt(grad_gate, gate_w[:, at]) + dot_nt(grad_up, up_w[:, at])
    put_rows(first_out, second_out, total.astype(bf))


def feed_call(kernel, name, table, first, second, hiddens, pieces, n_out):
    rows, dim = first.shape
    hidden = pieces[0].shape[-1]
    fixed = pl.BlockSpec((rows, dim), lambda i: (0, 0))
    wide = pl.BlockSpec((rows, hidden), lambda i: (i, 0))
    row_shape = jax.ShapeDtypeStruct((rows, dim), bf)
    wide_shape = jax.ShapeDtypeStruct((2 * rows, hidden), bf)
    return pl.pallas_call(
        functools.partial(kernel, len(pieces)),
        out_shape=(wide_shape,) * n_out + (row_shape, row_shape),
        grid=(2,),
        in_specs=[smem, fixed, fixed] + [wide] * len(hiddens) + [anywhere] * len(pieces),
        out_specs=(wide,) * n_out + (fixed, fixed),
        scratch_shapes=[pltpu.VMEM((rows, dim), bf)]
        + [pltpu.VMEM((dim, hidden), bf)] * 3
        + [pltpu.SemaphoreType.DMA((max(3, 2 * len(pieces)),))],
        compiler_params=pltpu.CompilerParams(vmem_limit_bytes=60 << 20),
        cost_estimate=pl.CostEstimate(
            flops=12 * rows * dim * hidden,
            bytes_accessed=6 * dim * hidden + 2 * rows * hidden * 2 * (n_out + len(hiddens)),
            transcendentals=2 * rows * hidden,
        ),
        name=name,
    )(table, first, second, *hiddens, *pieces)


def pass_on_kernel(moved, last, table, *refs):
    if moved:
        first_ref, second_ref, refs = refs[0], refs[1], refs[2:]
    gate_ref, up_ref, down_first, down_second = refs[:4]
    outs = refs[-3:] if last else refs[-2:]
    shard = gate_ref.shape[2]
    gate, up = gate_ref[0, 0].astype(f32), up_ref[0, 0].astype(f32)
    low, high = down_first[0, 0, :CUT].astype(f32), down_second[0, 0, CUT:].astype(f32)
    if moved:
        gate += first_ref[:shard].astype(f32)
        low += first_ref[shard:].astype(f32)
        up += second_ref[:shard].astype(f32)
        high += second_ref[shard:].astype(f32)
    if last:
        outs[0][...] = gate
        outs[1][...] = up
        outs[2][:CUT] = low
        outs[2][CUT:] = high
    else:
        outs[0][:shard] = gate.astype(bf)
        outs[0][shard:] = low.astype(bf)
        outs[1][:shard] = up.astype(bf)
        outs[1][shard:] = high.astype(bf)


def pass_on(table, moved, gate_up_w, down_w, s, earlier=()):
    _, _, shard, hidden = gate_up_w.shape
    width = 896
    last = s == 0

    def block(rows):
        return pl.BlockSpec((rows, width), lambda i, table: (0, i))

    def term(way, kind):
        return pl.BlockSpec(
            (1, 1, shard, width),
            lambda i, table: (table[AT_RING + way * GROUP + s], kind, 0, i),
        )

    heights = (shard,) * 3 if last else (shard + CUT, 2 * shard - CUT)
    kind = f32 if last else bf
    return pl.pallas_call(
        functools.partial(pass_on_kernel, len(moved), last),
        out_shape=tuple(jax.ShapeDtypeStruct((rows, hidden), kind) for rows in heights),
        grid_spec=pltpu.PrefetchScalarGridSpec(
            num_scalar_prefetch=1,
            grid=(pl.cdiv(hidden, width),),
            in_specs=[block(part.shape[0]) for part in moved]
            + [term(0, 0), term(1, 1), term(0, 0), term(1, 0)]
            + [anywhere] * len(earlier),
            out_specs=tuple(block(rows) for rows in heights),
        ),
        compiler_params=pltpu.CompilerParams(vmem_limit_bytes=60 << 20),
        name="pass_on",
    )(table, *moved, gate_up_w, gate_up_w, down_w, down_w, *earlier)


def weight_grad_kernel(number, *refs):
    blocks, halves = refs[:TENSOR], refs[TENSOR : TENSOR + 2 * number]
    out_ref, turned = refs[TENSOR + 2 * number :]
    rows = blocks[0].shape[0]

    @pl.when(pl.program_id(0) == 0)
    def _():
        for j in range(TENSOR):
            turned[:, j * rows : (j + 1) * rows] = blocks[j][...].T

    for k in range(number):
        total = dot_nn(turned[:, : 2 * rows], halves[2 * k][...])
        total += dot_nn(turned[:, 2 * rows :], halves[2 * k + 1][...])
        out_ref[:, k] = total.astype(bf).reshape(out_ref.shape[0], out_ref.shape[2], -1)


def weight_grads(name, blocks, halves, parts):
    rows, dim = blocks[0].shape
    hidden = halves[0].shape[1]
    number = len(halves) // 2
    width = 256
    return pl.pallas_call(
        functools.partial(weight_grad_kernel, number),
        out_shape=jax.ShapeDtypeStruct((parts, number, dim // parts, hidden), bf),
        grid=(pl.cdiv(hidden, width),),
        in_specs=[pl.BlockSpec((rows, dim), lambda i: (0, 0), pipeline_mode=pl.Buffered(1))]
        * TENSOR
        + [pl.BlockSpec((2 * rows, width), lambda i: (0, i))] * (2 * number),
        out_specs=pl.BlockSpec((parts, number, dim // parts, width), lambda i: (0, 0, 0, i)),
        scratch_shapes=[pltpu.VMEM((dim, TENSOR * rows), bf)],
        compiler_params=pltpu.CompilerParams(vmem_limit_bytes=48 << 20),
        cost_estimate=pl.CostEstimate(
            flops=3 * number * rows * dim * hidden,
            bytes_accessed=4 * rows * dim + number * (4 * rows + 2 * dim) * hidden,
            transcendentals=0,
        ),
        name=name,
    )(*blocks, *halves)


def local(
    layer_in,
    teacher,
    query_proj,
    key_proj,
    value_proj,
    out_proj,
    gate_proj,
    up_proj,
    down_proj,
    attn_norm,
    attn_post,
    ffw_norm,
    ffw_post,
    query_norm,
    key_norm,
    cont_prompt,
    cont_length,
    token_count,
    loss_scale,
):
    members = lax.axis_size("fsdp")
    fsdp_pos = lax.axis_index("fsdp")
    tensor_pos = lax.axis_index("tensor")
    core, side = tensor_pos % 2, tensor_pos // 2
    is_cont = side == 1
    group_slot = fsdp_pos % GROUP
    table = lax.dynamic_index_in_dim(
        jnp.asarray(place_table(members)), fsdp_pos * TENSOR + tensor_pos, 0, keepdims=False
    )
    dim = layer_in.shape[1]

    ringed = members == GROUP
    down_own = down_proj.T
    if ringed:
        parts = GROUP
        weights = Spread(
            jnp.concatenate([gate_proj, down_own[:CUT]], 0),
            jnp.concatenate([up_proj, down_own[CUT:]], 0),
        )
        for _ in range(GROUP - 1):
            weights.step()
        came = list(zip(weights.firsts, weights.seconds, strict=True))
    else:
        came = [()] * GROUP
        parts = 1
        pieces = (gate_proj, up_proj, down_own)
        pieces = [jnp.stack([lax.all_gather(w, "fsdp", axis=0, tiled=True) for w in pieces])]

    shard_kv = key_proj.shape[0]
    shard_gain, shard_head = attn_norm.shape[0], query_norm.shape[0]
    gains_own = jnp.stack(
        [
            jnp.pad(gain, (0, 2 * HEAD - gain.shape[0]))
            for gain in (attn_norm, attn_post, ffw_norm, ffw_post, query_norm, key_norm)
        ]
    )
    packed = jnp.concatenate([jnp.concatenate([key_proj, value_proj], 1), gains_own], 0)
    packed = jnp.pad(packed, ((0, -packed.shape[0] % 16), (0, 0)))
    packed_f = spread_y(spread_z(packed))
    packed_all = place(table, spread_tensor(packed_f))
    qo_own = jnp.concatenate([query_proj, out_proj.T], 1)
    qo_column = spread_z(after(qo_own, packed_f))
    kv_full = packed_all[:, :, :shard_kv].reshape(dim, 2 * HEAD)
    gains_all = packed_all[:, :, shard_kv : shard_kv + 6].astype(f32)

    def gain_of(number):
        return gains_all[:, :, number, :shard_gain].reshape(dim)

    def head_gain_of(number):
        return gains_all[:, :, 4 + number, :shard_head].reshape(HEAD)

    attn_gain, attn_post_gain, ffw_gain, ffw_post_gain = (gain_of(k) for k in range(4))
    query_gain, key_gain = head_gain_of(0), head_gain_of(1)

    local_rows = layer_in.shape[0]
    unit_ids = jnp.arange(local_rows, dtype=jnp.int32) % PSLICE
    positions = unit_ids + jnp.where(is_cont, PROMPT, group_slot * PSLICE)
    inverse_freq = jnp.exp(
        -math.log(rope_base) * 2.0 * jnp.arange(HEAD // 2, dtype=f32) / HEAD
    )
    angles = positions.astype(f32)[:, None] * inverse_freq[None, :]
    cosine, sine_part = jnp.cos(angles), jnp.sin(angles)
    input_f = layer_in.astype(f32)
    normed_in = rms_scale(input_f, attn_gain).astype(bf)

    kv_raw = dot_nn(normed_in, kv_full)
    key_raw = kv_raw[:, :HEAD]
    key_rot = head_prep(key_raw, key_gain, cosine, sine_part).astype(bf)
    own_pairs = jnp.concatenate([key_rot, kv_raw[:, HEAD:].astype(bf)], 1)
    own_pairs = after(own_pairs, qo_column, *came[1])
    qo_column = spread_y(after(qo_column, packed_all))
    across = lax.ppermute(own_pairs, "tensor", [(0, 2), (1, 3)])
    prompt_pairs = after(jnp.where(is_cont, across, own_pairs), qo_column, *came[2])
    if ringed:
        held_pairs = lax.all_gather(prompt_pairs, "fsdp", axis=0)
    else:
        held_pairs = [prompt_pairs]
        while len(held_pairs) < GROUP:
            held_pairs.append(ring_step(held_pairs[-1], 1))
        held_pairs = jnp.stack(held_pairs)
    qo_column = after(qo_column, across)
    qo_near, qo_far = spread_near(qo_column)
    query_full, out_full = (
        part.reshape(dim, HEADS * HEAD)
        for part in place_heads(
            table, (after(qo_column, *came[4]), qo_near, qo_far, swap_core(after(qo_far, *came[3])))
        )
    )
    query_raw = dot_nn(normed_in, query_full)
    query_heads = [
        head_prep(query_raw[:, h * HEAD : (h + 1) * HEAD], query_gain, cosine, sine_part).astype(bf)
        for h in range(HEADS)
    ]

    query_rot = jnp.concatenate(query_heads, 1)
    held_pairs = after(held_pairs, query_rot, *came[6])
    sources = held_pairs, lax.ppermute(held_pairs, "tensor", [(2, 3), (3, 2)])
    attn_low, log_sum = attend(
        table, cont_prompt, cont_length, query_rot, own_pairs, sources
    )
    attn_sum = dot_nt(attn_low, out_full)
    if ringed:
        pieces = weights.firsts + weights.seconds
    mixed = input_f + rms_scale(attn_sum, attn_post_gain)
    normed_mid = rms_scale(mixed, ffw_gain).astype(bf)

    mid_near, mid_far = spread_near(normed_mid)
    gate_0, up_0, act_0, *downs = feed_call(
        feed_kernel, "feed", table, normed_mid, mid_near, (), pieces, 3
    )
    mid_last = swap_core(after(mid_far, downs[0]))
    gate_1, up_1, act_1, *more = feed_call(
        feed_kernel, "feed", table, mid_far, mid_last, (), pieces, 3
    )
    downs += more
    ffw_sum = collect_tensor(*downs)
    result = mixed + rms_scale(ffw_sum, ffw_post_gain)

    row_length = jnp.where(
        jnp.arange(local_rows) < PSLICE,
        cont_length[core * UNITS],
        cont_length[core * UNITS + 1],
    )
    live_rows = jnp.where(is_cont & (unit_ids >= row_length), 0.0, 1.0).astype(f32)
    diff = result - teacher.astype(f32)
    loss_part = jnp.sum(live_rows[:, None] * diff * diff)
    count_f = token_count.astype(f32)
    grad_result = loss_scale / count_f * 2.0 * live_rows[:, None] * diff

    _, ffw_pull = jax.vjp(rms_scale, ffw_sum, ffw_post_gain)
    grad_ffw_sum, grad_ffw_post_gain = ffw_pull(grad_result)
    grad_ffw_low = grad_ffw_sum.astype(bf)
    grad_near, grad_far = spread_near(grad_ffw_low)
    gate_low_0, up_low_0, *mids = feed_call(
        feed_back_kernel, "feed_back", table, grad_ffw_low, grad_near, (gate_0, up_0), pieces, 2
    )
    grad_last = swap_core(after(grad_far, mids[0]))
    gate_low_1, up_low_1, *more = feed_call(
        feed_back_kernel, "feed_back", table, grad_far, grad_last, (gate_1, up_1), pieces, 2
    )
    mids += more
    mids_far = collect_far(*mids[2:])
    grad_mid = collect_near(*mids[:2], mids_far)
    down_w = weight_grads(
        "down_grad",
        (after(grad_ffw_low, mids_far), grad_near, grad_far, grad_last),
        (act_0, act_1),
        parts,
    )
    gate_up_w = weight_grads(
        "gate_up_grad",
        (after(normed_mid, mids_far), mid_near, mid_far, mid_last),
        (gate_low_0, gate_low_1, up_low_0, up_low_1),
        parts,
    )
    if ringed:
        held_sums = pass_on(table, (), gate_up_w, down_w, GROUP - 1)

        def move_sums():
            return ring_step(held_sums[0], -1), ring_step(held_sums[1], 1)

        def add_sums(moved, s, *earlier):
            return pass_on(table, moved, gate_up_w, down_w, s, earlier)

    else:
        out_down = lax.psum_scatter(down_w[0, 0], "fsdp", scatter_dimension=0, tiled=True)
        out_down = out_down.astype(f32)
        out_gate, out_up = lax.psum_scatter(
            gate_up_w[0], "fsdp", scatter_dimension=1, tiled=True
        ).astype(f32)

    _, mid_pull = jax.vjp(rms_scale, mixed, ffw_gain)
    grad_mixed_part, grad_ffw_gain = mid_pull(grad_mid)
    grad_mixed = grad_result + grad_mixed_part
    _, post_pull = jax.vjp(rms_scale, attn_sum, attn_post_gain)
    grad_attn_sum, grad_attn_post_gain = post_pull(grad_mixed)
    grad_attn_low = grad_attn_sum.astype(bf)
    grad_out_w = dot_tn(grad_attn_low, attn_low)
    grad_attn_rows = dot_nn(grad_attn_low, out_full).astype(bf)
    if ringed:
        held_sums = add_sums(move_sums(), 6, grad_attn_rows)
    grad_query_rot, grad_own, kept, given = attend_back(
        table, cont_prompt, cont_length, query_rot, grad_attn_rows, log_sum, own_pairs, sources, held_sums if ringed else ()
    )
    if ringed:
        moved = move_sums()
        given = after(given, *moved)
        held_sums = add_sums(moved, 5)
    given = lax.ppermute(given, "tensor", [(2, 3), (3, 2)])
    kept = (kept.astype(f32) + given.astype(f32)).astype(bf)
    if ringed:
        for s in (4, 3, 2):
            held_sums = add_sums(move_sums(), s)
        summed = lax.psum_scatter(kept, "fsdp", scatter_dimension=0)
        summed = after(summed, *held_sums).astype(f32)
    else:
        summed = kept[GROUP - 1]
        for s in reversed(range(GROUP - 1)):
            summed = (ring_step(summed, -1).astype(f32) + kept[s].astype(f32)).astype(bf)
        summed = summed.astype(f32)
    back = lax.ppermute(summed.astype(bf), "tensor", [(2, 0), (3, 1)]).astype(f32)
    grad_pairs = jnp.where(is_cont, grad_own, summed + back)

    _, query_pull = jax.vjp(
        lambda raw, gain: tuple(
            head_prep(raw[:, h * HEAD : (h + 1) * HEAD], gain, cosine, sine_part)
            for h in range(HEADS)
        ),
        query_raw,
        query_gain,
    )
    grad_query_raw, grad_query_gain = query_pull(
        tuple(grad_query_rot[:, h * HEAD : (h + 1) * HEAD] for h in range(HEADS))
    )
    _, key_pull = jax.vjp(
        lambda raw, gain: head_prep(raw, gain, cosine, sine_part), key_raw, key_gain
    )
    grad_key_raw, grad_key_gain = key_pull(grad_pairs[:, :HEAD])
    grad_query_low = grad_query_raw.astype(bf)
    grad_kv_low = jnp.concatenate([grad_key_raw, grad_pairs[:, HEAD:]], 1).astype(bf)
    grad_query_w = dot_tn(normed_in, grad_query_low)
    grad_kv_w = dot_tn(normed_in, grad_kv_low)
    grad_normed = dot_nt(grad_query_low, query_full) + dot_nt(grad_kv_low, kv_full)
    _, input_pull = jax.vjp(rms_scale, input_f, attn_gain)
    grad_input_part, grad_attn_gain = input_pull(grad_normed)
    grad_input = grad_mixed + grad_input_part

    qo_sum = collect_tensor(
        *(
            jnp.concatenate(
                [grad_query_w[:, h * HEAD : (h + 1) * HEAD], grad_out_w[:, h * HEAD : (h + 1) * HEAD]],
                1,
            )
            for h in range(HEADS)
        )
    ).reshape(members, dim // members, 2 * HEAD)
    out_qo = collect_fsdp(qo_sum, fsdp_pos)
    out_query, out_out = out_qo[:, :HEAD], out_qo[:, HEAD:].T
    kv_blocks = grad_kv_w.reshape(members, TENSOR, shard_kv, 2 * HEAD)
    kv_column = collect_tensor(
        *order_tensor([kv_blocks[:, t] for t in range(TENSOR)], tensor_pos)
    )
    out_kv = collect_fsdp(kv_column, fsdp_pos)

    if ringed:
        held_sums = add_sums(move_sums(), 1, grad_kv_w)
        held_sums = add_sums(move_sums(), 0)
        out_gate, out_up, out_down = held_sums
    out_down = out_down.T

    small = jnp.concatenate(
        [
            grad_attn_gain,
            grad_attn_post_gain,
            grad_ffw_gain,
            grad_ffw_post_gain,
            grad_query_gain,
            grad_key_gain,
            loss_part[None],
        ]
    )
    length = small.shape[0]
    small = jnp.pad(small, (0, -length % 1024)).reshape(-1, 128)
    small = sum_all(small).reshape(-1)
    device = fsdp_pos * TENSOR + tensor_pos
    wide = [
        lax.dynamic_slice(small, (k * dim + device * shard_gain,), (shard_gain,)) for k in range(4)
    ]
    narrow = [
        lax.dynamic_slice(small, (4 * dim + k * HEAD + device * shard_head,), (shard_head,))
        for k in range(2)
    ]
    loss = small[length - 1] / count_f
    return (
        result.astype(bf),
        loss,
        grad_input.astype(bf),
        out_query,
        out_kv[:, :HEAD],
        out_kv[:, HEAD:],
        out_out,
        out_gate,
        out_up,
        out_down,
        *wide,
        *narrow,
    )


def solution(mesh):
    rows = P(("fsdp", "tensor"), None)
    split = P(("fsdp", "tensor"))
    inward, outward = P("fsdp", "tensor"), P("tensor", "fsdp")
    return jax.shard_map(
        local,
        mesh=mesh,
        in_specs=(
            rows,
            rows,
            inward,
            rows,
            rows,
            outward,
            inward,
            inward,
            outward,
            *(split,) * 6,
            P("fsdp"),
            P("fsdp"),
            P(),
            P(),
        ),
        out_specs=(
            rows,
            P(),
            rows,
            inward,
            rows,
            rows,
            outward,
            inward,
            inward,
            outward,
            *(split,) * 6,
        ),
        check_vma=False,
    )
```

```python
import functools
import math

import jax
import jax.numpy as jnp
import numpy as np
from jax import lax
from jax.experimental import pallas as pl
from jax.experimental.pallas import tpu as pltpu
from jax.sharding import PartitionSpec as P

HEAD = 256
HEADS = 4
PROMPT = 2048
CONT = 256
GROUP = 8
GROUPS_DEV = 4
PSLICE = 256
UNITS = 2
TENSOR = 4

RING = (0, 2, 4, 6, 7, 5, 3, 1)
PLACE = tuple(RING.index(member) for member in range(GROUP))

eps_norm = 1e-06
rope_base = 1000000.0
masked_score = -1e30
score_scale = 1.0 / math.sqrt(HEAD)
bf = jnp.bfloat16
f32 = jnp.float32


def swap_core(value):
    return lax.ppermute(value, "tensor", [(t, t ^ 1) for t in range(TENSOR)])


def swap_x(value):
    return lax.ppermute(value, "tensor", [(t, t ^ 2) for t in range(TENSOR)])


def swap_bit(value, bit):
    size = lax.axis_size("fsdp")
    return lax.ppermute(value, "fsdp", [(f, f ^ bit) for f in range(size)])


def shift_z(value, step):
    pairs = [(z * 2 + y, (z + step) % 4 * 2 + y) for z in range(4) for y in range(2)]
    return lax.ppermute(value, "fsdp", pairs)


def ring_step(value, way):
    size = lax.axis_size("fsdp")
    pairs = []
    for base in range(0, size, GROUP):
        for at in range(GROUP):
            pairs.append((base + RING[at], base + RING[(at + way) % GROUP]))
    return lax.ppermute(value, "fsdp", pairs)


def spread_tensor(own):
    far = swap_x(own)
    near = swap_core(own)
    return own, near, far, swap_core(far)


def spread_near(own):
    return swap_core(own), swap_x(own)


def collect_tensor(part_0, part_1, part_2, part_3):
    return collect_near(part_0, part_1, collect_far(part_2, part_3))


def collect_far(part_2, part_3):
    return (part_2.astype(f32) + swap_core(part_3.astype(bf)).astype(f32)).astype(bf)


def collect_near(part_0, part_1, far):
    far = swap_x(far)
    near = part_0.astype(f32) + swap_core(part_1.astype(bf)).astype(f32)
    return near + far.astype(f32)


def after(value, *earlier):
    return lax.optimization_barrier((value,) + earlier)[0]


def pick(stack, index, axis=0):
    return lax.dynamic_index_in_dim(stack, index, axis, keepdims=False)


def spread_z(own):
    if lax.axis_size("fsdp") != GROUP:
        return own
    return jnp.stack([own] + [shift_z(own, step) for step in (1, 2, 3)])


def spread_y(column):
    if lax.axis_size("fsdp") != GROUP:
        return lax.all_gather(column, "fsdp", axis=0)
    return jnp.concatenate([column, swap_bit(column, 1)])


def collect_fsdp(parts, fsdp_pos):
    if lax.axis_size("fsdp") != GROUP:
        return lax.psum_scatter(parts.astype(bf), "fsdp", scatter_dimension=0).astype(f32)
    z, y = fsdp_pos // 2, fsdp_pos % 2
    paired = parts.reshape((4, 2) + parts.shape[1:])
    give = pick(paired, 1 - y, 1).astype(bf)
    column = pick(paired, y, 1).astype(f32) + swap_bit(give, 1).astype(f32)
    total = pick(column, z)
    for step in (1, 2, 3):
        total = total + shift_z(pick(column, (z + step) % 4).astype(bf), step).astype(f32)
    return total


def order_tensor(blocks, tensor_pos):
    odd = tensor_pos % 2 == 1
    high = tensor_pos // 2 == 1
    a, b, c, d = blocks
    a, b = jnp.where(odd, b, a), jnp.where(odd, a, b)
    c, d = jnp.where(odd, d, c), jnp.where(odd, c, d)
    return (
        jnp.where(high, c, a),
        jnp.where(high, d, b),
        jnp.where(high, a, c),
        jnp.where(high, b, d),
    )


def sum_all(value):
    value = value + swap_core(value)
    value = value + swap_x(value)
    bit = 1
    while bit < lax.axis_size("fsdp"):
        value = value + swap_bit(value, bit)
        bit *= 2
    return value


class Spread:
    def __init__(self, first, second):
        self.firsts, self.seconds = [first], [second]

    def step(self, *earlier):
        first, second = self.firsts[-1], self.seconds[-1]
        if earlier:
            first, second = after(first, *earlier), after(second, *earlier)
        self.firsts.append(ring_step(first, 1))
        self.seconds.append(ring_step(second, -1))
        return self.firsts[-1], self.seconds[-1]


def rms_scale(tensor_in, gain_vec):
    return (
        tensor_in
        * lax.rsqrt(jnp.mean(tensor_in * tensor_in, axis=-1, keepdims=True) + eps_norm)
        * (1.0 + gain_vec)
    )


def rotate(tensor_in, cosine, sine_part):
    half_dim = tensor_in.shape[-1] // 2
    first_half = tensor_in[..., :half_dim]
    second_half = tensor_in[..., half_dim:]
    return jnp.concatenate(
        [
            first_half * cosine - second_half * sine_part,
            second_half * cosine + first_half * sine_part,
        ],
        axis=-1,
    )


def head_prep(raw_in, gain_vec, cosine, sine_part):
    return rotate(rms_scale(raw_in, gain_vec), cosine, sine_part)


def dot_nn(left, right):
    return jnp.dot(left, right, preferred_element_type=f32)


def dot_tn(left, right):
    return lax.dot_general(left, right, (((0,), (0,)), ((), ())), preferred_element_type=f32)


def dot_nt(left, right):
    return lax.dot_general(left, right, (((1,), (1,)), ((), ())), preferred_element_type=f32)


AT_FSDP, AT_TENSOR, AT_REACH, AT_CONT, AT_CORE, AT_RING = 0, 64, 68, 84, 85, 88
TABLE_WIDTH = 128
FAR = 1 << 20


def place_table(members):
    table = np.zeros((members * TENSOR, TABLE_WIDTH), np.int32)
    for f in range(members):
        slot = f % GROUP
        place = PLACE[slot]
        for t in range(TENSOR):
            row = table[f * TENSOR + t]
            for r in range(members):
                if members == GROUP:
                    row[AT_FSDP + r] = (f // 2 - r % 4) % 4 * 2 + (f % 2 ^ r // 4)
                else:
                    row[AT_FSDP + r] = r
            row[AT_TENSOR : AT_TENSOR + TENSOR] = [t ^ j for j in range(TENSOR)]
            for unit in range(UNITS):
                for s in range(GROUP):
                    source = RING[(place - s * (1 - 2 * unit)) % GROUP]
                    row[AT_RING + unit * GROUP + s] = source
            for s in range(GROUP):
                source = s if members == GROUP else RING[(place - s) % GROUP]
                row[AT_REACH + s] = FAR if t // 2 else (slot - source) * PSLICE
            row[AT_CONT], row[AT_CORE] = t // 2, t % 2
    return table


KEYS = PROMPT + CONT
smem = pl.BlockSpec(memory_space=pltpu.SMEM)
anywhere = pl.BlockSpec(memory_space=pl.ANY)


def place_kernel(table, *refs):
    for r in range(refs[0].shape[0]):
        for j in range(TENSOR):
            refs[TENSOR][table[AT_FSDP + r], table[AT_TENSOR + j]] = refs[j][r]


def place(table, blocks):
    members, rows, width = blocks[0].shape
    return pl.pallas_call(
        place_kernel,
        out_shape=jax.ShapeDtypeStruct((members, TENSOR, rows, width), bf),
        in_specs=[smem] + [pl.BlockSpec(memory_space=pltpu.VMEM)] * TENSOR,
        out_specs=pl.BlockSpec(memory_space=pltpu.VMEM),
        name="place_pairs",
    )(table, *blocks)


def place_heads_kernel(table, *refs):
    query_ref, out_ref = refs[TENSOR:]
    for j in range(TENSOR):
        at = slice(j * HEAD, (j + 1) * HEAD)
        query_ref[0, :, at] = refs[j][0, :, :HEAD]
        out_ref[0, :, at] = refs[j][0, :, HEAD:]


def place_heads(table, blocks):
    members, rows, width = blocks[0].shape
    shape = jax.ShapeDtypeStruct((members, rows, HEADS * HEAD), bf)
    spec = pl.BlockSpec(
        (1, rows, HEADS * HEAD), lambda r, table: (table[AT_FSDP + r], 0, 0)
    )
    return pl.pallas_call(
        place_heads_kernel,
        out_shape=(shape, shape),
        grid_spec=pltpu.PrefetchScalarGridSpec(
            num_scalar_prefetch=1,
            grid=(members,),
            in_specs=[pl.BlockSpec((1, rows, width), lambda r, table: (r, 0, 0))] * TENSOR,
            out_specs=(spec, spec),
        ),
        name="place_heads",
    )(table, *blocks)


def slot_of(table, mapped, unit):
    core = table[AT_CORE]
    target = mapped[core * UNITS + unit]
    other = jnp.where(target // UNITS == core, 0, UNITS)
    return jnp.where(table[AT_CONT] == 1, other + target % UNITS, unit)


def load_pairs(table, mapped, sources, own_ref, pairs, sems, unit, start):
    slot = slot_of(table, mapped, unit)
    for option in range(2 * UNITS):

        @pl.when(slot == option)
        def _(option=option):
            rows = pl.ds(option % UNITS * PSLICE, PSLICE)
            copy = pltpu.make_async_copy(
                sources[option // UNITS].at[:, rows],
                pairs.at[unit, pl.ds(0, GROUP)],
                sems.at[unit, 0],
            )
            copy.start() if start else copy.wait()

    copy = pltpu.make_async_copy(
        own_ref.at[pl.ds(unit * PSLICE, PSLICE)], pairs.at[unit, GROUP], sems.at[unit, 1]
    )
    copy.start() if start else copy.wait()


def pair_half(pairs, unit, half):
    return pairs[unit, :, :, half * HEAD : (half + 1) * HEAD].reshape(KEYS, HEAD)


def all_pairs(table, mapped, sources, own_ref, pairs, sems):
    unit, head = pl.program_id(0), pl.program_id(1)

    @pl.when((unit == 0) & (head == 0))
    def _():
        for number in range(UNITS):
            load_pairs(table, mapped, sources, own_ref, pairs, sems, number, True)

    for number in range(UNITS):

        @pl.when((unit == number) & (head == 0))
        def _(number=number):
            load_pairs(table, mapped, sources, own_ref, pairs, sems, number, False)


def masked(table, length, scores, unit):
    key_of = lax.broadcasted_iota(jnp.int32, (PSLICE, PSLICE), 0)
    lag = key_of - lax.broadcasted_iota(jnp.int32, (PSLICE, PSLICE), 1)
    parts = []
    for s in range(GROUP):
        reach = table[AT_REACH + s]
        part = scores[s * PSLICE : (s + 1) * PSLICE]
        parts.append(jnp.where(lag <= reach, part, masked_score))
    live = length[table[AT_CORE] * UNITS + unit]
    live = jnp.where(table[AT_CONT] == 1, live, 0)
    parts.append(jnp.where((lag <= 0) & (key_of < live), scores[PROMPT:], masked_score))
    return jnp.concatenate(parts, 0)


def attend_kernel(table, mapped, length, query_ref, own_ref, *refs):
    sources = refs[:2]
    out_ref, sum_ref, pairs, values_t, sems = refs[2:]
    unit, head = pl.program_id(0), pl.program_id(1)
    all_pairs(table, mapped, sources, own_ref, pairs, sems)

    @pl.when(head == 0)
    def _():
        values_t[...] = pair_half(pairs, unit, 1).T

    query = query_ref[...] * score_scale
    scores = masked(table, length, dot_nt(pair_half(pairs, unit, 0), query), unit)
    top = jnp.max(scores, axis=0, keepdims=True)
    shifted = jnp.exp(scores - top)
    total = jnp.sum(shifted, axis=0, keepdims=True)
    out = dot_nn(values_t[...], shifted.astype(bf)) / total
    out_ref[...] = out.T.astype(bf)
    sum_ref[0] = top + jnp.log(total)


unit_head = pl.BlockSpec((PSLICE, HEAD), lambda u, h: (u, h))
sum_spec = pl.BlockSpec((1, 1, PSLICE), lambda u, h: (u * HEADS + h, 0, 0))


def attend(table, mapped, length, query, own_pairs, sources):
    rows = UNITS * PSLICE
    return pl.pallas_call(
        attend_kernel,
        out_shape=(
            jax.ShapeDtypeStruct((rows, HEADS * HEAD), bf),
            jax.ShapeDtypeStruct((UNITS * HEADS, 1, PSLICE), f32),
        ),
        grid=(UNITS, HEADS),
        in_specs=[smem, smem, smem, unit_head] + [anywhere] * 3,
        out_specs=(unit_head, sum_spec),
        scratch_shapes=[
            pltpu.VMEM((UNITS, GROUP + 1, PSLICE, 2 * HEAD), bf),
            pltpu.VMEM((HEAD, KEYS), bf),
            pltpu.SemaphoreType.DMA((UNITS, 2)),
        ],
        compiler_params=pltpu.CompilerParams(vmem_limit_bytes=40 << 20),
        cost_estimate=pl.CostEstimate(
            flops=4 * rows * HEADS * KEYS * HEAD,
            bytes_accessed=2 * KEYS * 2 * HEAD * 2 + 4 * rows * HEADS * HEAD,
            transcendentals=rows * HEADS * KEYS,
        ),
        name="attend",
    )(table, mapped, length, query, own_pairs, *sources)


def attend_back_kernel(table, mapped, length, query_ref, grad_ref, sum_ref, own_ref, *refs):
    sources = refs[:2]
    grad_query_ref, grad_own_ref, *targets, pairs, keys_t, grads, sems = refs[-8:]
    unit, head = pl.program_id(0), pl.program_id(1)
    all_pairs(table, mapped, sources, own_ref, pairs, sems)

    @pl.when(head == 0)
    def _():
        keys_t[...] = pair_half(pairs, unit, 0).T
        grads[unit] = jnp.zeros((KEYS, 2 * HEAD), f32)

    query = query_ref[...] * score_scale
    grad = grad_ref[...]
    scores = masked(table, length, dot_nt(pair_half(pairs, unit, 0), query), unit)
    probs = jnp.exp(scores - sum_ref[0])
    grad_probs = dot_nt(pair_half(pairs, unit, 1), grad)
    row_dot = jnp.sum(probs * grad_probs, axis=0, keepdims=True)
    grad_scores = (probs * (grad_probs - row_dot)).astype(bf)
    grads[unit, :, :HEAD] += dot_nn(grad_scores, query)
    grads[unit, :, HEAD:] += dot_nn(probs.astype(bf), grad)
    grad_query_ref[...] = dot_nn(keys_t[...], grad_scores).T * score_scale

    @pl.when((unit == UNITS - 1) & (head == HEADS - 1))
    def _():
        slots = [slot_of(table, mapped, number) for number in range(UNITS)]
        for s in range(GROUP):
            at = slice(s * PSLICE, (s + 1) * PSLICE)
            for option in range(2 * UNITS):
                total = jnp.zeros((PSLICE, 2 * HEAD), f32)
                for number in range(UNITS):
                    total += jnp.where(slots[number] == option, grads[number, at], 0.0)
                rows = pl.ds(option % UNITS * PSLICE, PSLICE)
                targets[option // UNITS][s, rows] = total.astype(bf)
        for number in range(UNITS):
            grad_own_ref[number * PSLICE : (number + 1) * PSLICE] = grads[number, PROMPT:]


def attend_back(table, mapped, length, query, grad, log_sum, own_pairs, sources, earlier):
    rows = UNITS * PSLICE
    whole = pl.BlockSpec(memory_space=pltpu.VMEM)
    return pl.pallas_call(
        attend_back_kernel,
        out_shape=(
            jax.ShapeDtypeStruct((rows, HEADS * HEAD), f32),
            jax.ShapeDtypeStruct((rows, 2 * HEAD), f32),
        )
        + (jax.ShapeDtypeStruct((GROUP, UNITS * PSLICE, 2 * HEAD), bf),) * 2,
        grid=(UNITS, HEADS),
        in_specs=[smem, smem, smem, unit_head, unit_head, sum_spec]
        + [anywhere] * (3 + len(earlier)),
        out_specs=(unit_head,) + (whole,) * 3,
        scratch_shapes=[
            pltpu.VMEM((UNITS, GROUP + 1, PSLICE, 2 * HEAD), bf),
            pltpu.VMEM((HEAD, KEYS), bf),
            pltpu.VMEM((UNITS, KEYS, 2 * HEAD), f32),
            pltpu.SemaphoreType.DMA((UNITS, 2)),
        ],
        compiler_params=pltpu.CompilerParams(vmem_limit_bytes=56 << 20),
        cost_estimate=pl.CostEstimate(
            flops=10 * rows * HEADS * KEYS * HEAD,
            bytes_accessed=2 * KEYS * 2 * HEAD * 6 + 10 * rows * HEADS * HEAD,
            transcendentals=rows * HEADS * KEYS,
        ),
        name="attend_back",
    )(table, mapped, length, query, grad, log_sum, own_pairs, *sources, *earlier)


GELU_SCALE = math.sqrt(2.0 / math.pi)
GELU_CUBE = 0.044715


def gelu_parts(gate):
    bent = jnp.tanh(GELU_SCALE * (gate + GELU_CUBE * (gate * gate * gate)))
    return bent, 0.5 * (1.0 + bent)


CUT = 80


def weight_copies(table, pieces, held, sems):
    copies = ([], [], [])

    def add(kind, source, target):
        number = sum(len(kept) for kept in copies)
        copies[kind].append(pltpu.make_async_copy(source, target, sems.at[number]))

    if len(pieces) == 1:
        for kind in range(3):
            add(kind, pieces[0].at[kind], held[kind])
        return copies
    shard = held[0].shape[0] // GROUP
    for way in range(2):
        for s in range(GROUP):
            piece = pieces[way * GROUP + s]
            start = pl.multiple_of(table[AT_RING + way * GROUP + s] * shard, 16)
            low, high = ((0, CUT), (CUT, shard))[way]
            add(way, piece.at[pl.ds(0, shard)], held[way].at[pl.ds(start, shard)])
            add(
                2,
                piece.at[pl.ds(shard, high - low)],
                held[2].at[pl.ds(pl.multiple_of(start + low, 16), high - low)],
            )
    return copies


def bring(copies, kinds, start):
    @pl.when(pl.program_id(0) == 0)
    def _():
        for kind in kinds:
            for copy in copies[kind]:
                copy.start() if start else copy.wait()


def pick_rows(first_ref, second_ref, rows):
    step = pl.program_id(0)

    @pl.when(step == 0)
    def _():
        rows[...] = first_ref[...]

    @pl.when(step == 1)
    def _():
        rows[...] = second_ref[...]


def put_rows(first_ref, second_ref, total):
    step = pl.program_id(0)

    @pl.when(step == 0)
    def _():
        first_ref[...] = total

    @pl.when(step == 1)
    def _():
        second_ref[...] = total


def feed_kernel(n_pieces, table, first_ref, second_ref, *refs):
    pieces, refs = refs[:n_pieces], refs[n_pieces:]
    gate_ref, up_ref, act_ref, first_out, second_out, rows, gate_w, up_w, down_w, sems = refs
    copies = weight_copies(table, pieces, (gate_w, up_w, down_w), sems)
    bring(copies, (0, 1, 2), True)
    pick_rows(first_ref, second_ref, rows)
    bring(copies, (0,), False)
    gate = dot_nn(rows[...], gate_w[...])
    bring(copies, (1,), False)
    up = dot_nn(rows[...], up_w[...])
    act = (gate * gelu_parts(gate)[1] * up).astype(bf)
    gate_ref[...] = gate.astype(bf)
    up_ref[...] = up.astype(bf)
    act_ref[...] = act
    bring(copies, (2,), False)
    put_rows(first_out, second_out, dot_nt(act, down_w[...]).astype(bf))


def feed_back_kernel(n_pieces, table, first_ref, second_ref, gate_ref, up_ref, *refs):
    pieces, refs = refs[:n_pieces], refs[n_pieces:]
    gate_out, up_out, first_out, second_out, rows, gate_w, up_w, down_w, sems = refs
    copies = weight_copies(table, pieces, (gate_w, up_w, down_w), sems)
    bring(copies, (2, 0, 1), True)
    pick_rows(first_ref, second_ref, rows)
    bring(copies, (2, 0, 1), False)
    total = jnp.zeros(rows.shape, f32)
    hidden = gate_ref.shape[1]
    for low in range(0, hidden, 512):
        at = slice(low, min(low + 512, hidden))
        grad_act = dot_nn(rows[...], down_w[:, at])
        gate, up = gate_ref[:, at].astype(f32), up_ref[:, at].astype(f32)
        bent, share = gelu_parts(gate)
        slope = share + 0.5 * gate * (1.0 - bent * bent) * (
            GELU_SCALE * (1.0 + 3.0 * GELU_CUBE * (gate * gate))
        )
        grad_gate = (grad_act * up * slope).astype(bf)
        grad_up = (grad_act * (gate * share)).astype(bf)
        gate_out[:, at] = grad_gate
        up_out[:, at] = grad_up
        total += dot_nt(grad_gate, gate_w[:, at]) + dot_nt(grad_up, up_w[:, at])
    put_rows(first_out, second_out, total.astype(bf))


def feed_call(kernel, name, table, first, second, hiddens, pieces, n_out):
    rows, dim = first.shape
    hidden = pieces[0].shape[-1]
    fixed = pl.BlockSpec((rows, dim), lambda i: (0, 0))
    wide = pl.BlockSpec((rows, hidden), lambda i: (i, 0))
    row_shape = jax.ShapeDtypeStruct((rows, dim), bf)
    wide_shape = jax.ShapeDtypeStruct((2 * rows, hidden), bf)
    return pl.pallas_call(
        functools.partial(kernel, len(pieces)),
        out_shape=(wide_shape,) * n_out + (row_shape, row_shape),
        grid=(2,),
        in_specs=[smem, fixed, fixed] + [wide] * len(hiddens) + [anywhere] * len(pieces),
        out_specs=(wide,) * n_out + (fixed, fixed),
        scratch_shapes=[pltpu.VMEM((rows, dim), bf)]
        + [pltpu.VMEM((dim, hidden), bf)] * 3
        + [pltpu.SemaphoreType.DMA((max(3, 2 * len(pieces)),))],
        compiler_params=pltpu.CompilerParams(vmem_limit_bytes=60 << 20),
        cost_estimate=pl.CostEstimate(
            flops=12 * rows * dim * hidden,
            bytes_accessed=6 * dim * hidden + 2 * rows * hidden * 2 * (n_out + len(hiddens)),
            transcendentals=2 * rows * hidden,
        ),
        name=name,
    )(table, first, second, *hiddens, *pieces)


def pass_on_kernel(moved, last, table, *refs):
    if moved:
        first_ref, second_ref, refs = refs[0], refs[1], refs[2:]
    gate_ref, up_ref, down_first, down_second = refs[:4]
    outs = refs[-3:] if last else refs[-2:]
    shard = gate_ref.shape[2]
    gate, up = gate_ref[0, 0].astype(f32), up_ref[0, 0].astype(f32)
    low, high = down_first[0, 0, :CUT].astype(f32), down_second[0, 0, CUT:].astype(f32)
    if moved:
        gate += first_ref[:shard].astype(f32)
        low += first_ref[shard:].astype(f32)
        up += second_ref[:shard].astype(f32)
        high += second_ref[shard:].astype(f32)
    if last:
        outs[0][...] = gate
        outs[1][...] = up
        outs[2][:CUT] = low
        outs[2][CUT:] = high
    else:
        outs[0][:shard] = gate.astype(bf)
        outs[0][shard:] = low.astype(bf)
        outs[1][:shard] = up.astype(bf)
        outs[1][shard:] = high.astype(bf)


def pass_on(table, moved, gate_up_w, down_w, s, earlier=()):
    _, _, shard, hidden = gate_up_w.shape
    width = 896
    last = s == 0

    def block(rows):
        return pl.BlockSpec((rows, width), lambda i, table: (0, i))

    def term(way, kind):
        return pl.BlockSpec(
            (1, 1, shard, width),
            lambda i, table: (table[AT_RING + way * GROUP + s], kind, 0, i),
        )

    heights = (shard,) * 3 if last else (shard + CUT, 2 * shard - CUT)
    kind = f32 if last else bf
    return pl.pallas_call(
        functools.partial(pass_on_kernel, len(moved), last),
        out_shape=tuple(jax.ShapeDtypeStruct((rows, hidden), kind) for rows in heights),
        grid_spec=pltpu.PrefetchScalarGridSpec(
            num_scalar_prefetch=1,
            grid=(pl.cdiv(hidden, width),),
            in_specs=[block(part.shape[0]) for part in moved]
            + [term(0, 0), term(1, 1), term(0, 0), term(1, 0)]
            + [anywhere] * len(earlier),
            out_specs=tuple(block(rows) for rows in heights),
        ),
        compiler_params=pltpu.CompilerParams(vmem_limit_bytes=60 << 20),
        name="pass_on",
    )(table, *moved, gate_up_w, gate_up_w, down_w, down_w, *earlier)


def weight_grad_kernel(number, *refs):
    blocks, halves = refs[:TENSOR], refs[TENSOR : TENSOR + 2 * number]
    out_ref, turned = refs[TENSOR + 2 * number :]
    rows = blocks[0].shape[0]

    @pl.when(pl.program_id(0) == 0)
    def _():
        for j in range(TENSOR):
            turned[:, j * rows : (j + 1) * rows] = blocks[j][...].T

    for k in range(number):
        total = dot_nn(turned[:, : 2 * rows], halves[2 * k][...])
        total += dot_nn(turned[:, 2 * rows :], halves[2 * k + 1][...])
        out_ref[:, k] = total.astype(bf).reshape(out_ref.shape[0], out_ref.shape[2], -1)


def weight_grads(name, blocks, halves, parts):
    rows, dim = blocks[0].shape
    hidden = halves[0].shape[1]
    number = len(halves) // 2
    width = 256
    return pl.pallas_call(
        functools.partial(weight_grad_kernel, number),
        out_shape=jax.ShapeDtypeStruct((parts, number, dim // parts, hidden), bf),
        grid=(pl.cdiv(hidden, width),),
        in_specs=[pl.BlockSpec((rows, dim), lambda i: (0, 0), pipeline_mode=pl.Buffered(1))]
        * TENSOR
        + [pl.BlockSpec((2 * rows, width), lambda i: (0, i))] * (2 * number),
        out_specs=pl.BlockSpec((parts, number, dim // parts, width), lambda i: (0, 0, 0, i)),
        scratch_shapes=[pltpu.VMEM((dim, TENSOR * rows), bf)],
        compiler_params=pltpu.CompilerParams(vmem_limit_bytes=48 << 20),
        cost_estimate=pl.CostEstimate(
            flops=3 * number * rows * dim * hidden,
            bytes_accessed=4 * rows * dim + number * (4 * rows + 2 * dim) * hidden,
            transcendentals=0,
        ),
        name=name,
    )(*blocks, *halves)


def norm_rate(value):
    return lax.rsqrt(jnp.mean(value * value, axis=-1, keepdims=True) + eps_norm)


def norm_back(value, gain, grad):
    rate = norm_rate(value)
    scaled = (1.0 + gain) * grad
    back = rate * scaled - value * (rate * rate * rate) * jnp.mean(
        value * scaled, axis=-1, keepdims=True
    )
    return back, jnp.sum(value * rate * grad, axis=0, keepdims=True)


def add_up(ref, value):
    step = pl.program_id(0)

    @pl.when(step == 0)
    def _():
        ref[...] = value

    @pl.when(step > 0)
    def _():
        ref[...] += value


def three_parts(refs):
    return refs[0][...].astype(f32) + refs[1][...].astype(f32) + refs[2][...].astype(f32)


def result_kernel(table, length, scale, *refs):
    mixed_ref, teacher_ref, gain_ref = refs[3:6]
    result_ref, grad_ref, low_ref, gain_out, loss_out = refs[6:]
    gain = gain_ref[...]
    value = three_parts(refs)
    result = mixed_ref[...] + value * norm_rate(value) * (1.0 + gain)
    result_ref[...] = result.astype(bf)
    row = lax.broadcasted_iota(jnp.int32, (PSLICE, 1), 0)
    live = length[table[AT_CORE] * UNITS + pl.program_id(0)]
    live = jnp.where(table[AT_CONT] == 1, live, PSLICE)
    diff = jnp.where(row < live, result - teacher_ref[...].astype(f32), 0.0)
    add_up(loss_out, jnp.sum(diff * diff, axis=0, keepdims=True))
    grad = scale[0] * diff
    grad_ref[...] = grad
    back, gain_grad = norm_back(value, gain, grad)
    low_ref[...] = back.astype(bf)
    add_up(gain_out, gain_grad)


def mixed_kernel(*refs):
    mixed_ref, sum_ref, grad_ref, ffw_gain_ref, post_gain_ref = refs[3:8]
    mixed_out, low_out, ffw_out, post_out = refs[8:]
    back, ffw_grad = norm_back(mixed_ref[...], ffw_gain_ref[...], three_parts(refs))
    grad_mixed = grad_ref[...] + back
    mixed_out[...] = grad_mixed
    add_up(ffw_out, ffw_grad)
    back, post_grad = norm_back(sum_ref[...], post_gain_ref[...], grad_mixed)
    low_out[...] = back.astype(bf)
    add_up(post_out, post_grad)


def input_kernel(part_ref, low_ref, kv_ref, input_ref, grad_ref, gain_ref, out_ref, gain_out):
    grad = part_ref[...] + dot_nt(low_ref[...], kv_ref[...])
    back, gain_grad = norm_back(input_ref[...].astype(f32), gain_ref[...], grad)
    out_ref[...] = (grad_ref[...] + back).astype(bf)
    add_up(gain_out, gain_grad)


def by_rows(kernel, name, scalars, operands, outs):
    def spec(shape, whole=False):
        if whole or shape[0] == 1:
            return pl.BlockSpec(shape, lambda i: (0, 0))
        return pl.BlockSpec((PSLICE, shape[1]), lambda i: (i, 0))

    operands = [part if isinstance(part, tuple) else (part, False) for part in operands]
    return pl.pallas_call(
        kernel,
        out_shape=tuple(jax.ShapeDtypeStruct(shape, kind) for shape, kind in outs),
        grid=(UNITS,),
        in_specs=[smem] * len(scalars) + [spec(part.shape, whole) for part, whole in operands],
        out_specs=tuple(spec(shape) for shape, _ in outs),
        compiler_params=pltpu.CompilerParams(vmem_limit_bytes=48 << 20),
        cost_estimate=pl.CostEstimate(
            flops=20 * UNITS * PSLICE * 1152, bytes_accessed=16 << 20, transcendentals=0
        ),
        name=name,
    )(*scalars, *[part for part, _ in operands])


def local(
    layer_in,
    teacher,
    query_proj,
    key_proj,
    value_proj,
    out_proj,
    gate_proj,
    up_proj,
    down_proj,
    attn_norm,
    attn_post,
    ffw_norm,
    ffw_post,
    query_norm,
    key_norm,
    cont_prompt,
    cont_length,
    token_count,
    loss_scale,
):
    members = lax.axis_size("fsdp")
    fsdp_pos = lax.axis_index("fsdp")
    tensor_pos = lax.axis_index("tensor")
    core, side = tensor_pos % 2, tensor_pos // 2
    is_cont = side == 1
    group_slot = fsdp_pos % GROUP
    table = lax.dynamic_index_in_dim(
        jnp.asarray(place_table(members)), fsdp_pos * TENSOR + tensor_pos, 0, keepdims=False
    )
    dim = layer_in.shape[1]

    ringed = members == GROUP
    down_own = down_proj.T
    if ringed:
        parts = GROUP
        weights = Spread(
            jnp.concatenate([gate_proj, down_own[:CUT]], 0),
            jnp.concatenate([up_proj, down_own[CUT:]], 0),
        )
        came = [()] + [weights.step() for _ in range(4)]
    else:
        came = [()] * (GROUP + 1)
        parts = 1
        pieces = (gate_proj, up_proj, down_own)
        pieces = [jnp.stack([lax.all_gather(w, "fsdp", axis=0, tiled=True) for w in pieces])]

    shard_kv = key_proj.shape[0]
    shard_gain, shard_head = attn_norm.shape[0], query_norm.shape[0]
    gains_own = jnp.stack(
        [
            jnp.pad(gain, (0, 2 * HEAD - gain.shape[0]))
            for gain in (attn_norm, attn_post, ffw_norm, ffw_post, query_norm, key_norm)
        ]
    )
    packed = jnp.concatenate([jnp.concatenate([key_proj, value_proj], 1), gains_own], 0)
    packed = jnp.pad(packed, ((0, -packed.shape[0] % 16), (0, 0)))
    packed_f = spread_y(spread_z(packed))
    packed_all = place(table, spread_tensor(packed_f))
    qo_own = jnp.concatenate([query_proj, out_proj.T], 1)
    qo_column = spread_z(after(qo_own, packed_f))
    kv_full = packed_all[:, :, :shard_kv].reshape(dim, 2 * HEAD)
    gains_all = packed_all[:, :, shard_kv : shard_kv + 6].astype(f32)

    def gain_of(number):
        return gains_all[:, :, number, :shard_gain].reshape(dim)

    def head_gain_of(number):
        return gains_all[:, :, 4 + number, :shard_head].reshape(HEAD)

    attn_gain, attn_post_gain, ffw_gain, ffw_post_gain = (gain_of(k) for k in range(4))
    query_gain, key_gain = head_gain_of(0), head_gain_of(1)

    local_rows = layer_in.shape[0]
    unit_ids = jnp.arange(local_rows, dtype=jnp.int32) % PSLICE
    positions = unit_ids + jnp.where(is_cont, PROMPT, group_slot * PSLICE)
    inverse_freq = jnp.exp(
        -math.log(rope_base) * 2.0 * jnp.arange(HEAD // 2, dtype=f32) / HEAD
    )
    angles = positions.astype(f32)[:, None] * inverse_freq[None, :]
    cosine, sine_part = jnp.cos(angles), jnp.sin(angles)
    input_f = layer_in.astype(f32)
    normed_in = rms_scale(input_f, attn_gain).astype(bf)

    kv_raw = dot_nn(normed_in, kv_full)
    key_raw = kv_raw[:, :HEAD]
    key_rot = head_prep(key_raw, key_gain, cosine, sine_part).astype(bf)
    own_pairs = jnp.concatenate([key_rot, kv_raw[:, HEAD:].astype(bf)], 1)
    own_pairs = after(own_pairs, qo_column, *came[1])
    qo_column = spread_y(after(qo_column, packed_all))
    across = lax.ppermute(own_pairs, "tensor", [(0, 2), (1, 3)])
    prompt_pairs = after(jnp.where(is_cont, across, own_pairs), qo_column, *came[2])
    if ringed:
        held_pairs = lax.all_gather(prompt_pairs, "fsdp", axis=0)
    else:
        held_pairs = [prompt_pairs]
        while len(held_pairs) < GROUP:
            held_pairs.append(ring_step(held_pairs[-1], 1))
        held_pairs = jnp.stack(held_pairs)
    qo_column = after(qo_column, across)
    qo_near, qo_far = spread_near(qo_column)
    query_full, out_full = (
        part.reshape(dim, HEADS * HEAD)
        for part in place_heads(
            table, (qo_column, qo_near, qo_far, swap_core(after(qo_far, *came[3])))
        )
    )
    query_raw = dot_nn(normed_in, query_full)
    query_heads = [
        head_prep(query_raw[:, h * HEAD : (h + 1) * HEAD], query_gain, cosine, sine_part).astype(bf)
        for h in range(HEADS)
    ]

    query_rot = jnp.concatenate(query_heads, 1)
    if ringed:
        came += [weights.step(query_rot), weights.step(), weights.step()]
    held_pairs = after(held_pairs, query_rot, *came[5])
    query_rot = after(query_rot, *came[6])
    sources = held_pairs, lax.ppermute(held_pairs, "tensor", [(2, 3), (3, 2)])
    attn_low, log_sum = attend(
        table, cont_prompt, cont_length, query_rot, own_pairs, sources
    )
    attn_sum = dot_nt(attn_low, out_full)
    if ringed:
        pieces = weights.firsts + weights.seconds
    mixed = input_f + rms_scale(attn_sum, attn_post_gain)
    normed_mid = rms_scale(mixed, ffw_gain).astype(bf)

    mid_near, mid_far = spread_near(after(normed_mid, *came[7]))
    gate_0, up_0, act_0, *downs = feed_call(
        feed_kernel, "feed", table, normed_mid, mid_near, (), pieces, 3
    )
    mid_last = swap_core(after(mid_far, downs[0]))
    gate_1, up_1, act_1, *more = feed_call(
        feed_kernel, "feed", table, mid_far, mid_last, (), pieces, 3
    )
    downs += more
    downs_moved = swap_core(downs[1]), swap_x(collect_far(*downs[2:]))
    count_f = token_count.astype(f32)
    row_kind, gain_kind = (local_rows, dim), ((1, dim), f32)
    result_low, grad_result, grad_ffw_low, grad_ffw_post_gain, loss_lanes = by_rows(
        result_kernel,
        "result",
        (table, cont_length, (loss_scale / count_f * 2.0)[None]),
        (downs[0], *downs_moved, mixed, teacher, ffw_post_gain[None]),
        ((row_kind, bf), (row_kind, f32), (row_kind, bf), gain_kind, gain_kind),
    )
    loss_part = jnp.sum(loss_lanes)

    grad_near, grad_far = spread_near(grad_ffw_low)
    gate_low_0, up_low_0, *mids = feed_call(
        feed_back_kernel, "feed_back", table, grad_ffw_low, grad_near, (gate_0, up_0), pieces, 2
    )
    grad_last = swap_core(after(grad_far, mids[0]))
    gate_low_1, up_low_1, *more = feed_call(
        feed_back_kernel, "feed_back", table, grad_far, grad_last, (gate_1, up_1), pieces, 2
    )
    mids += more
    mids_far = collect_far(*mids[2:])
    mids_moved = swap_core(mids[1]), swap_x(mids_far)
    down_w = weight_grads(
        "down_grad",
        (after(grad_ffw_low, mids_far), grad_near, grad_far, grad_last),
        (act_0, act_1),
        parts,
    )
    gate_up_w = weight_grads(
        "gate_up_grad",
        (after(normed_mid, mids_far), mid_near, mid_far, mid_last),
        (gate_low_0, gate_low_1, up_low_0, up_low_1),
        parts,
    )
    if ringed:
        held_sums = pass_on(table, (), gate_up_w, down_w, GROUP - 1)

        def move_sums():
            return ring_step(held_sums[0], -1), ring_step(held_sums[1], 1)

        def add_sums(moved, s, *earlier):
            return pass_on(table, moved, gate_up_w, down_w, s, earlier)

    else:
        out_down = lax.psum_scatter(down_w[0, 0], "fsdp", scatter_dimension=0, tiled=True)
        out_down = out_down.astype(f32)
        out_gate, out_up = lax.psum_scatter(
            gate_up_w[0], "fsdp", scatter_dimension=1, tiled=True
        ).astype(f32)

    grad_mixed, grad_attn_low, grad_ffw_gain, grad_attn_post_gain = by_rows(
        mixed_kernel,
        "mixed_back",
        (),
        (mids[0], *mids_moved, mixed, attn_sum, grad_result, ffw_gain[None], attn_post_gain[None]),
        ((row_kind, f32), (row_kind, bf), gain_kind, gain_kind),
    )
    grad_out_w = dot_tn(grad_attn_low, attn_low)
    grad_attn_rows = dot_nn(grad_attn_low, out_full).astype(bf)
    if ringed:
        held_sums = add_sums(move_sums(), 6, grad_attn_rows)
    grad_query_rot, grad_own, kept, given = attend_back(
        table, cont_prompt, cont_length, query_rot, grad_attn_rows, log_sum, own_pairs, sources, held_sums if ringed else ()
    )
    if ringed:
        moved = move_sums()
        given = after(given, *moved)
        held_sums = add_sums(moved, 5)
    given = lax.ppermute(given, "tensor", [(2, 3), (3, 2)])
    kept = (kept.astype(f32) + given.astype(f32)).astype(bf)
    if ringed:
        for s in (4, 3, 2):
            held_sums = add_sums(move_sums(), s)
        summed = lax.psum_scatter(kept, "fsdp", scatter_dimension=0)
        summed = after(summed, *held_sums).astype(f32)
    else:
        summed = kept[GROUP - 1]
        for s in reversed(range(GROUP - 1)):
            summed = (ring_step(summed, -1).astype(f32) + kept[s].astype(f32)).astype(bf)
        summed = summed.astype(f32)
    back = lax.ppermute(summed.astype(bf), "tensor", [(2, 0), (3, 1)]).astype(f32)
    grad_pairs = jnp.where(is_cont, grad_own, summed + back)

    _, query_pull = jax.vjp(
        lambda raw, gain: tuple(
            head_prep(raw[:, h * HEAD : (h + 1) * HEAD], gain, cosine, sine_part)
            for h in range(HEADS)
        ),
        query_raw,
        query_gain,
    )
    grad_query_raw, grad_query_gain = query_pull(
        tuple(grad_query_rot[:, h * HEAD : (h + 1) * HEAD] for h in range(HEADS))
    )
    _, key_pull = jax.vjp(
        lambda raw, gain: head_prep(raw, gain, cosine, sine_part), key_raw, key_gain
    )
    grad_key_raw, grad_key_gain = key_pull(grad_pairs[:, :HEAD])
    grad_query_low = grad_query_raw.astype(bf)
    grad_kv_low = jnp.concatenate([grad_key_raw, grad_pairs[:, HEAD:]], 1).astype(bf)
    grad_query_w = dot_tn(normed_in, grad_query_low)
    grad_kv_w = dot_tn(normed_in, grad_kv_low)
    grad_input, grad_attn_gain = by_rows(
        input_kernel,
        "input_back",
        (),
        (
            dot_nt(grad_query_low, query_full),
            grad_kv_low,
            (kv_full, True),
            layer_in,
            grad_mixed,
            attn_gain[None],
        ),
        ((row_kind, bf), gain_kind),
    )

    qo_sum = collect_tensor(
        *(
            jnp.concatenate(
                [grad_query_w[:, h * HEAD : (h + 1) * HEAD], grad_out_w[:, h * HEAD : (h + 1) * HEAD]],
                1,
            )
            for h in range(HEADS)
        )
    ).reshape(members, dim // members, 2 * HEAD)
    out_qo = collect_fsdp(qo_sum, fsdp_pos)
    out_query, out_out = out_qo[:, :HEAD], out_qo[:, HEAD:].T
    kv_blocks = grad_kv_w.reshape(members, TENSOR, shard_kv, 2 * HEAD)
    kv_column = collect_tensor(
        *order_tensor([kv_blocks[:, t] for t in range(TENSOR)], tensor_pos)
    )
    out_kv = collect_fsdp(kv_column, fsdp_pos)

    if ringed:
        held_sums = add_sums(move_sums(), 1, grad_kv_w)
        held_sums = add_sums(move_sums(), 0)
        out_gate, out_up, out_down = held_sums
    out_down = out_down.T

    small = jnp.concatenate(
        [
            grad_attn_gain[0],
            grad_attn_post_gain[0],
            grad_ffw_gain[0],
            grad_ffw_post_gain[0],
            grad_query_gain,
            grad_key_gain,
            loss_part[None],
        ]
    )
    length = small.shape[0]
    small = jnp.pad(small, (0, -length % 1024)).reshape(-1, 128)
    small = sum_all(small).reshape(-1)
    device = fsdp_pos * TENSOR + tensor_pos
    wide = [
        lax.dynamic_slice(small, (k * dim + device * shard_gain,), (shard_gain,)) for k in range(4)
    ]
    narrow = [
        lax.dynamic_slice(small, (4 * dim + k * HEAD + device * shard_head,), (shard_head,))
        for k in range(2)
    ]
    loss = small[length - 1] / count_f
    return (
        result_low,
        loss,
        grad_input,
        out_query,
        out_kv[:, :HEAD],
        out_kv[:, HEAD:],
        out_out,
        out_gate,
        out_up,
        out_down,
        *wide,
        *narrow,
    )


def solution(mesh):
    rows = P(("fsdp", "tensor"), None)
    split = P(("fsdp", "tensor"))
    inward, outward = P("fsdp", "tensor"), P("tensor", "fsdp")
    return jax.shard_map(
        local,
        mesh=mesh,
        in_specs=(
            rows,
            rows,
            inward,
            rows,
            rows,
            outward,
            inward,
            inward,
            outward,
            *(split,) * 6,
            P("fsdp"),
            P("fsdp"),
            P(),
            P(),
        ),
        out_specs=(
            rows,
            P(),
            rows,
            inward,
            rows,
            rows,
            outward,
            inward,
            inward,
            outward,
            *(split,) * 6,
        ),
        check_vma=False,
    )
```

```python
import functools
import math

import jax
import jax.numpy as jnp
import numpy as np
from jax import lax
from jax.experimental import pallas as pl
from jax.experimental.pallas import tpu as pltpu
from jax.sharding import PartitionSpec as P

HEAD = 256
HEADS = 4
PROMPT = 2048
CONT = 256
GROUP = 8
GROUPS_DEV = 4
PSLICE = 256
UNITS = 2
TENSOR = 4

RING = (0, 2, 4, 6, 7, 5, 3, 1)
PLACE = tuple(RING.index(member) for member in range(GROUP))

eps_norm = 1e-06
rope_base = 1000000.0
masked_score = -1e30
score_scale = 1.0 / math.sqrt(HEAD)
bf = jnp.bfloat16
f32 = jnp.float32


def swap_core(value):
    return lax.ppermute(value, "tensor", [(t, t ^ 1) for t in range(TENSOR)])


def swap_x(value):
    return lax.ppermute(value, "tensor", [(t, t ^ 2) for t in range(TENSOR)])


def swap_bit(value, bit):
    size = lax.axis_size("fsdp")
    return lax.ppermute(value, "fsdp", [(f, f ^ bit) for f in range(size)])


def shift_z(value, step):
    pairs = [(z * 2 + y, (z + step) % 4 * 2 + y) for z in range(4) for y in range(2)]
    return lax.ppermute(value, "fsdp", pairs)


def ring_step(value, way):
    size = lax.axis_size("fsdp")
    pairs = []
    for base in range(0, size, GROUP):
        for at in range(GROUP):
            pairs.append((base + RING[at], base + RING[(at + way) % GROUP]))
    return lax.ppermute(value, "fsdp", pairs)


def spread_tensor(own):
    far = swap_x(own)
    near = swap_core(own)
    return own, near, far, swap_core(far)


def spread_near(own):
    return swap_core(own), swap_x(own)


def collect_tensor(part_0, part_1, part_2, part_3):
    return collect_near(part_0, part_1, collect_far(part_2, part_3))


def collect_far(part_2, part_3):
    return (part_2.astype(f32) + swap_core(part_3.astype(bf)).astype(f32)).astype(bf)


def collect_near(part_0, part_1, far):
    far = swap_x(far)
    near = part_0.astype(f32) + swap_core(part_1.astype(bf)).astype(f32)
    return near + far.astype(f32)


def after(value, *earlier):
    return lax.optimization_barrier((value,) + earlier)[0]


def pick(stack, index, axis=0):
    return lax.dynamic_index_in_dim(stack, index, axis, keepdims=False)


def spread_z(own):
    if lax.axis_size("fsdp") != GROUP:
        return own
    return jnp.stack([own] + [shift_z(own, step) for step in (1, 2, 3)])


def spread_y(column):
    if lax.axis_size("fsdp") != GROUP:
        return lax.all_gather(column, "fsdp", axis=0)
    return jnp.concatenate([column, swap_bit(column, 1)])


def collect_fsdp(parts, fsdp_pos):
    if lax.axis_size("fsdp") != GROUP:
        return lax.psum_scatter(parts.astype(bf), "fsdp", scatter_dimension=0).astype(f32)
    z, y = fsdp_pos // 2, fsdp_pos % 2
    paired = parts.reshape((4, 2) + parts.shape[1:])
    give = pick(paired, 1 - y, 1).astype(bf)
    column = pick(paired, y, 1).astype(f32) + swap_bit(give, 1).astype(f32)
    total = pick(column, z)
    for step in (1, 2, 3):
        total = total + shift_z(pick(column, (z + step) % 4).astype(bf), step).astype(f32)
    return total


def order_tensor(blocks, tensor_pos):
    odd = tensor_pos % 2 == 1
    high = tensor_pos // 2 == 1
    a, b, c, d = blocks
    a, b = jnp.where(odd, b, a), jnp.where(odd, a, b)
    c, d = jnp.where(odd, d, c), jnp.where(odd, c, d)
    return (
        jnp.where(high, c, a),
        jnp.where(high, d, b),
        jnp.where(high, a, c),
        jnp.where(high, b, d),
    )


def sum_all(value):
    value = value + swap_core(value)
    value = value + swap_x(value)
    bit = 1
    while bit < lax.axis_size("fsdp"):
        value = value + swap_bit(value, bit)
        bit *= 2
    return value


def sum_both(parts, small, fsdp_pos):
    z, y = fsdp_pos // 2, fsdp_pos % 2
    moved = swap_core(parts[1].astype(bf)), swap_core(parts[3].astype(bf)), swap_core(small)
    far = (parts[2].astype(f32) + moved[1].astype(f32)).astype(bf)
    near = parts[0].astype(f32) + moved[0].astype(f32)
    far, near, small = lax.optimization_barrier((far, near, small + moved[2]))
    moved = swap_x(far), swap_x(small)
    column = near + moved[0].astype(f32)
    column, small = lax.optimization_barrier((column, small + moved[1]))
    paired = column.reshape((4, 2) + column.shape[1:])
    moved = swap_bit(pick(paired, 1 - y, 1).astype(bf), 1), swap_bit(small, 1)
    column = pick(paired, y, 1) + moved[0].astype(f32)
    column, small = lax.optimization_barrier((column, small + moved[1]))
    moved = [shift_z(pick(column, (z + step) % 4).astype(bf), step) for step in (1, 2, 3)]
    small = small + swap_bit(small, 2)
    total = pick(column, z)
    for part in moved:
        total = total + part.astype(f32)
    return total, small + swap_bit(small, 4), column


class Spread:
    def __init__(self, first, second):
        self.firsts, self.seconds = [first], [second]

    def step(self, *earlier):
        first, second = self.firsts[-1], self.seconds[-1]
        if earlier:
            first, second = after(first, *earlier), after(second, *earlier)
        self.firsts.append(ring_step(first, 1))
        self.seconds.append(ring_step(second, -1))
        return self.firsts[-1], self.seconds[-1]


def rms_scale(tensor_in, gain_vec):
    return (
        tensor_in
        * lax.rsqrt(jnp.mean(tensor_in * tensor_in, axis=-1, keepdims=True) + eps_norm)
        * (1.0 + gain_vec)
    )


def rotate(tensor_in, cosine, sine_part):
    half_dim = tensor_in.shape[-1] // 2
    first_half = tensor_in[..., :half_dim]
    second_half = tensor_in[..., half_dim:]
    return jnp.concatenate(
        [
            first_half * cosine - second_half * sine_part,
            second_half * cosine + first_half * sine_part,
        ],
        axis=-1,
    )


def head_prep(raw_in, gain_vec, cosine, sine_part):
    return rotate(rms_scale(raw_in, gain_vec), cosine, sine_part)


def dot_nn(left, right):
    return jnp.dot(left, right, preferred_element_type=f32)


def dot_tn(left, right):
    return lax.dot_general(left, right, (((0,), (0,)), ((), ())), preferred_element_type=f32)


def dot_nt(left, right):
    return lax.dot_general(left, right, (((1,), (1,)), ((), ())), preferred_element_type=f32)


AT_FSDP, AT_TENSOR, AT_REACH, AT_CONT, AT_CORE, AT_RING = 0, 64, 68, 84, 85, 88
TABLE_WIDTH = 128
FAR = 1 << 20


def place_table(members):
    table = np.zeros((members * TENSOR, TABLE_WIDTH), np.int32)
    for f in range(members):
        slot = f % GROUP
        place = PLACE[slot]
        for t in range(TENSOR):
            row = table[f * TENSOR + t]
            for r in range(members):
                if members == GROUP:
                    row[AT_FSDP + r] = (f // 2 - r % 4) % 4 * 2 + (f % 2 ^ r // 4)
                else:
                    row[AT_FSDP + r] = r
            row[AT_TENSOR : AT_TENSOR + TENSOR] = [t ^ j for j in range(TENSOR)]
            for unit in range(UNITS):
                for s in range(GROUP):
                    source = RING[(place - s * (1 - 2 * unit)) % GROUP]
                    row[AT_RING + unit * GROUP + s] = source
            for s in range(GROUP):
                source = s if members == GROUP else RING[(place - s) % GROUP]
                row[AT_REACH + s] = FAR if t // 2 else (slot - source) * PSLICE
            row[AT_CONT], row[AT_CORE] = t // 2, t % 2
    return table


KEYS = PROMPT + CONT
smem = pl.BlockSpec(memory_space=pltpu.SMEM)
anywhere = pl.BlockSpec(memory_space=pl.ANY)


def place_kernel(table, *refs):
    for r in range(refs[0].shape[0]):
        for j in range(TENSOR):
            refs[TENSOR][table[AT_FSDP + r], table[AT_TENSOR + j]] = refs[j][r]


def place(table, blocks):
    members, rows, width = blocks[0].shape
    return pl.pallas_call(
        place_kernel,
        out_shape=jax.ShapeDtypeStruct((members, TENSOR, rows, width), bf),
        in_specs=[smem] + [pl.BlockSpec(memory_space=pltpu.VMEM)] * TENSOR,
        out_specs=pl.BlockSpec(memory_space=pltpu.VMEM),
        name="place_pairs",
    )(table, *blocks)


def place_heads_kernel(table, *refs):
    query_ref, out_ref = refs[TENSOR:]
    for j in range(TENSOR):
        at = slice(j * HEAD, (j + 1) * HEAD)
        query_ref[0, :, at] = refs[j][0, :, :HEAD]
        out_ref[0, :, at] = refs[j][0, :, HEAD:]


def place_heads(table, blocks):
    members, rows, width = blocks[0].shape
    shape = jax.ShapeDtypeStruct((members, rows, HEADS * HEAD), bf)
    spec = pl.BlockSpec(
        (1, rows, HEADS * HEAD), lambda r, table: (table[AT_FSDP + r], 0, 0)
    )
    return pl.pallas_call(
        place_heads_kernel,
        out_shape=(shape, shape),
        grid_spec=pltpu.PrefetchScalarGridSpec(
            num_scalar_prefetch=1,
            grid=(members,),
            in_specs=[pl.BlockSpec((1, rows, width), lambda r, table: (r, 0, 0))] * TENSOR,
            out_specs=(spec, spec),
        ),
        name="place_heads",
    )(table, *blocks)


def slot_of(table, mapped, unit):
    core = table[AT_CORE]
    target = mapped[core * UNITS + unit]
    other = jnp.where(target // UNITS == core, 0, UNITS)
    return jnp.where(table[AT_CONT] == 1, other + target % UNITS, unit)


def load_pairs(table, mapped, sources, own_ref, pairs, sems, unit, start):
    slot = slot_of(table, mapped, unit)
    for option in range(2 * UNITS):

        @pl.when(slot == option)
        def _(option=option):
            rows = pl.ds(option % UNITS * PSLICE, PSLICE)
            copy = pltpu.make_async_copy(
                sources[option // UNITS].at[:, rows],
                pairs.at[unit, pl.ds(0, GROUP)],
                sems.at[unit, 0],
            )
            copy.start() if start else copy.wait()

    copy = pltpu.make_async_copy(
        own_ref.at[pl.ds(unit * PSLICE, PSLICE)], pairs.at[unit, GROUP], sems.at[unit, 1]
    )
    copy.start() if start else copy.wait()


def pair_half(pairs, unit, half):
    return pairs[unit, :, :, half * HEAD : (half + 1) * HEAD].reshape(KEYS, HEAD)


def all_pairs(table, mapped, sources, own_ref, pairs, sems):
    unit, head = pl.program_id(0), pl.program_id(1)

    @pl.when((unit == 0) & (head == 0))
    def _():
        for number in range(UNITS):
            load_pairs(table, mapped, sources, own_ref, pairs, sems, number, True)

    for number in range(UNITS):

        @pl.when((unit == number) & (head == 0))
        def _(number=number):
            load_pairs(table, mapped, sources, own_ref, pairs, sems, number, False)


def masked(table, length, scores, unit):
    key_of = lax.broadcasted_iota(jnp.int32, (PSLICE, PSLICE), 0)
    lag = key_of - lax.broadcasted_iota(jnp.int32, (PSLICE, PSLICE), 1)
    parts = []
    for s in range(GROUP):
        reach = table[AT_REACH + s]
        part = scores[s * PSLICE : (s + 1) * PSLICE]
        parts.append(jnp.where(lag <= reach, part, masked_score))
    live = length[table[AT_CORE] * UNITS + unit]
    live = jnp.where(table[AT_CONT] == 1, live, 0)
    parts.append(jnp.where((lag <= 0) & (key_of < live), scores[PROMPT:], masked_score))
    return jnp.concatenate(parts, 0)


def attend_kernel(table, mapped, length, query_ref, own_ref, *refs):
    sources = refs[:2]
    out_ref, sum_ref, pairs, values_t, sems = refs[2:]
    unit, head = pl.program_id(0), pl.program_id(1)
    all_pairs(table, mapped, sources, own_ref, pairs, sems)

    @pl.when(head == 0)
    def _():
        values_t[...] = pair_half(pairs, unit, 1).T

    query = query_ref[...] * score_scale
    scores = masked(table, length, dot_nt(pair_half(pairs, unit, 0), query), unit)
    top = jnp.max(scores, axis=0, keepdims=True)
    shifted = jnp.exp(scores - top)
    total = jnp.sum(shifted, axis=0, keepdims=True)
    out = dot_nn(values_t[...], shifted.astype(bf)) / total
    out_ref[...] = out.T.astype(bf)
    sum_ref[0] = top + jnp.log(total)


unit_head = pl.BlockSpec((PSLICE, HEAD), lambda u, h: (u, h))
sum_spec = pl.BlockSpec((1, 1, PSLICE), lambda u, h: (u * HEADS + h, 0, 0))


def attend(table, mapped, length, query, own_pairs, sources):
    rows = UNITS * PSLICE
    return pl.pallas_call(
        attend_kernel,
        out_shape=(
            jax.ShapeDtypeStruct((rows, HEADS * HEAD), bf),
            jax.ShapeDtypeStruct((UNITS * HEADS, 1, PSLICE), f32),
        ),
        grid=(UNITS, HEADS),
        in_specs=[smem, smem, smem, unit_head] + [anywhere] * 3,
        out_specs=(unit_head, sum_spec),
        scratch_shapes=[
            pltpu.VMEM((UNITS, GROUP + 1, PSLICE, 2 * HEAD), bf),
            pltpu.VMEM((HEAD, KEYS), bf),
            pltpu.SemaphoreType.DMA((UNITS, 2)),
        ],
        compiler_params=pltpu.CompilerParams(vmem_limit_bytes=40 << 20),
        cost_estimate=pl.CostEstimate(
            flops=4 * rows * HEADS * KEYS * HEAD,
            bytes_accessed=2 * KEYS * 2 * HEAD * 2 + 4 * rows * HEADS * HEAD,
            transcendentals=rows * HEADS * KEYS,
        ),
        name="attend",
    )(table, mapped, length, query, own_pairs, *sources)


def attend_back_kernel(table, mapped, length, query_ref, grad_ref, sum_ref, own_ref, *refs):
    sources = refs[:2]
    grad_query_ref, grad_own_ref, *targets, pairs, keys_t, grads, sems = refs[-8:]
    unit, head = pl.program_id(0), pl.program_id(1)
    all_pairs(table, mapped, sources, own_ref, pairs, sems)

    @pl.when(head == 0)
    def _():
        keys_t[...] = pair_half(pairs, unit, 0).T
        grads[unit] = jnp.zeros((KEYS, 2 * HEAD), f32)

    query = query_ref[...] * score_scale
    grad = grad_ref[...]
    scores = masked(table, length, dot_nt(pair_half(pairs, unit, 0), query), unit)
    probs = jnp.exp(scores - sum_ref[0])
    grad_probs = dot_nt(pair_half(pairs, unit, 1), grad)
    row_dot = jnp.sum(probs * grad_probs, axis=0, keepdims=True)
    grad_scores = (probs * (grad_probs - row_dot)).astype(bf)
    grads[unit, :, :HEAD] += dot_nn(grad_scores, query)
    grads[unit, :, HEAD:] += dot_nn(probs.astype(bf), grad)
    grad_query_ref[...] = dot_nn(keys_t[...], grad_scores).T * score_scale

    @pl.when((unit == UNITS - 1) & (head == HEADS - 1))
    def _():
        slots = [slot_of(table, mapped, number) for number in range(UNITS)]
        for s in range(GROUP):
            at = slice(s * PSLICE, (s + 1) * PSLICE)
            for option in range(2 * UNITS):
                total = jnp.zeros((PSLICE, 2 * HEAD), f32)
                for number in range(UNITS):
                    total += jnp.where(slots[number] == option, grads[number, at], 0.0)
                rows = pl.ds(option % UNITS * PSLICE, PSLICE)
                targets[option // UNITS][s, rows] = total.astype(bf)
        for number in range(UNITS):
            grad_own_ref[number * PSLICE : (number + 1) * PSLICE] = grads[number, PROMPT:]


def attend_back(table, mapped, length, query, grad, log_sum, own_pairs, sources, earlier):
    rows = UNITS * PSLICE
    whole = pl.BlockSpec(memory_space=pltpu.VMEM)
    return pl.pallas_call(
        attend_back_kernel,
        out_shape=(
            jax.ShapeDtypeStruct((rows, HEADS * HEAD), f32),
            jax.ShapeDtypeStruct((rows, 2 * HEAD), f32),
        )
        + (jax.ShapeDtypeStruct((GROUP, UNITS * PSLICE, 2 * HEAD), bf),) * 2,
        grid=(UNITS, HEADS),
        in_specs=[smem, smem, smem, unit_head, unit_head, sum_spec]
        + [anywhere] * (3 + len(earlier)),
        out_specs=(unit_head,) + (whole,) * 3,
        scratch_shapes=[
            pltpu.VMEM((UNITS, GROUP + 1, PSLICE, 2 * HEAD), bf),
            pltpu.VMEM((HEAD, KEYS), bf),
            pltpu.VMEM((UNITS, KEYS, 2 * HEAD), f32),
            pltpu.SemaphoreType.DMA((UNITS, 2)),
        ],
        compiler_params=pltpu.CompilerParams(vmem_limit_bytes=56 << 20),
        cost_estimate=pl.CostEstimate(
            flops=10 * rows * HEADS * KEYS * HEAD,
            bytes_accessed=2 * KEYS * 2 * HEAD * 6 + 10 * rows * HEADS * HEAD,
            transcendentals=rows * HEADS * KEYS,
        ),
        name="attend_back",
    )(table, mapped, length, query, grad, log_sum, own_pairs, *sources, *earlier)


GELU_SCALE = math.sqrt(2.0 / math.pi)
GELU_CUBE = 0.044715


def gelu_parts(gate):
    bent = jnp.tanh(GELU_SCALE * (gate + GELU_CUBE * (gate * gate * gate)))
    return bent, 0.5 * (1.0 + bent)


CUT = 80


def weight_copies(table, pieces, held, sems):
    copies = ([], [], [])

    def add(kind, source, target):
        number = sum(len(kept) for kept in copies)
        copies[kind].append(pltpu.make_async_copy(source, target, sems.at[number]))

    if len(pieces) == 1:
        for kind in range(3):
            add(kind, pieces[0].at[kind], held[kind])
        return copies
    shard = held[0].shape[0] // GROUP
    for way in range(2):
        for s in range(GROUP):
            piece = pieces[way * GROUP + s]
            start = pl.multiple_of(table[AT_RING + way * GROUP + s] * shard, 16)
            low, high = ((0, CUT), (CUT, shard))[way]
            add(way, piece.at[pl.ds(0, shard)], held[way].at[pl.ds(start, shard)])
            add(
                2,
                piece.at[pl.ds(shard, high - low)],
                held[2].at[pl.ds(pl.multiple_of(start + low, 16), high - low)],
            )
    return copies


def bring(copies, kinds, start):
    @pl.when(pl.program_id(0) == 0)
    def _():
        for kind in kinds:
            for copy in copies[kind]:
                copy.start() if start else copy.wait()


def pick_rows(first_ref, second_ref, rows):
    step = pl.program_id(0)

    @pl.when(step == 0)
    def _():
        rows[...] = first_ref[...]

    @pl.when(step == 1)
    def _():
        rows[...] = second_ref[...]


def put_rows(first_ref, second_ref, total):
    step = pl.program_id(0)

    @pl.when(step == 0)
    def _():
        first_ref[...] = total

    @pl.when(step == 1)
    def _():
        second_ref[...] = total


def feed_kernel(n_pieces, table, first_ref, second_ref, *refs):
    pieces, refs = refs[:n_pieces], refs[n_pieces:]
    gate_ref, up_ref, act_ref, first_out, second_out, rows, gate_w, up_w, down_w, sems = refs
    copies = weight_copies(table, pieces, (gate_w, up_w, down_w), sems)
    bring(copies, (0, 1, 2), True)
    pick_rows(first_ref, second_ref, rows)
    bring(copies, (0,), False)
    gate = dot_nn(rows[...], gate_w[...])
    bring(copies, (1,), False)
    up = dot_nn(rows[...], up_w[...])
    act = (gate * gelu_parts(gate)[1] * up).astype(bf)
    gate_ref[...] = gate.astype(bf)
    up_ref[...] = up.astype(bf)
    act_ref[...] = act
    bring(copies, (2,), False)
    put_rows(first_out, second_out, dot_nt(act, down_w[...]).astype(bf))


def feed_back_kernel(n_pieces, table, first_ref, second_ref, gate_ref, up_ref, *refs):
    pieces, refs = refs[:n_pieces], refs[n_pieces:]
    gate_out, up_out, first_out, second_out, rows, gate_w, up_w, down_w, sems = refs
    copies = weight_copies(table, pieces, (gate_w, up_w, down_w), sems)
    bring(copies, (2, 0, 1), True)
    pick_rows(first_ref, second_ref, rows)
    bring(copies, (2, 0, 1), False)
    total = jnp.zeros(rows.shape, f32)
    hidden = gate_ref.shape[1]
    for low in range(0, hidden, 512):
        at = slice(low, min(low + 512, hidden))
        grad_act = dot_nn(rows[...], down_w[:, at])
        gate, up = gate_ref[:, at].astype(f32), up_ref[:, at].astype(f32)
        bent, share = gelu_parts(gate)
        slope = share + 0.5 * gate * (1.0 - bent * bent) * (
            GELU_SCALE * (1.0 + 3.0 * GELU_CUBE * (gate * gate))
        )
        grad_gate = (grad_act * up * slope).astype(bf)
        grad_up = (grad_act * (gate * share)).astype(bf)
        gate_out[:, at] = grad_gate
        up_out[:, at] = grad_up
        total += dot_nt(grad_gate, gate_w[:, at]) + dot_nt(grad_up, up_w[:, at])
    put_rows(first_out, second_out, total.astype(bf))


def feed_call(kernel, name, table, first, second, hiddens, pieces, n_out):
    rows, dim = first.shape
    hidden = pieces[0].shape[-1]
    fixed = pl.BlockSpec((rows, dim), lambda i: (0, 0))
    wide = pl.BlockSpec((rows, hidden), lambda i: (i, 0))
    row_shape = jax.ShapeDtypeStruct((rows, dim), bf)
    wide_shape = jax.ShapeDtypeStruct((2 * rows, hidden), bf)
    return pl.pallas_call(
        functools.partial(kernel, len(pieces)),
        out_shape=(wide_shape,) * n_out + (row_shape, row_shape),
        grid=(2,),
        in_specs=[smem, fixed, fixed] + [wide] * len(hiddens) + [anywhere] * len(pieces),
        out_specs=(wide,) * n_out + (fixed, fixed),
        scratch_shapes=[pltpu.VMEM((rows, dim), bf)]
        + [pltpu.VMEM((dim, hidden), bf)] * 3
        + [pltpu.SemaphoreType.DMA((max(3, 2 * len(pieces)),))],
        compiler_params=pltpu.CompilerParams(vmem_limit_bytes=60 << 20),
        cost_estimate=pl.CostEstimate(
            flops=12 * rows * dim * hidden,
            bytes_accessed=6 * dim * hidden + 2 * rows * hidden * 2 * (n_out + len(hiddens)),
            transcendentals=2 * rows * hidden,
        ),
        name=name,
    )(table, first, second, *hiddens, *pieces)


def pass_on_kernel(moved, last, table, *refs):
    if moved:
        first_ref, second_ref, refs = refs[0], refs[1], refs[2:]
    gate_ref, up_ref, down_first, down_second = refs[:4]
    outs = refs[-3:] if last else refs[-2:]
    shard = gate_ref.shape[2]
    gate, up = gate_ref[0, 0].astype(f32), up_ref[0, 0].astype(f32)
    low, high = down_first[0, 0, :CUT].astype(f32), down_second[0, 0, CUT:].astype(f32)
    if moved:
        gate += first_ref[:shard].astype(f32)
        low += first_ref[shard:].astype(f32)
        up += second_ref[:shard].astype(f32)
        high += second_ref[shard:].astype(f32)
    if last:
        outs[0][...] = gate
        outs[1][...] = up
        outs[2][:CUT] = low
        outs[2][CUT:] = high
    else:
        outs[0][:shard] = gate.astype(bf)
        outs[0][shard:] = low.astype(bf)
        outs[1][:shard] = up.astype(bf)
        outs[1][shard:] = high.astype(bf)


def pass_on(table, moved, gate_up_w, down_w, s, earlier=()):
    _, _, shard, hidden = gate_up_w.shape
    width = 896
    last = s == 0

    def block(rows):
        return pl.BlockSpec((rows, width), lambda i, table: (0, i))

    def term(way, kind):
        return pl.BlockSpec(
            (1, 1, shard, width),
            lambda i, table: (table[AT_RING + way * GROUP + s], kind, 0, i),
        )

    heights = (shard,) * 3 if last else (shard + CUT, 2 * shard - CUT)
    kind = f32 if last else bf
    return pl.pallas_call(
        functools.partial(pass_on_kernel, len(moved), last),
        out_shape=tuple(jax.ShapeDtypeStruct((rows, hidden), kind) for rows in heights),
        grid_spec=pltpu.PrefetchScalarGridSpec(
            num_scalar_prefetch=1,
            grid=(pl.cdiv(hidden, width),),
            in_specs=[block(part.shape[0]) for part in moved]
            + [term(0, 0), term(1, 1), term(0, 0), term(1, 0)]
            + [anywhere] * len(earlier),
            out_specs=tuple(block(rows) for rows in heights),
        ),
        compiler_params=pltpu.CompilerParams(vmem_limit_bytes=60 << 20),
        name="pass_on",
    )(table, *moved, gate_up_w, gate_up_w, down_w, down_w, *earlier)


def weight_grad_kernel(number, *refs):
    blocks, halves = refs[:TENSOR], refs[TENSOR : TENSOR + 2 * number]
    out_ref, turned = refs[TENSOR + 2 * number :]
    rows = blocks[0].shape[0]

    @pl.when(pl.program_id(0) == 0)
    def _():
        for j in range(TENSOR):
            turned[:, j * rows : (j + 1) * rows] = blocks[j][...].T

    for k in range(number):
        total = dot_nn(turned[:, : 2 * rows], halves[2 * k][...])
        total += dot_nn(turned[:, 2 * rows :], halves[2 * k + 1][...])
        out_ref[:, k] = total.astype(bf).reshape(out_ref.shape[0], out_ref.shape[2], -1)


def weight_grads(name, blocks, halves, parts):
    rows, dim = blocks[0].shape
    hidden = halves[0].shape[1]
    number = len(halves) // 2
    width = 256
    return pl.pallas_call(
        functools.partial(weight_grad_kernel, number),
        out_shape=jax.ShapeDtypeStruct((parts, number, dim // parts, hidden), bf),
        grid=(pl.cdiv(hidden, width),),
        in_specs=[pl.BlockSpec((rows, dim), lambda i: (0, 0), pipeline_mode=pl.Buffered(1))]
        * TENSOR
        + [pl.BlockSpec((2 * rows, width), lambda i: (0, i))] * (2 * number),
        out_specs=pl.BlockSpec((parts, number, dim // parts, width), lambda i: (0, 0, 0, i)),
        scratch_shapes=[pltpu.VMEM((dim, TENSOR * rows), bf)],
        compiler_params=pltpu.CompilerParams(vmem_limit_bytes=48 << 20),
        cost_estimate=pl.CostEstimate(
            flops=3 * number * rows * dim * hidden,
            bytes_accessed=4 * rows * dim + number * (4 * rows + 2 * dim) * hidden,
            transcendentals=0,
        ),
        name=name,
    )(*blocks, *halves)


def norm_rate(value):
    return lax.rsqrt(jnp.mean(value * value, axis=-1, keepdims=True) + eps_norm)


def norm_back(value, gain, grad):
    rate = norm_rate(value)
    scaled = (1.0 + gain) * grad
    back = rate * scaled - value * (rate * rate * rate) * jnp.mean(
        value * scaled, axis=-1, keepdims=True
    )
    return back, jnp.sum(value * rate * grad, axis=0, keepdims=True)


def add_up(ref, value):
    step = pl.program_id(0)

    @pl.when(step == 0)
    def _():
        ref[...] = value

    @pl.when(step > 0)
    def _():
        ref[...] += value


def three_parts(refs):
    return refs[0][...].astype(f32) + refs[1][...].astype(f32) + refs[2][...].astype(f32)


def result_kernel(table, length, scale, *refs):
    mixed_ref, teacher_ref, gain_ref = refs[3:6]
    result_ref, grad_ref, low_ref, gain_out, loss_out = refs[6:]
    gain = gain_ref[...]
    value = three_parts(refs)
    result = mixed_ref[...] + value * norm_rate(value) * (1.0 + gain)
    result_ref[...] = result.astype(bf)
    row = lax.broadcasted_iota(jnp.int32, (PSLICE, 1), 0)
    live = length[table[AT_CORE] * UNITS + pl.program_id(0)]
    live = jnp.where(table[AT_CONT] == 1, live, PSLICE)
    diff = jnp.where(row < live, result - teacher_ref[...].astype(f32), 0.0)
    add_up(loss_out, jnp.sum(diff * diff, axis=0, keepdims=True))
    grad = scale[0] * diff
    grad_ref[...] = grad
    back, gain_grad = norm_back(value, gain, grad)
    low_ref[...] = back.astype(bf)
    add_up(gain_out, gain_grad)


def mixed_kernel(*refs):
    mixed_ref, sum_ref, grad_ref, ffw_gain_ref, post_gain_ref = refs[3:8]
    mixed_out, low_out, ffw_out, post_out = refs[8:]
    back, ffw_grad = norm_back(mixed_ref[...], ffw_gain_ref[...], three_parts(refs))
    grad_mixed = grad_ref[...] + back
    mixed_out[...] = grad_mixed
    add_up(ffw_out, ffw_grad)
    back, post_grad = norm_back(sum_ref[...], post_gain_ref[...], grad_mixed)
    low_out[...] = back.astype(bf)
    add_up(post_out, post_grad)


def input_kernel(part_ref, low_ref, kv_ref, input_ref, grad_ref, gain_ref, out_ref, gain_out):
    grad = part_ref[...] + dot_nt(low_ref[...], kv_ref[...])
    back, gain_grad = norm_back(input_ref[...].astype(f32), gain_ref[...], grad)
    out_ref[...] = (grad_ref[...] + back).astype(bf)
    add_up(gain_out, gain_grad)


def by_rows(kernel, name, scalars, operands, outs):
    def spec(shape, whole=False):
        if whole or shape[0] == 1:
            return pl.BlockSpec(shape, lambda i: (0, 0))
        return pl.BlockSpec((PSLICE, shape[1]), lambda i: (i, 0))

    operands = [part if isinstance(part, tuple) else (part, False) for part in operands]
    return pl.pallas_call(
        kernel,
        out_shape=tuple(jax.ShapeDtypeStruct(shape, kind) for shape, kind in outs),
        grid=(UNITS,),
        in_specs=[smem] * len(scalars) + [spec(part.shape, whole) for part, whole in operands],
        out_specs=tuple(spec(shape) for shape, _ in outs),
        compiler_params=pltpu.CompilerParams(vmem_limit_bytes=48 << 20),
        cost_estimate=pl.CostEstimate(
            flops=20 * UNITS * PSLICE * 1152, bytes_accessed=16 << 20, transcendentals=0
        ),
        name=name,
    )(*scalars, *[part for part, _ in operands])


def local(
    layer_in,
    teacher,
    query_proj,
    key_proj,
    value_proj,
    out_proj,
    gate_proj,
    up_proj,
    down_proj,
    attn_norm,
    attn_post,
    ffw_norm,
    ffw_post,
    query_norm,
    key_norm,
    cont_prompt,
    cont_length,
    token_count,
    loss_scale,
):
    members = lax.axis_size("fsdp")
    fsdp_pos = lax.axis_index("fsdp")
    tensor_pos = lax.axis_index("tensor")
    core, side = tensor_pos % 2, tensor_pos // 2
    is_cont = side == 1
    group_slot = fsdp_pos % GROUP
    table = lax.dynamic_index_in_dim(
        jnp.asarray(place_table(members)), fsdp_pos * TENSOR + tensor_pos, 0, keepdims=False
    )
    dim = layer_in.shape[1]

    ringed = members == GROUP
    down_own = down_proj.T
    if ringed:
        parts = GROUP
        weights = Spread(
            jnp.concatenate([gate_proj, down_own[:CUT]], 0),
            jnp.concatenate([up_proj, down_own[CUT:]], 0),
        )
        came = [()] + [weights.step() for _ in range(4)]
    else:
        came = [()] * (GROUP + 1)
        parts = 1
        pieces = (gate_proj, up_proj, down_own)
        pieces = [jnp.stack([lax.all_gather(w, "fsdp", axis=0, tiled=True) for w in pieces])]

    shard_kv = key_proj.shape[0]
    shard_gain, shard_head = attn_norm.shape[0], query_norm.shape[0]
    gains_own = jnp.stack(
        [
            jnp.pad(gain, (0, 2 * HEAD - gain.shape[0]))
            for gain in (attn_norm, attn_post, ffw_norm, ffw_post, query_norm, key_norm)
        ]
    )
    packed = jnp.concatenate([jnp.concatenate([key_proj, value_proj], 1), gains_own], 0)
    packed = jnp.pad(packed, ((0, -packed.shape[0] % 16), (0, 0)))
    packed_f = spread_y(spread_z(packed))
    packed_all = place(table, spread_tensor(packed_f))
    qo_own = jnp.concatenate([query_proj, out_proj.T], 1)
    qo_column = spread_z(after(qo_own, packed_f))
    kv_full = packed_all[:, :, :shard_kv].reshape(dim, 2 * HEAD)
    gains_all = packed_all[:, :, shard_kv : shard_kv + 6].astype(f32)

    def gain_of(number):
        return gains_all[:, :, number, :shard_gain].reshape(dim)

    def head_gain_of(number):
        return gains_all[:, :, 4 + number, :shard_head].reshape(HEAD)

    attn_gain, attn_post_gain, ffw_gain, ffw_post_gain = (gain_of(k) for k in range(4))
    query_gain, key_gain = head_gain_of(0), head_gain_of(1)

    local_rows = layer_in.shape[0]
    unit_ids = jnp.arange(local_rows, dtype=jnp.int32) % PSLICE
    positions = unit_ids + jnp.where(is_cont, PROMPT, group_slot * PSLICE)
    inverse_freq = jnp.exp(
        -math.log(rope_base) * 2.0 * jnp.arange(HEAD // 2, dtype=f32) / HEAD
    )
    angles = positions.astype(f32)[:, None] * inverse_freq[None, :]
    cosine, sine_part = jnp.cos(angles), jnp.sin(angles)
    input_f = layer_in.astype(f32)
    normed_in = rms_scale(input_f, attn_gain).astype(bf)

    kv_raw = dot_nn(normed_in, kv_full)
    key_raw = kv_raw[:, :HEAD]
    key_rot = head_prep(key_raw, key_gain, cosine, sine_part).astype(bf)
    own_pairs = jnp.concatenate([key_rot, kv_raw[:, HEAD:].astype(bf)], 1)
    own_pairs = after(own_pairs, qo_column, *came[1])
    qo_column = spread_y(after(qo_column, packed_all))
    across = lax.ppermute(own_pairs, "tensor", [(0, 2), (1, 3)])
    prompt_pairs = after(jnp.where(is_cont, across, own_pairs), qo_column, *came[2])
    if ringed:
        held_pairs = lax.all_gather(prompt_pairs, "fsdp", axis=0)
    else:
        held_pairs = [prompt_pairs]
        while len(held_pairs) < GROUP:
            held_pairs.append(ring_step(held_pairs[-1], 1))
        held_pairs = jnp.stack(held_pairs)
    qo_column = after(qo_column, across)
    qo_near, qo_far = spread_near(qo_column)
    query_full, out_full = (
        part.reshape(dim, HEADS * HEAD)
        for part in place_heads(
            table, (qo_column, qo_near, qo_far, swap_core(after(qo_far, *came[3])))
        )
    )
    query_raw = dot_nn(normed_in, query_full)
    query_heads = [
        head_prep(query_raw[:, h * HEAD : (h + 1) * HEAD], query_gain, cosine, sine_part).astype(bf)
        for h in range(HEADS)
    ]

    query_rot = jnp.concatenate(query_heads, 1)
    if ringed:
        came += [weights.step(query_rot), weights.step(), weights.step()]
    held_pairs = after(held_pairs, query_rot, *came[5])
    query_rot = after(query_rot, *came[6])
    sources = held_pairs, lax.ppermute(held_pairs, "tensor", [(2, 3), (3, 2)])
    attn_low, log_sum = attend(
        table, cont_prompt, cont_length, query_rot, own_pairs, sources
    )
    attn_sum = dot_nt(attn_low, out_full)
    if ringed:
        pieces = weights.firsts + weights.seconds
    mixed = input_f + rms_scale(attn_sum, attn_post_gain)
    normed_mid = rms_scale(mixed, ffw_gain).astype(bf)

    mid_near, mid_far = spread_near(after(normed_mid, *came[7]))
    gate_0, up_0, act_0, *downs = feed_call(
        feed_kernel, "feed", table, normed_mid, mid_near, (), pieces, 3
    )
    mid_last = swap_core(after(mid_far, downs[0]))
    gate_1, up_1, act_1, *more = feed_call(
        feed_kernel, "feed", table, mid_far, mid_last, (), pieces, 3
    )
    downs += more
    downs_moved = swap_core(downs[1]), swap_x(collect_far(*downs[2:]))
    count_f = token_count.astype(f32)
    row_kind, gain_kind = (local_rows, dim), ((1, dim), f32)
    result_low, grad_result, grad_ffw_low, grad_ffw_post_gain, loss_lanes = by_rows(
        result_kernel,
        "result",
        (table, cont_length, (loss_scale / count_f * 2.0)[None]),
        (downs[0], *downs_moved, mixed, teacher, ffw_post_gain[None]),
        ((row_kind, bf), (row_kind, f32), (row_kind, bf), gain_kind, gain_kind),
    )
    loss_part = jnp.sum(loss_lanes)

    grad_near, grad_far = spread_near(grad_ffw_low)
    gate_low_0, up_low_0, *mids = feed_call(
        feed_back_kernel, "feed_back", table, grad_ffw_low, grad_near, (gate_0, up_0), pieces, 2
    )
    grad_last = swap_core(after(grad_far, mids[0]))
    gate_low_1, up_low_1, *more = feed_call(
        feed_back_kernel, "feed_back", table, grad_far, grad_last, (gate_1, up_1), pieces, 2
    )
    mids += more
    mids_far = collect_far(*mids[2:])
    mids_moved = swap_core(mids[1]), swap_x(mids_far)
    down_w = weight_grads(
        "down_grad",
        (after(grad_ffw_low, mids_far), grad_near, grad_far, grad_last),
        (act_0, act_1),
        parts,
    )
    gate_up_w = weight_grads(
        "gate_up_grad",
        (after(normed_mid, mids_far), mid_near, mid_far, mid_last),
        (gate_low_0, gate_low_1, up_low_0, up_low_1),
        parts,
    )
    if ringed:
        held_sums = pass_on(table, (), gate_up_w, down_w, GROUP - 1)

        def move_sums():
            return ring_step(held_sums[0], -1), ring_step(held_sums[1], 1)

        def add_sums(moved, s, *earlier):
            return pass_on(table, moved, gate_up_w, down_w, s, earlier)

    else:
        out_down = lax.psum_scatter(down_w[0, 0], "fsdp", scatter_dimension=0, tiled=True)
        out_down = out_down.astype(f32)
        out_gate, out_up = lax.psum_scatter(
            gate_up_w[0], "fsdp", scatter_dimension=1, tiled=True
        ).astype(f32)

    grad_mixed, grad_attn_low, grad_ffw_gain, grad_attn_post_gain = by_rows(
        mixed_kernel,
        "mixed_back",
        (),
        (mids[0], *mids_moved, mixed, attn_sum, grad_result, ffw_gain[None], attn_post_gain[None]),
        ((row_kind, f32), (row_kind, bf), gain_kind, gain_kind),
    )
    grad_out_w = dot_tn(grad_attn_low, attn_low)
    grad_attn_rows = dot_nn(grad_attn_low, out_full).astype(bf)
    if ringed:
        held_sums = add_sums(move_sums(), 6, grad_attn_rows)
    grad_query_rot, grad_own, kept, given = attend_back(
        table, cont_prompt, cont_length, query_rot, grad_attn_rows, log_sum, own_pairs, sources, held_sums if ringed else ()
    )
    _, query_pull = jax.vjp(
        lambda raw, gain: tuple(
            head_prep(raw[:, h * HEAD : (h + 1) * HEAD], gain, cosine, sine_part)
            for h in range(HEADS)
        ),
        query_raw,
        query_gain,
    )
    grad_query_raw, grad_query_gain = query_pull(
        tuple(grad_query_rot[:, h * HEAD : (h + 1) * HEAD] for h in range(HEADS))
    )
    grad_query_low = grad_query_raw.astype(bf)
    grad_query_w = dot_tn(normed_in, grad_query_low)
    qo_sum = collect_tensor(
        *(
            jnp.concatenate(
                [grad_query_w[:, h * HEAD : (h + 1) * HEAD], grad_out_w[:, h * HEAD : (h + 1) * HEAD]],
                1,
            )
            for h in range(HEADS)
        )
    ).reshape(members, dim // members, 2 * HEAD)
    out_qo = collect_fsdp(qo_sum, fsdp_pos)
    out_query, out_out = out_qo[:, :HEAD], out_qo[:, HEAD:].T
    if ringed:
        moved = move_sums()
        given = after(given, *moved)
        held_sums = add_sums(moved, 5)
    given = lax.ppermute(given, "tensor", [(2, 3), (3, 2)])
    kept = (kept.astype(f32) + given.astype(f32)).astype(bf)
    if ringed:
        for s in (4, 3, 2):
            held_sums = add_sums(move_sums(), s)
        summed = lax.psum_scatter(kept, "fsdp", scatter_dimension=0)
        summed = after(summed, *held_sums).astype(f32)
    else:
        summed = kept[GROUP - 1]
        for s in reversed(range(GROUP - 1)):
            summed = (ring_step(summed, -1).astype(f32) + kept[s].astype(f32)).astype(bf)
        summed = summed.astype(f32)
    back = lax.ppermute(summed.astype(bf), "tensor", [(2, 0), (3, 1)]).astype(f32)
    grad_pairs = jnp.where(is_cont, grad_own, summed + back)

    _, key_pull = jax.vjp(
        lambda raw, gain: head_prep(raw, gain, cosine, sine_part), key_raw, key_gain
    )
    grad_key_raw, grad_key_gain = key_pull(grad_pairs[:, :HEAD])
    grad_kv_low = jnp.concatenate([grad_key_raw, grad_pairs[:, HEAD:]], 1).astype(bf)
    grad_kv_w = dot_tn(normed_in, grad_kv_low)
    grad_input, grad_attn_gain = by_rows(
        input_kernel,
        "input_back",
        (),
        (
            dot_nt(grad_query_low, query_full),
            grad_kv_low,
            (kv_full, True),
            layer_in,
            grad_mixed,
            attn_gain[None],
        ),
        ((row_kind, bf), gain_kind),
    )

    kv_blocks = grad_kv_w.reshape(members, TENSOR, shard_kv, 2 * HEAD)
    kv_parts = order_tensor([kv_blocks[:, t] for t in range(TENSOR)], tensor_pos)

    if ringed:
        moved = move_sums()
        kv_parts = kv_parts[:1] + (after(kv_parts[1], out_qo, *moved),) + kv_parts[2:]
        held_sums = add_sums(moved, 1)

    small = jnp.concatenate(
        [
            grad_attn_gain[0],
            grad_attn_post_gain[0],
            grad_ffw_gain[0],
            grad_ffw_post_gain[0],
            grad_query_gain,
            grad_key_gain,
            loss_part[None],
        ]
    )
    length = small.shape[0]
    small = jnp.pad(small, (0, -length % 1024)).reshape(-1, 128)
    if ringed:
        out_kv, small, column = sum_both(kv_parts, small, fsdp_pos)
        out_gate, out_up, out_down = add_sums(move_sums(), 0, column)
    else:
        out_kv = collect_fsdp(collect_tensor(*kv_parts), fsdp_pos)
        small = sum_all(small)
    out_down = out_down.T
    small = small.reshape(-1)
    device = fsdp_pos * TENSOR + tensor_pos
    wide = [
        lax.dynamic_slice(small, (k * dim + device * shard_gain,), (shard_gain,)) for k in range(4)
    ]
    narrow = [
        lax.dynamic_slice(small, (4 * dim + k * HEAD + device * shard_head,), (shard_head,))
        for k in range(2)
    ]
    loss = small[length - 1] / count_f
    return (
        result_low,
        loss,
        grad_input,
        out_query,
        out_kv[:, :HEAD],
        out_kv[:, HEAD:],
        out_out,
        out_gate,
        out_up,
        out_down,
        *wide,
        *narrow,
    )


def solution(mesh):
    rows = P(("fsdp", "tensor"), None)
    split = P(("fsdp", "tensor"))
    inward, outward = P("fsdp", "tensor"), P("tensor", "fsdp")
    return jax.shard_map(
        local,
        mesh=mesh,
        in_specs=(
            rows,
            rows,
            inward,
            rows,
            rows,
            outward,
            inward,
            inward,
            outward,
            *(split,) * 6,
            P("fsdp"),
            P("fsdp"),
            P(),
            P(),
        ),
        out_specs=(
            rows,
            P(),
            rows,
            inward,
            rows,
            rows,
            outward,
            inward,
            inward,
            outward,
            *(split,) * 6,
        ),
        check_vma=False,
    )
```
